32 devices in a mesh: gx: 2 (over y), yz: 16 (over z, x, core).
Axes of the slice: x: 2, y: 2, z: 4, core: 2. Of those that a mesh axis runs over, the one named last changes fastest.
Arguments:
- old_pos: float32 [3, 8192], P(None, ('gx', 'yz')), may hold values from 0 to 1
- old_species: int32 [8192], P(('gx', 'yz')), may hold values from 0 to 4
- block_dest: int32 [64, 1], P(('gx', 'yz')), may hold values from 0 to 2; in each aligned block of 2 rows (0 to 1, 2 to 3, ...) no two rows name the same one
- block_count: int32 [64], P(('gx', 'yz')), may hold values from 1 to 128
- send_list: int32 [128, 64], P(('gx', 'yz')), may hold values from 0 to 383
- neighbours: int32 [4, 12288], P(None, ('gx', 'yz')), may hold values from 0 to 639
- embed: float32 [5, 128], replicated, may hold values from -6 to 6
- atom_ref: float32 [5], replicated, may hold values from -3 to -0.5
- w_up: float32 [2, 128, 128], replicated, may hold values from -0.5 to 0.5
- gammas: float32 [2, 8], replicated, may hold values from 0.3 to 3
- w_rad: float32 [2, 8, 384], replicated, may hold values from -2 to 2
- w_mix: float32 [2, 128, 128], replicated, may hold values from -0.5 to 0.5
- readout: float32 [2, 128], replicated, may hold values from -0.5 to 0.5
Outputs:
- forces: float32 [3, 12288], P(None, ('gx', 'yz'))
- energy: float32 [], replicated
The draws below stay inside these ranges and needn't reach their ends.
Inputs may be any that keep to these rules, and one draw needn't show every extreme that they name: `block_dest`: 0 sends a block to the previous index along yz, 1 keeps it, 2 sends it to the next; among the 2 blocks of one brick at most 1 share a destination, and some destination has exactly 1. `send_list`: slots after migration; row f of a brick's four rows lists what it sends to face f of its neighbours (rows 0, 1 to the next and previous index along gx, rows 2, 3 to the next and previous along yz). `neighbours`: an entry below 384 is a slot of the brick; 384 + f * 64 + g is ghost g of face f.
All inputs are finite; a program needn't handle non-finite values.
Results may differ from the reference program's by a relative error of at most 0.0003.
Values sent between devices are 32-bit elements; how exact they have to be, the bound alone decides.
No kernel may reach another device: no remote copies, remote signals or barrier semaphores. Data moves between devices by JAX's collectives and lax.ppermute only.
A program may use at most 64 MiB of HBM per device.

```python
import math
import jax
import jax.numpy as jnp
import numpy as np
from jax import lax

C = 128
NR = 8
SPEC = 5
LAYERS = 2
NE = 4
BLK = 128
NB = 2
MOST = 1
SL = 384
GH = 64
OLD_SLOTS = 8192
BLOCKS = 64
SLOTS = 12288
LISTS = 128
N_GX = 2
N_YZ = 16


def plant(values, stream_key, least, top_value):
    longest = values.shape.index(max(values.shape))
    spots = []
    for shift in (0, 1):
        where = [jax.random.randint(jax.random.fold_in(stream_key, axis), (), 0, length) for axis, length in enumerate(values.shape)]
        where[longest] = (where[longest] + shift) % values.shape[longest]
        spots.append(tuple(where))
    return values.at[spots[0]].set(least).at[spots[1]].set(top_value)


def steps_of(stream_key, shape, shards, low, high):
    gain = 1.0
    for dim, parts in shards:
        steps = jax.random.uniform(jax.random.fold_in(jax.random.fold_in(stream_key, 6), dim), (parts,), jnp.float32, low / len(shards), high / len(shards))
        gain = gain * jnp.repeat(jnp.exp(steps), shape[dim] // parts).reshape((-1,) + (1,) * (len(shape) - 1 - dim))
    return gain


def deal_out(stream_key, own, number, rows, count, top, reach, slope):
    order = jax.random.permutation(stream_key, count)
    heavy_load, common = load_shares(count, rows * top, reach, slope, True), load_shares(count, rows * top, reach, slope, False)
    places = jnp.arange(count)

    def named(lengths, rotation):
        used = int((lengths > 0).sum())
        fixed = max(1, used // 4)
        shifted = fixed + (places - fixed + rotation * (used - fixed)) % max(1, count - fixed)
        return jnp.zeros((count,), jnp.int32).at[order[jnp.where(places < fixed, places, shifted)]].set(jnp.asarray(lengths, jnp.int32))

    lengths = jnp.where(number % 4 == 0, named(heavy_load, number // 4), named(common, number - number // 4 - 1))
    mixed = jax.random.permutation(jax.random.fold_in(own, 3), count)
    donor, receiver = mixed[0:count // 2 * 2:2], mixed[1:count // 2 * 2:2]
    slack = jnp.minimum(lengths[donor] - 1, reach - lengths[receiver]) // 2
    slack = jnp.where((donor == order[0]) | (receiver == order[0]) | (lengths[receiver] == 0), 0, jnp.maximum(slack, 0))
    shifted = jax.random.randint(jax.random.fold_in(own, 4), (count // 2,), 0, 1 << 20) % (slack + 1)
    lengths = lengths.at[donor].add(-shifted).at[receiver].add(shifted)
    labels = jnp.searchsorted(jnp.cumsum(lengths), jnp.arange(rows * top), side="right").astype(jnp.int32)
    listing = labels.reshape(top, rows).T
    listing = listing[jax.random.permutation(jax.random.fold_in(own, 1), rows)]
    rotation = jax.random.randint(jax.random.fold_in(own, 2), (rows, 1), 0, top)
    return jnp.take_along_axis(listing, (jnp.arange(top)[None, :] + rotation) % top, axis=1)


def load_shares(count, total, bound, slope, full):
    loads = [(1 << 20) // math.isqrt(standing ** slope) + 1 for standing in range(1, count + 1)]
    largest = bound if full else min(bound, max(-(-total // count), total * loads[0] // sum(loads)))
    least = 1 if total - largest >= count - 1 else 0
    given, spare = [largest] + [least] * (count - 1), total - largest - least * (count - 1)
    while spare > 0:
        movable = [i for i in range(1, count) if given[i] < largest] or [i for i in range(1, count) if given[i] < bound]
        mass, left = sum([loads[i] for i in movable]), spare
        for i in movable:
            more = min(bound - given[i], max(1, left * loads[i] // mass), spare)
            given[i] = given[i] + more
            spare = spare - more
    return np.array(given)


def noise(own_key, dims, scale, limit, kind=jnp.bfloat16):
    return jnp.clip(scale * jax.random.normal(own_key, dims, jnp.float32), -limit, limit).astype(kind)


def setup_inputs(seed: int = 0) -> dict:
    arg_keys = jax.random.split(jax.random.key(seed), 14)
    old_pos = jnp.clip(1.0 * jax.random.uniform(arg_keys[0], (3, OLD_SLOTS), jnp.float32) ** steps_of(arg_keys[0], (3, OLD_SLOTS), ((1, 32),), -0.2, 0.2), 0.0, 1.0)
    old_species = plant(jax.random.randint(arg_keys[1], (OLD_SLOTS,), 0, SPEC), jax.random.fold_in(arg_keys[1], 1), 0, SPEC - 1).astype(jnp.int32)
    block_dest_keys = jax.random.split(jax.random.fold_in(arg_keys[2], 1), BLOCKS // NB)
    block_dest_turns = jax.random.permutation(jax.random.fold_in(arg_keys[2], 3), BLOCKS // NB)
    block_dest = jax.vmap(lambda own, number: deal_out(jax.random.fold_in(arg_keys[2], 2), own, number, NB, 3, 1, MOST, 1))(block_dest_keys, block_dest_turns).reshape((BLOCKS, 1))
    block_count = plant(jax.random.randint(arg_keys[3], (BLOCKS,), 1, BLK + 1), jax.random.fold_in(arg_keys[3], 1), 1, BLK).astype(jnp.int32)
    send_list = plant(jax.random.randint(arg_keys[4], (LISTS, GH), 0, SL), jax.random.fold_in(arg_keys[4], 1), 0, SL - 1).astype(jnp.int32)
    neighbours = plant(jax.random.randint(arg_keys[5], (NE, SLOTS), 0, SL + 4 * GH), jax.random.fold_in(arg_keys[5], 1), 0, (SL + 4 * GH) - 1).astype(jnp.int32)
    embed = noise(arg_keys[6], (SPEC, C), 1.0, 6.0, jnp.float32)
    atom_ref = jnp.clip(jax.random.uniform(arg_keys[7], (SPEC,), jnp.float32, -3.0, -0.5), -3.0, -0.5)
    w_up = noise(arg_keys[8], (LAYERS, C, C), C ** -0.5, 0.5, jnp.float32)
    gammas = jnp.clip(jnp.exp(jax.random.uniform(arg_keys[9], (LAYERS, NR), jnp.float32, math.log(0.3), math.log(3.0))), 0.3, 3.0)
    w_rad = noise(arg_keys[10], (LAYERS, NR, 3 * C), NR ** -0.5, 2.0, jnp.float32)
    w_mix = noise(arg_keys[11], (LAYERS, C, C), C ** -0.5, 0.5, jnp.float32)
    readout = noise(arg_keys[12], (LAYERS, C), C ** -0.5, 0.5, jnp.float32)
    return {"old_pos": old_pos, "old_species": old_species, "block_dest": block_dest, "block_count": block_count, "send_list": send_list, "neighbours": neighbours, "embed": embed, "atom_ref": atom_ref, "w_up": w_up, "gammas": gammas, "w_rad": w_rad, "w_mix": w_mix, "readout": readout}


root_three = math.sqrt(3.0)
root_fifteen = math.sqrt(15.0)
root_five_half = 0.5 * math.sqrt(5.0)
root_fifteen_half = 0.5 * math.sqrt(15.0)
degree_of = (0, 1, 1, 1, 2, 2, 2, 2, 2)
highest = lax.Precision.HIGHEST

def harmonics(unit_x, unit_y, unit_z):
    square = unit_x * unit_x + unit_y * unit_y + unit_z * unit_z
    return jnp.stack([jnp.ones_like(unit_x), root_three * unit_x, root_three * unit_y, root_three * unit_z, root_fifteen * unit_x * unit_y, root_fifteen * unit_y * unit_z, root_five_half * (3.0 * unit_z * unit_z - square), root_fifteen * unit_x * unit_z, root_fifteen_half * (unit_x * unit_x - unit_y * unit_y)], axis=1)

def edge_terms(source_pos, target_pos, source_feat, gammas, w_rad):
    offset = source_pos - target_pos
    length_sq = lax.optimization_barrier(jnp.sum(offset * offset, axis=0))
    basis = jnp.exp(-gammas[:, None] * length_sq[None, :])
    radial = jnp.einsum('qs,qf->sf', basis, w_rad, precision=highest)
    channels = source_feat.shape[1]
    radial = radial.reshape(-1, 3, channels)[:, jnp.asarray(degree_of, dtype=jnp.int32), :]
    scale = lax.rsqrt(1.0 + length_sq)
    unit = offset * scale[None, :]
    angular = harmonics(unit[0], unit[1], unit[2])
    return radial * angular[:, :, None] * source_feat[:, None, :]

def gather_messages(pos_ext, projected, neighbours, gammas, w_rad):
    slots = neighbours.shape[1]
    target_pos = pos_ext[:, :slots]

    def add_edges(column, total):
        source = neighbours[column]
        return total + edge_terms(pos_ext[:, source], target_pos, projected[source], gammas, w_rad)
    start = jnp.zeros((slots, 9, projected.shape[1]), pos_ext.dtype)
    return lax.fori_loop(0, neighbours.shape[0], add_edges, start)

def update(h_local, summed, live, w_mix, entries):
    averaged = summed / entries
    invariant = averaged[:, 0, :] + lax.optimization_barrier(jnp.sum(averaged[:, 1:4, :] * averaged[:, 1:4, :], axis=1)) + lax.optimization_barrier(jnp.sum(averaged[:, 4:, :] * averaged[:, 4:, :], axis=1))
    mixed = jnp.dot(invariant, w_mix, precision=highest)
    return (h_local + jax.nn.silu(mixed)) * live[:, None]

def layer_forward(pos_ext, h_ext, neighbours, live, w_up, gammas, w_rad, w_mix):
    projected = jnp.dot(h_ext, w_up, precision=highest)
    summed = gather_messages(pos_ext, projected, neighbours, gammas, w_rad)
    return update(h_ext[:neighbours.shape[1]], summed, live, w_mix, neighbours.shape[0])

def species_onehot(species, width, dtype):
    return (species[:, None] == jnp.arange(width, dtype=jnp.int32)[None, :]).astype(dtype)

def embed_rows(species, live, embed):
    onehot = species_onehot(species, embed.shape[0], embed.dtype)
    return jnp.dot(onehot, embed, precision=highest) * live[:, None]

def base_energy(species, live, atom_ref):
    onehot = species_onehot(species, atom_ref.shape[0], atom_ref.dtype)
    return jnp.dot(onehot, atom_ref, precision=highest) * live

def pack_blocks(old_pos, old_species, dest, count):
    n_blocks = dest.shape[0]
    per_block = old_species.shape[0] // n_blocks
    capacity = n_blocks // 2
    order = jnp.arange(n_blocks, dtype=jnp.int32)
    earlier = (order[:, None] > order[None, :]).astype(jnp.int32)
    same_dest = (dest[:, None] == dest[None, :]).astype(jnp.int32)
    rank = lax.optimization_barrier(jnp.sum(earlier * same_dest, axis=1))
    select = ((dest[None, None, :] == jnp.arange(3, dtype=jnp.int32)[:, None, None]) & (rank[None, None, :] == jnp.arange(capacity, dtype=jnp.int32)[None, :, None])).astype(jnp.int32)
    blocks_pos = old_pos.reshape(3, n_blocks, per_block)
    packed_pos = lax.optimization_barrier(jnp.sum(select.astype(old_pos.dtype)[:, :, None, :, None] * blocks_pos[None, None, :, :, :], axis=3))
    packed_species = lax.optimization_barrier(jnp.sum(select[:, :, :, None] * old_species.reshape(n_blocks, per_block)[None, None, :, :], axis=2))
    packed_count = lax.optimization_barrier(jnp.sum(select * count[None, None, :], axis=2))
    return (packed_pos, packed_species, packed_count)

def extend(rows, lists):
    picked = jax.vmap(jax.vmap(lambda table, chosen: table[chosen]))(rows, lists)
    faces = [jnp.roll(picked[:, :, 0], 1, axis=0), jnp.roll(picked[:, :, 1], -1, axis=0), jnp.roll(picked[:, :, 2], 1, axis=1), jnp.roll(picked[:, :, 3], -1, axis=1)]
    ghosts = jnp.stack(faces, axis=2).reshape(rows.shape[0], rows.shape[1], -1, rows.shape[3])
    return jnp.concatenate([rows, ghosts], axis=2)

def reference(old_pos, old_species, block_dest, block_count, send_list, neighbours, embed, atom_ref, w_up, gammas, w_rad, w_mix, readout):
    grid_x = N_GX
    grid_yz = N_YZ
    devices = grid_x * grid_yz
    pos_dev = old_pos.reshape(3, devices, -1).transpose(1, 0, 2)
    species_dev = old_species.reshape(devices, -1)
    dest_dev = block_dest.reshape(devices, -1)
    count_dev = block_count.reshape(devices, -1)
    packed_pos, packed_species, packed_count = jax.vmap(pack_blocks)(pos_dev, species_dev, dest_dev, count_dev)

    def arrive(packed):
        packed = packed.reshape((grid_x, grid_yz) + packed.shape[1:])
        return jnp.stack([jnp.roll(packed[:, :, group], group - 1, axis=1) for group in range(3)], axis=2)
    positions = arrive(packed_pos).transpose(0, 1, 4, 2, 3, 5).reshape(grid_x, grid_yz, 3, -1)
    species = arrive(packed_species).reshape(grid_x, grid_yz, -1)
    counts = arrive(packed_count).reshape(grid_x, grid_yz, -1)
    live = (jnp.arange(BLK, dtype=jnp.int32)[None, None, None, :] < counts[..., None]).astype(jnp.float32).reshape(grid_x, grid_yz, -1)
    slots = species.shape[2]
    lists = send_list.reshape(grid_x, grid_yz, 4, -1)
    edges = neighbours.reshape(NE, grid_x, grid_yz, slots).transpose(1, 2, 0, 3).reshape(devices, NE, slots)
    flat_live = live.reshape(devices, slots)
    per_device = jax.vmap(jax.vmap(embed_rows, in_axes=(0, 0, None)), in_axes=(0, 0, None))
    h_zero = per_device(species, live, embed)
    base = jax.vmap(jax.vmap(base_energy, in_axes=(0, 0, None)), in_axes=(0, 0, None))(species, live, atom_ref)

    def run_layer(layer, pos_ext, h_ext):

        def single(operands):
            return layer_forward(operands[0], operands[1], operands[2], operands[3], w_up[layer], gammas[layer], w_rad[layer], w_mix[layer])
        result = lax.map(jax.checkpoint(single), (pos_ext.reshape(devices, 3, -1), h_ext.reshape(devices, -1, h_ext.shape[-1]), edges, flat_live))
        return result.reshape(grid_x, grid_yz, slots, -1)

    def total_energy(coords):
        pos_ext = extend(coords.transpose(0, 1, 3, 2), lists).transpose(0, 1, 3, 2)
        h_one = run_layer(0, pos_ext, extend(h_zero, lists))
        h_two = run_layer(1, pos_ext, extend(h_one, lists))
        atomic = jnp.einsum('gysc,c->gys', h_one, readout[0], precision=highest) + jnp.einsum('gysc,c->gys', h_two, readout[1], precision=highest)
        return jnp.sum(base + live * atomic)
    total, grads = jax.value_and_grad(total_energy)(positions)
    energy = total / jnp.sum(live)
    forces = -grads.transpose(2, 0, 1, 3).reshape(3, -1)
    return (forces, energy)
```

```python
import functools
import math

import jax
import jax.numpy as jnp
from jax import lax
from jax.experimental import pallas as pl
from jax.experimental.pallas import tpu as pltpu
from jax.sharding import PartitionSpec as P

root_three = math.sqrt(3.0)
root_five = math.sqrt(5.0)
root_fifteen = math.sqrt(15.0)
f32 = jnp.float32
bf16 = jnp.bfloat16
ROWS = 8
LANES = 128
VMEM_BYTES = 48 * 1024 * 1024


def split2(value):
    high = value.astype(bf16)
    return high, (value - high.astype(f32)).astype(bf16)


def split3(value):
    high = value.astype(bf16)
    rest = value - high.astype(f32)
    mid = rest.astype(bf16)
    return high, mid, (rest - mid.astype(f32)).astype(bf16)


def dot(left, right, left_dim, right_dim):
    return lax.dot_general(
        left, right, (((left_dim,), (right_dim,)), ((), ())), preferred_element_type=f32
    )


def dot3(left, right, left_dim, right_dim):
    lh, ll = split2(left)
    rh, rl = split2(right)
    return (
        dot(lh, rh, left_dim, right_dim)
        + dot(lh, rl, left_dim, right_dim)
        + dot(ll, rh, left_dim, right_dim)
    )


def pieces(table):
    high = table.astype(bf16).astype(f32)
    rest = table - high
    mid = rest.astype(bf16).astype(f32)
    return jnp.concatenate([high, mid, rest - mid], axis=0).astype(bf16)


def whole(stack):
    return stack[0:ROWS] + stack[ROWS : 2 * ROWS] + stack[2 * ROWS : 3 * ROWS]


def onehot_rows(count, row):
    places = lax.broadcasted_iota(jnp.int32, (count, row.shape[1]), 0)
    return jnp.where(places == row, 1.0, 0.0).astype(bf16)


def column(row):
    n = row.shape[1]
    down = lax.broadcasted_iota(jnp.int32, (n, n), 0)
    across = lax.broadcasted_iota(jnp.int32, (n, n), 1)
    return jnp.sum(jnp.where(down == across, jnp.broadcast_to(row, (n, n)), 0.0), axis=1, keepdims=True)


def left_half(shape):
    return lax.broadcasted_iota(jnp.int32, shape, 1) < shape[1] // 2


def is_even():
    return lax.rem(lax.axis_index("yz"), 2) == 0


def previous_and_next(core, chip):
    even = is_even()
    return jnp.where(even, chip, core), jnp.where(even, core, chip)


def faces_yz(core, chip):
    before, after = previous_and_next(core, chip)
    return jnp.where(left_half(core.shape), before, after)


def returned_yz(core, chip):
    before, after = previous_and_next(core, chip)
    return jnp.where(left_half(core.shape), after, before)


def gamma_column(gammas, layer, count, width):
    which = lax.broadcasted_iota(jnp.int32, (count, width), 0)
    value = jnp.zeros((count, width), f32)
    for q in range(count):
        value = jnp.where(which == q, gammas[layer, q], value)
    return value


def radial_weights(w_rad, layer, entries):
    weights = w_rad[layer] * (1.0 / entries)
    high = weights.astype(bf16).astype(f32)
    low = weights - high
    return jnp.concatenate([high, low, high], axis=0).astype(bf16)


def radial(stacked_weights, basis):
    high = basis.astype(bf16).astype(f32)
    stacked = jnp.concatenate([high, high, basis - high], axis=0).astype(bf16)
    return dot(stacked_weights, stacked, 0, 0)


def geometry(entry, found, table, gamma, weights, u_ref, r_ref, y_ref, rad_ref, slope_ref):
    slots = found.shape[1]
    spread = lambda row: jnp.broadcast_to(row, (ROWS, slots))
    rx, ry, rz = [spread(found[d : d + 1] - table[d : d + 1, 0:slots]) for d in range(3)]
    square = rx * rx + ry * ry + rz * rz
    scale = lax.rsqrt(1.0 + square)
    ux, uy, uz = rx * scale, ry * scale, rz * scale
    basis = jnp.exp(-gamma * square)
    rad_ref[entry] = radial(weights, basis)
    if slope_ref is not None:
        slope_ref[entry] = radial(weights, -gamma * basis)
        r_ref[entry, 0] = rx
        r_ref[entry, 1] = ry
        r_ref[entry, 2] = rz
        r_ref[entry, 3] = scale
        u_ref[entry, 0] = ux
        u_ref[entry, 1] = uy
        u_ref[entry, 2] = uz
    unit_square = ux * ux + uy * uy + uz * uz
    y_ref[entry, 0] = root_three * ux
    y_ref[entry, 1] = root_three * uy
    y_ref[entry, 2] = root_three * uz
    y_ref[entry, 3] = root_fifteen * ux * uy
    y_ref[entry, 4] = root_fifteen * uy * uz
    y_ref[entry, 5] = 0.5 * root_five * (3.0 * uz * uz - unit_square)
    y_ref[entry, 6] = root_fifteen * ux * uz
    y_ref[entry, 7] = 0.5 * root_fifteen * (ux * ux - uy * uy)


def tile(index):
    return pl.ds(pl.multiple_of(index * ROWS, ROWS), ROWS)


def gather_sums(y_ref, rad_ref, feat_ref, sums_ref, invariant_ref):
    entries, channels, slots = feat_ref.shape
    for part in range(slots // LANES):
        lanes = pl.ds(part * LANES, LANES)

        def body(index, carry):
            rows = tile(index)
            sums = [None] * 9
            for k in range(entries):
                feat = feat_ref[k, rows, lanes]
                weighted = [
                    rad_ref[k, pl.ds(pl.multiple_of(degree * channels + index * ROWS, ROWS), ROWS), lanes] * feat
                    for degree in range(3)
                ]
                terms = [weighted[0]]
                for m in range(8):
                    terms.append(y_ref[k, m, :, lanes] * weighted[1 if m < 3 else 2])
                sums = terms if k == 0 else [old + new for old, new in zip(sums, terms)]
            total = sums[0]
            for m in range(8):
                total = total + sums[m + 1] * sums[m + 1]
                if sums_ref is not None:
                    sums_ref[m, rows, lanes] = sums[m + 1]
            invariant_ref[rows, lanes] = total
            return carry

        lax.fori_loop(0, channels // ROWS, body, 0, unroll=2)


def edge_gradients(u_ref, r_ref, rad_ref, slope_ref, feat_ref, sums_ref, g_ref, g_feat_ref, g_off_ref):
    entries, channels, slots = feat_ref.shape
    for part in range(slots // LANES):
        lanes = pl.ds(part * LANES, LANES)
        for k in range(entries):
            ux, uy, uz = [u_ref[k, d, :, lanes] for d in range(3)]

            def body(index, carry):
                rows = tile(index)
                degree_rows = [
                    pl.ds(pl.multiple_of(degree * channels + index * ROWS, ROWS), ROWS) for degree in range(3)
                ]
                g_s, g_x, g_y, g_z = carry
                g = g_ref[rows, lanes]
                feat = feat_ref[k, rows, lanes]
                s = [sums_ref[m, rows, lanes] for m in range(8)]
                b1, b2, b3 = [(2.0 * root_three) * s[m] for m in range(3)]
                c4, c5, c7, c8 = [(2.0 * root_fifteen) * s[m] for m in (3, 4, 6, 7)]
                c6 = (2.0 * root_five) * s[5]
                h_x = uy * c4 + uz * c7 + ux * (c8 - c6)
                h_y = ux * c4 + uz * c5 - uy * (c8 + c6)
                h_z = uy * c5 + ux * c7 + uz * (c6 + c6)
                one = ux * b1 + uy * b2 + uz * b3
                two = 0.5 * (ux * h_x + uy * h_y + uz * h_z)
                r0, r1, r2 = [rad_ref[k, d, lanes] for d in degree_rows]
                d0, d1, d2 = [slope_ref[k, d, lanes] for d in degree_rows]
                if g_feat_ref is not None:
                    g_feat_ref[k, rows, lanes] = g * (r0 + r1 * one + r2 * two)
                q = g * feat
                q1, q2 = q * r1, q * r2
                return (
                    g_s + q * (d0 + d1 * one + d2 * two),
                    g_x + (q1 * b1 + q2 * h_x),
                    g_y + (q1 * b2 + q2 * h_y),
                    g_z + (q1 * b3 + q2 * h_z),
                )

            zero = jnp.zeros((ROWS, LANES), f32)
            found = lax.fori_loop(0, channels // ROWS, body, (zero,) * 4, unroll=4)
            g_s, g_x, g_y, g_z = [jnp.sum(item, axis=0, keepdims=True) for item in found]
            rx, ry, rz, scale = [r_ref[k, d, 0:1, lanes] for d in range(4)]
            along = g_x * rx + g_y * ry + g_z * rz
            radial_part = 2.0 * g_s - scale * scale * scale * along
            g_off_ref[k, 0:1, lanes] = scale * g_x + rx * radial_part
            g_off_ref[k, 1:2, lanes] = scale * g_y + ry * radial_part
            g_off_ref[k, 2:3, lanes] = scale * g_z + rz * radial_part


def silu_and_slope(mixed):
    sigma = 1.0 / (1.0 + jnp.exp(-mixed))
    return mixed * sigma, sigma * (1.0 + mixed * (1.0 - sigma))


def species_features(code, count, weights):
    chosen = onehot_rows(count, code.astype(jnp.int32))
    high, mid, low = split3(weights)
    return dot(high, chosen, 1, 0) + dot(mid, chosen, 1, 0) + dot(low, chosen, 1, 0)


def pad_species(embed_ref, padded_ref):
    padded_ref[...] = jnp.zeros(padded_ref.shape, f32)
    padded_ref[0 : embed_ref.shape[0], :] = embed_ref[...]
    return padded_ref[...]


def pack_kernel(dest, count, pos, species, out):
    blocks, width = species.shape
    place = lax.broadcasted_iota(jnp.int32, (1, width), 1)
    out[...] = jnp.zeros(out.shape, f32)
    for group in range(3):
        coords = jnp.zeros((3, width), f32)
        code = jnp.full((1, width), -1.0, f32)
        for b in range(blocks):
            hit = dest[b, 0] == group
            coords = jnp.where(hit, pos[:, b * width : (b + 1) * width], coords)
            alive = jnp.where(place < count[b], species[b : b + 1, :].astype(f32), -1.0)
            code = jnp.where(hit, alive, code)
        out[group * ROWS : group * ROWS + 3, :] = coords
        out[group * ROWS + 3 : group * ROWS + 4, :] = code


def assemble_kernel(own, core, chip, lists, table, pick_gx, pick_yz):
    before, after = previous_and_next(core[...], chip[...])
    blocks = [after[0:ROWS], own[ROWS : 2 * ROWS, :], before[2 * ROWS : 3 * ROWS]]
    slots = jnp.concatenate(blocks, axis=1)
    table[...] = slots
    parts = pieces(slots)
    for row, out in ((0, pick_gx), (1, pick_yz)):
        out[...] = whole(dot(parts, onehot_rows(slots.shape[1], lists[row : row + 1, :]), 1, 0))


def send_features(h, lists, send_gx, send_yz):
    high, low = split2(h)
    for row, out in ((0, send_gx), (1, send_yz)):
        chosen = onehot_rows(h.shape[1], lists[row : row + 1, :])
        out[...] = dot(high, chosen, 1, 0) + dot(low, chosen, 1, 0)


def first_layer_kernel(
    gammas, table, got_gx, got_core, got_chip, nbr, lists, embed, w_up, w_rad, w_mix,
    ext, h_out, slope_out, send_gx, send_yz,
    padded, y_ref, rad_ref, feat_ref, inv_ref,
):
    slots = table.shape[1]
    entries = nbr.shape[0]
    ext_now = jnp.concatenate(
        [table[...], got_gx[...], faces_yz(got_core[...], got_chip[...])], axis=1
    )
    ext[...] = ext_now
    parts = pieces(ext_now)
    species = pad_species(embed, padded)
    up = dot3(w_up[0], species, 0, 1)
    gamma = gamma_column(gammas, 0, w_rad.shape[1], slots)
    weights = radial_weights(w_rad, 0, entries)
    for k in range(entries):
        found = whole(dot(parts, onehot_rows(ext_now.shape[1], nbr[k : k + 1, :]), 1, 0))
        geometry(k, found, ext_now, gamma, weights, None, None, y_ref, rad_ref, None)
        feat_ref[k] = species_features(found[3:4], ROWS, up)
    gather_sums(y_ref, rad_ref, feat_ref, None, inv_ref)
    mixed = dot3(w_mix[0], inv_ref[...], 0, 0)
    code = ext_now[3:4, 0:slots]
    live = jnp.where(code >= 0.0, 1.0, 0.0)
    h_zero = species_features(code, ROWS, species.T)
    value, slope = silu_and_slope(mixed)
    h_one = live * (h_zero + value)
    h_out[...] = h_one
    slope_out[...] = live * slope
    send_features(h_one, lists, send_gx, send_yz)


def second_layer_kernel(
    gammas, atom_ref, ext, h_one, got_gx, got_core, got_chip, nbr, w_up, w_rad, w_mix, readout,
    g_h, send_gx, send_yz, g_pos, tally,
    onehot, u_ref, r_ref, y_ref, rad_ref, slope_ref, feat_ref, sums_ref, inv_ref, g_ref, g_feat, g_off,
):
    entries, slots = nbr.shape
    ext_now = ext[...]
    wide = ext_now.shape[1]
    h_local = h_one[...]
    channels = h_local.shape[0]
    h_ext = jnp.concatenate(
        [h_local, got_gx[...], faces_yz(got_core[...], got_chip[...])], axis=1
    )
    projected = dot3(w_up[1], h_ext, 0, 0)
    high, low = split2(projected)
    table = jnp.concatenate([high, low], axis=0)
    parts = pieces(ext_now)
    gamma = gamma_column(gammas, 1, w_rad.shape[1], slots)
    weights = radial_weights(w_rad, 1, entries)
    for k in range(entries):
        chosen = onehot_rows(wide, nbr[k : k + 1, :])
        onehot[k] = chosen
        found = whole(dot(parts, chosen, 1, 0))
        geometry(k, found, ext_now, gamma, weights, u_ref, r_ref, y_ref, rad_ref, slope_ref)
        both = dot(table, chosen, 1, 0)
        feat_ref[k] = both[0:channels] + both[channels : 2 * channels]
    gather_sums(y_ref, rad_ref, feat_ref, sums_ref, inv_ref)
    mixed = dot3(w_mix[1], inv_ref[...], 0, 0)
    code = ext_now[3:4, 0:slots]
    live = jnp.where(code >= 0.0, 1.0, 0.0)
    value, slope = silu_and_slope(mixed)
    h_two = live * (h_local + value)
    read_one = column(readout[0:1, :])
    read_two = column(readout[1:2, :])
    energy = jnp.sum(read_one * h_local + read_two * h_two, axis=0, keepdims=True)
    for kind in range(atom_ref.shape[0]):
        energy = energy + jnp.where(code == float(kind), atom_ref[kind], 0.0)
    fold = lambda row: sum(row[:, c : c + LANES] for c in range(0, slots, LANES))
    tally[...] = jnp.zeros(tally.shape, f32)
    tally[0:1, :] = fold(energy)
    tally[1:2, :] = fold(live)
    g_ref[...] = dot3(w_mix[1], (live * read_two) * slope, 1, 0)
    g_off[...] = jnp.zeros(g_off.shape, f32)
    edge_gradients(u_ref, r_ref, rad_ref, slope_ref, feat_ref, sums_ref, g_ref, g_feat, g_off)
    g_proj = jnp.zeros((2 * channels, wide), f32)
    g_ext = jnp.zeros((3 * ROWS, wide), f32)
    own = jnp.zeros((ROWS, slots), f32)
    for k in range(entries):
        chosen = onehot[k]
        high, low = split2(g_feat[k])
        g_proj = g_proj + dot(jnp.concatenate([high, low], axis=0), chosen, 1, 1)
        g_ext = g_ext + dot(pieces(g_off[k]), chosen, 1, 1)
        own = own + g_off[k]
    g_all = dot3(w_up[1], g_proj[0:channels] + g_proj[channels : 2 * channels], 1, 0)
    g_h[...] = g_all[:, 0:slots] + live * (read_one + read_two)
    send_gx[...] = g_all[:, slots : slots + LANES]
    send_yz[...] = g_all[:, slots + LANES : slots + 2 * LANES]
    g_ext = whole(g_ext)
    g_pos[:, 0:slots] = g_ext[:, 0:slots] - own
    g_pos[:, slots:wide] = g_ext[:, slots:wide]


def first_gradient_kernel(
    gammas, ext, g_h, got_gx, got_core, got_chip, slope, g_pos_two, nbr, lists, embed, w_up, w_rad, w_mix,
    g_pos, send_gx, send_yz,
    padded, onehot, u_ref, r_ref, y_ref, rad_ref, slope_ref, feat_ref, sums_ref, inv_ref, g_ref, g_off,
):
    entries, slots = nbr.shape
    ext_now = ext[...]
    wide = ext_now.shape[1]
    parts = pieces(ext_now)
    species = pad_species(embed, padded)
    up = dot3(w_up[0], species, 0, 1)
    gamma = gamma_column(gammas, 0, w_rad.shape[1], slots)
    weights = radial_weights(w_rad, 0, entries)
    for k in range(entries):
        chosen = onehot_rows(wide, nbr[k : k + 1, :])
        onehot[k] = chosen
        found = whole(dot(parts, chosen, 1, 0))
        geometry(k, found, ext_now, gamma, weights, u_ref, r_ref, y_ref, rad_ref, slope_ref)
        feat_ref[k] = species_features(found[3:4], ROWS, up)
    gather_sums(y_ref, rad_ref, feat_ref, sums_ref, inv_ref)
    g_total = g_h[...]
    for row, back in ((0, got_gx[...]), (1, returned_yz(got_core[...], got_chip[...]))):
        chosen = onehot_rows(slots, lists[row : row + 1, :])
        high, low = split2(back)
        g_total = g_total + (dot(high, chosen, 1, 1) + dot(low, chosen, 1, 1))
    g_ref[...] = dot3(w_mix[0], g_total * slope[...], 1, 0)
    g_off[...] = jnp.zeros(g_off.shape, f32)
    edge_gradients(u_ref, r_ref, rad_ref, slope_ref, feat_ref, sums_ref, g_ref, None, g_off)
    g_ext = jnp.zeros((3 * ROWS, wide), f32)
    own = jnp.zeros((ROWS, slots), f32)
    for k in range(entries):
        g_ext = g_ext + dot(pieces(g_off[k]), onehot[k], 1, 1)
        own = own + g_off[k]
    g_ext = whole(g_ext) + g_pos_two[...]
    g_pos[...] = g_ext[:, 0:slots] - own
    send_gx[...] = g_ext[:, slots : slots + LANES]
    send_yz[...] = g_ext[:, slots + LANES : slots + 2 * LANES]


def force_kernel(g_pos, got_gx, got_core, got_chip, lists, forces):
    slots = g_pos.shape[1]
    total = g_pos[...]
    for row, back in ((0, got_gx[...]), (1, returned_yz(got_core[...], got_chip[...]))):
        chosen = onehot_rows(slots, lists[row : row + 1, :])
        total = total + whole(dot(pieces(back), chosen, 1, 1))
    forces[...] = -total[0:3]


def call(kernel, outs, scalars, arrays, scratch=(), name=None):
    in_vmem = pl.BlockSpec(memory_space=pltpu.VMEM)
    in_smem = pl.BlockSpec(memory_space=pltpu.SMEM)
    shapes = [jax.ShapeDtypeStruct(shape, f32) for shape in outs]
    return pl.pallas_call(
        kernel,
        out_shape=shapes,
        in_specs=[in_smem] * len(scalars) + [in_vmem] * len(arrays),
        out_specs=[in_vmem] * len(outs),
        scratch_shapes=[pltpu.VMEM(shape, kind) for shape, kind in scratch],
        compiler_params=pltpu.CompilerParams(vmem_limit_bytes=VMEM_BYTES),
        name=name,
    )(*scalars, *arrays)


def swap_core(value):
    size = lax.axis_size("yz")
    return lax.ppermute(value, "yz", [(i, i ^ 1) for i in range(size)])


def swap_chip(value):
    size = lax.axis_size("yz")
    return lax.ppermute(value, "yz", [(i, (i + 1 if i % 2 else i - 1) % size) for i in range(size)])


def shift(value, axis, by):
    size = lax.axis_size(axis)
    return lax.ppermute(value, axis, [(i, (i + by) % size) for i in range(size)])


def swap_gx(value):
    size = lax.axis_size("gx")
    if size == 2:
        return shift(value, "gx", 1)
    half = value.shape[1] // 2
    return jnp.concatenate(
        [shift(value[:, :half], "gx", 1), shift(value[:, half:], "gx", -1)], axis=1
    )


def return_gx(value):
    size = lax.axis_size("gx")
    if size == 2:
        return shift(value, "gx", 1)
    half = value.shape[1] // 2
    return jnp.concatenate(
        [shift(value[:, :half], "gx", -1), shift(value[:, half:], "gx", 1)], axis=1
    )


def sum_everywhere(value):
    for axis in ("yz", "gx"):
        size = lax.axis_size(axis)
        step = 1
        while step < size:
            value = value + lax.ppermute(value, axis, [(i, i ^ step) for i in range(size)])
            step *= 2
    return value


def shards(
    old_pos,
    old_species,
    block_dest,
    block_count,
    send_list,
    neighbours,
    embed,
    atom_ref,
    w_up,
    gammas,
    w_rad,
    w_mix,
    readout,
):
    entries, slots = neighbours.shape
    blocks = block_dest.shape[0]
    width = old_species.shape[0] // blocks
    channels = w_up.shape[1]
    wide = slots + send_list.size
    lists = send_list.reshape(2, -1)
    species = old_species.reshape(blocks, width)

    (packed,) = call(
        pack_kernel, [(3 * ROWS, width)], [block_dest, block_count], [old_pos, species], name="pack"
    )
    got_chip = swap_chip(packed)
    got_core = swap_core(packed)
    table, pick_gx, pick_yz = call(
        assemble_kernel,
        [(ROWS, slots), (ROWS, LANES), (ROWS, LANES)],
        [],
        [packed, got_core, got_chip, lists],
        name="assemble",
    )
    got_chip = swap_chip(pick_yz)
    got_gx = swap_gx(pick_gx)
    got_core = swap_core(pick_yz)
    rows = w_rad.shape[2]
    edge = ((entries, 8, ROWS, slots), f32)
    rad = ((entries, rows, slots), f32)
    feat = ((entries, channels, slots), f32)
    flat = ((channels, slots), f32)
    sums = ((8, channels, slots), f32)
    u_shape = ((entries, 3, ROWS, slots), f32)
    r_shape = ((entries, 4, ROWS, slots), f32)
    off = ((entries, ROWS, slots), f32)
    chosen = ((entries, wide, slots), bf16)
    padded = ((ROWS, channels), f32)
    square = (channels, LANES)

    ext, h_one, slope, send_gx, send_yz = call(
        first_layer_kernel,
        [(ROWS, wide), (channels, slots), (channels, slots), square, square],
        [gammas],
        [table, got_gx, got_core, got_chip, neighbours, lists, embed, w_up, w_rad, w_mix],
        [padded, edge, rad, feat, flat],
        name="first_layer",
    )
    got_chip = swap_chip(send_yz)
    got_gx = swap_gx(send_gx)
    got_core = swap_core(send_yz)
    g_h, send_gx, send_yz, g_pos_two, tally = call(
        second_layer_kernel,
        [(channels, slots), square, square, (ROWS, wide), (ROWS, LANES)],
        [gammas, atom_ref],
        [ext, h_one, got_gx, got_core, got_chip, neighbours, w_up, w_rad, w_mix, readout],
        [chosen, u_shape, r_shape, edge, rad, rad, feat, sums, flat, flat, feat, off],
        name="second_layer",
    )
    got_chip = swap_chip(send_yz)
    got_gx = return_gx(send_gx)
    got_core = swap_core(send_yz)
    g_pos, send_gx, send_yz = call(
        first_gradient_kernel,
        [(ROWS, slots), (ROWS, LANES), (ROWS, LANES)],
        [gammas],
        [ext, g_h, got_gx, got_core, got_chip, slope, g_pos_two, neighbours, lists, embed, w_up, w_rad, w_mix],
        [padded, chosen, u_shape, r_shape, edge, rad, rad, feat, sums, flat, flat, off],
        name="first_gradient",
    )
    got_chip = swap_chip(send_yz)
    got_gx = return_gx(send_gx)
    got_core = swap_core(send_yz)
    (forces,) = call(
        force_kernel, [(3, slots)], [], [g_pos, got_gx, got_core, got_chip, lists], name="forces"
    )
    tally = sum_everywhere(tally)
    energy = jnp.sum(tally[0]) / jnp.sum(tally[1])
    return (forces, energy)


def solution(mesh):
    return jax.shard_map(
        shards,
        mesh=mesh,
        in_specs=(
            P(None, ("gx", "yz")),
            P(("gx", "yz")),
            P(("gx", "yz"), None),
            P(("gx", "yz")),
            P(("gx", "yz"), None),
            P(None, ("gx", "yz")),
            P(),
            P(),
            P(),
            P(),
            P(),
            P(),
            P(),
        ),
        out_specs=(P(None, ("gx", "yz")), P()),
        check_vma=False,
    )
```

```python
import functools
import math

import jax
import jax.numpy as jnp
from jax import lax
from jax.experimental import pallas as pl
from jax.experimental.pallas import tpu as pltpu
from jax.sharding import PartitionSpec as P

root_three = math.sqrt(3.0)
root_five = math.sqrt(5.0)
root_fifteen = math.sqrt(15.0)
f32 = jnp.float32
bf16 = jnp.bfloat16
ROWS = 8
LANES = 128
VMEM_BYTES = 16 * 1024 * 1024


def split2(value):
    high = value.astype(bf16)
    return high, (value - high.astype(f32)).astype(bf16)


def split3(value):
    high = value.astype(bf16)
    rest = value - high.astype(f32)
    mid = rest.astype(bf16)
    return high, mid, (rest - mid.astype(f32)).astype(bf16)


def dot(left, right, left_dim, right_dim):
    return lax.dot_general(
        left, right, (((left_dim,), (right_dim,)), ((), ())), preferred_element_type=f32
    )


def dot3(left, right, left_dim, right_dim):
    lh, ll = split2(left)
    rh, rl = split2(right)
    return (
        dot(lh, rh, left_dim, right_dim)
        + dot(lh, rl, left_dim, right_dim)
        + dot(ll, rh, left_dim, right_dim)
    )


def pieces(table):
    high = table.astype(bf16).astype(f32)
    rest = table - high
    mid = rest.astype(bf16).astype(f32)
    return jnp.concatenate([high, mid, rest - mid], axis=0).astype(bf16)


def pieces_f32(table):
    high = table.astype(bf16).astype(f32)
    rest = table - high
    mid = rest.astype(bf16).astype(f32)
    return jnp.concatenate([high, mid, rest - mid], axis=0)


def whole(stack):
    return stack[0:ROWS] + stack[ROWS : 2 * ROWS] + stack[2 * ROWS : 3 * ROWS]


def onehot_rows(count, row):
    places = lax.broadcasted_iota(jnp.int32, (count, row.shape[1]), 0)
    return jnp.where(places == row, 1.0, 0.0).astype(bf16)


def column(row):
    n = row.shape[1]
    down = lax.broadcasted_iota(jnp.int32, (n, n), 0)
    across = lax.broadcasted_iota(jnp.int32, (n, n), 1)
    return jnp.sum(jnp.where(down == across, jnp.broadcast_to(row, (n, n)), 0.0), axis=1, keepdims=True)


def left_half(shape):
    return lax.broadcasted_iota(jnp.int32, shape, 1) < shape[1] // 2


def is_even():
    return lax.rem(lax.axis_index("yz"), 2) == 0


def previous_and_next(core, chip):
    even = is_even()
    return jnp.where(even, chip, core), jnp.where(even, core, chip)


def faces_yz(core, chip):
    before, after = previous_and_next(core, chip)
    return jnp.where(left_half(core.shape), before, after)


def returned_yz(core, chip):
    before, after = previous_and_next(core, chip)
    return jnp.where(left_half(core.shape), after, before)


def stacked_left(weights):
    high, low = split2(weights)
    return jnp.concatenate([high, high, low], axis=1)


def stacked_right(value):
    high, low = split2(value)
    return jnp.concatenate([high, low, high], axis=0)


def stacked_rows(value):
    high = value.astype(bf16).astype(f32)
    return jnp.concatenate([high, high, value - high], axis=0).astype(bf16)


def stacked_rows_left(value):
    high = value.astype(bf16).astype(f32)
    low = value - high
    return jnp.concatenate([high, low, high], axis=0)


def species_onehot(code, count):
    places = lax.rem(lax.broadcasted_iota(jnp.int32, (3 * count, code.shape[1]), 0), count)
    return jnp.where(places == code.astype(jnp.int32), 1.0, 0.0).astype(bf16)


def matmul(left, right):
    return dot(left, right, 1, 0)


def repeat(row, times):
    return jnp.concatenate([row] * times, axis=1)


def tile(index):
    return pl.ds(pl.multiple_of(index * ROWS, ROWS), ROWS)


def degree_tiles(index, channels):
    return [pl.ds(pl.multiple_of(degree * channels + index * ROWS, ROWS), ROWS) for degree in range(3)]


def lane_parts(slots, entries):
    for part in range(slots // LANES):
        yield pl.ds(part * LANES, LANES), [pl.ds(k * slots + part * LANES, LANES) for k in range(entries)]


U, R, SCALE, SQUARE = 0, 3, 6, 7


def gather_sums(y_ref, rad_ref, feat_ref, fields_ref, invariant_ref):
    channels, slots = invariant_ref.shape
    entries = feat_ref.shape[1] // slots
    for lanes, edges in lane_parts(slots, entries):
        angular = [[y_ref[m, :, edges[k]] for m in range(8)] for k in range(entries)]

        def body(index, carry):
            rows = tile(index)
            degrees = degree_tiles(index, channels)
            sums = None
            for k in range(entries):
                feat = feat_ref[rows, edges[k]]
                weighted = [rad_ref[degree, edges[k]] * feat for degree in degrees]
                terms = [weighted[0]] + [angular[k][m] * weighted[1 if m < 3 else 2] for m in range(8)]
                sums = terms if k == 0 else [old + new for old, new in zip(sums, terms)]
            total = sums[0]
            for item in sums[1:]:
                total = total + item * item
            invariant_ref[rows, lanes] = total
            a1, a2, a3, a4, a5, a6, a7, a8 = sums[1:]
            c6, c8 = (2.0 * root_five) * a6, (2.0 * root_fifteen) * a8
            fields = [(2.0 * root_three) * a for a in (a1, a2, a3)]
            fields += [(2.0 * root_fifteen) * a for a in (a4, a5, a7)]
            fields += [c8 - c6, c8 + c6, c6 + c6]
            for number, field in enumerate(fields):
                fields_ref[number, rows, lanes] = field
            return carry

        lax.fori_loop(0, channels // ROWS, body, 0, unroll=2)


def direction_terms(fields, unit):
    b1, b2, b3, c4, c5, c7, minus, plus, twice = fields
    ux, uy, uz = unit
    h_x = uy * c4 + uz * c7 + ux * minus
    h_y = ux * c4 + uz * c5 - uy * plus
    h_z = uy * c5 + ux * c7 + uz * twice
    one = ux * b1 + uy * b2 + uz * b3
    two = 0.5 * (ux * h_x + uy * h_y + uz * h_z)
    return h_x, h_y, h_z, one, two


def offset_gradients(found, geo_ref, edges):
    g_s, g_x, g_y, g_z = [jnp.sum(item, axis=0, keepdims=True) for item in found]
    rx, ry, rz = [geo_ref[R + d, 0:1, edges] for d in range(3)]
    scale = geo_ref[SCALE, 0:1, edges]
    along = g_x * rx + g_y * ry + g_z * rz
    radial_part = 2.0 * g_s - scale * scale * scale * along
    return scale * g_x + rx * radial_part, scale * g_y + ry * radial_part, scale * g_z + rz * radial_part


def silu_and_slope(mixed):
    sigma = 1.0 / (1.0 + jnp.exp(-mixed))
    return mixed * sigma, sigma * (1.0 + mixed * (1.0 - sigma))


def fetch(pairs, sems):
    copies = [pltpu.make_async_copy(source, target, sems.at[i]) for i, (source, target) in enumerate(pairs)]
    for copy in copies:
        copy.start()
    return copies


def pack_kernel(dest_hbm, count_hbm, pos_hbm, species_hbm, out, dest, count, pos, species, sems):
    copies = fetch(((dest_hbm, dest), (count_hbm, count), (pos_hbm, pos), (species_hbm, species)), sems)
    blocks, width = species.shape
    place = lax.broadcasted_iota(jnp.int32, (1, width), 1)
    out[...] = jnp.zeros(out.shape, f32)
    for copy in copies:
        copy.wait()
    for group in range(3):
        coords = jnp.zeros((3, width), f32)
        code = jnp.full((1, width), -1.0, f32)
        for b in range(blocks):
            hit = dest[0, b] == group
            coords = jnp.where(hit, pos[:, b * width : (b + 1) * width], coords)
            alive = jnp.where(place < count[b], species[b : b + 1, :].astype(f32), -1.0)
            code = jnp.where(hit, alive, code)
        out[group * ROWS : group * ROWS + 3, :] = coords
        out[group * ROWS + 3 : group * ROWS + 4, :] = code


def prepare_kernel(
    gammas_hbm, nbr_hbm, lists_hbm, embed_hbm, w_up_hbm, w_rad_hbm, w_mix_hbm, readout_hbm,
    onehot, send, gamma, radials, species_up, species_in, weights, reads, onehot_t, send_t,
    gammas, nbr, lists, embed, w_up, w_rad, w_mix, readout, padded, sems,
):
    copies = fetch(
        (
            (nbr_hbm, nbr),
            (lists_hbm, lists),
            (gammas_hbm, gammas),
            (w_rad_hbm, w_rad),
            (embed_hbm, embed),
            (w_up_hbm, w_up),
            (w_mix_hbm, w_mix),
            (readout_hbm, readout),
        ),
        sems,
    )
    entries, slots = nbr.shape
    for copy in copies:
        copy.wait()
    wide = onehot.shape[0]
    for k in range(entries):
        onehot[:, k * slots : (k + 1) * slots] = onehot_rows(wide, nbr[k : k + 1, :])
    faces, ghosts = lists.shape
    for face in range(faces):
        send[:, face * ghosts : (face + 1) * ghosts] = onehot_rows(slots, lists[face : face + 1, :])
    count = w_rad.shape[1]
    which = lax.broadcasted_iota(jnp.int32, gamma.shape[1:], 0)
    for layer in range(2):
        value = jnp.zeros(which.shape, f32)
        for q in range(count):
            value = jnp.where(which == q, gammas[layer, q], value)
        gamma[layer] = value
        radials[layer] = stacked_rows_left(w_rad[layer] * (1.0 / entries)).T.astype(bf16)
    padded[...] = jnp.zeros(padded.shape, f32)
    padded[0 : embed.shape[0], :] = embed[...]
    species = padded[...]
    species_up[...] = pieces_f32(dot3(species, w_up[0], 1, 0)).T.astype(bf16)
    species_in[...] = pieces_f32(species).T.astype(bf16)
    for number, item in enumerate(
        (w_mix[0].T, w_up[1].T, w_mix[1].T, w_mix[1], w_up[1], w_mix[0])
    ):
        weights[number] = stacked_left(item)
    for layer in range(2):
        reads[layer] = jnp.broadcast_to(column(readout[layer : layer + 1, :]), reads.shape[1:])
    index_rows = jnp.concatenate([nbr[...].astype(f32), jnp.zeros((ROWS - entries, slots), f32)], axis=0)
    index_columns = index_rows.T
    across = lax.broadcasted_iota(jnp.int32, (slots, wide), 1).astype(f32)
    for k in range(entries):
        onehot_t[k * slots : (k + 1) * slots, :] = jnp.where(
            across == index_columns[:, k : k + 1], 1.0, 0.0
        ).astype(bf16)
    list_rows = jnp.concatenate([lists[...].astype(f32), jnp.zeros((ROWS - faces, ghosts), f32)], axis=0)
    list_columns = list_rows.T
    across = lax.broadcasted_iota(jnp.int32, (ghosts, slots), 1).astype(f32)
    for face in range(faces):
        send_t[face * ghosts : (face + 1) * ghosts, :] = jnp.where(
            across == list_columns[:, face : face + 1], 1.0, 0.0
        ).astype(bf16)


def assemble_kernel(own, core, chip, send, table, pick_gx, pick_yz):
    before, after = previous_and_next(core[...], chip[...])
    blocks = [after[0:ROWS], own[ROWS : 2 * ROWS, :], before[2 * ROWS : 3 * ROWS]]
    slots = jnp.concatenate(blocks, axis=1)
    table[...] = slots
    picked = whole(matmul(pieces(slots), send[...]))
    pick_gx[...] = picked[:, 0:LANES]
    pick_yz[...] = picked[:, LANES : 2 * LANES]


def first_layer_kernel(
    table, got_gx, got_core, got_chip, onehot, send, gamma, radials, species_up, species_in, weights,
    h_out, slope_out, send_gx, send_yz, geo, y_ref, rad_ref, feat_ref, fields_ref,
    inv_ref,
):
    slots = table.shape[1]
    edges = onehot.shape[1]
    entries = edges // slots
    ext = jnp.concatenate([table[...], got_gx[...], faces_yz(got_core[...], got_chip[...])], axis=1)
    found = whole(matmul(pieces(ext), onehot[...]))
    feat_ref[...] = matmul(species_up[...], species_onehot(found[3:4], ROWS))
    spread = lambda row: jnp.broadcast_to(row, (ROWS, edges))
    rx, ry, rz = [
        spread(found[d : d + 1] - repeat(ext[d : d + 1, 0:slots], entries)) for d in range(3)
    ]
    square = rx * rx + ry * ry + rz * rz
    basis = jnp.exp(-gamma[0] * square)
    rad_ref[...] = matmul(radials[0], stacked_rows(basis))
    scale = lax.rsqrt(1.0 + square)
    ux, uy, uz = rx * scale, ry * scale, rz * scale
    for number, item in enumerate((ux, uy, uz, rx, ry, rz, scale, square)):
        geo[number] = item
    unit_square = ux * ux + uy * uy + uz * uz
    y_ref[0] = root_three * ux
    y_ref[1] = root_three * uy
    y_ref[2] = root_three * uz
    y_ref[3] = root_fifteen * ux * uy
    y_ref[4] = root_fifteen * uy * uz
    y_ref[5] = 0.5 * root_five * (3.0 * uz * uz - unit_square)
    y_ref[6] = root_fifteen * ux * uz
    y_ref[7] = 0.5 * root_fifteen * (ux * ux - uy * uy)
    gather_sums(y_ref, rad_ref, feat_ref, fields_ref, inv_ref)
    mixed = matmul(weights[0], stacked_right(inv_ref[...]))
    code = ext[3:4, 0:slots]
    live = jnp.where(code >= 0.0, 1.0, 0.0)
    h_zero = matmul(species_in[...], species_onehot(code, ROWS))
    value, slope = silu_and_slope(mixed)
    h_one = live * (h_zero + value)
    h_out[...] = h_one
    slope_out[...] = live * slope
    channels = h_one.shape[0]
    picked = matmul(jnp.concatenate(split2(h_one), axis=0), send[...])
    picked = picked[0:channels] + picked[channels : 2 * channels]
    send_gx[...] = picked[:, 0:LANES]
    send_yz[...] = picked[:, LANES : 2 * LANES]


def factor_kernel(
    atom_ref, geo, gamma, radials, table, rad_ref, feat_ref, fields_ref,
    factors, rad_two, slope_two, base,
    slope_ref,
):
    square = geo[SQUARE]
    basis = jnp.exp(-gamma[1] * square)
    rad_two[...] = matmul(radials[1], stacked_rows(basis))
    slope_two[...] = matmul(radials[1], stacked_rows(-gamma[1] * basis))
    slope_ref[...] = matmul(radials[0], stacked_rows(-gamma[0] * jnp.exp(-gamma[0] * square)))
    code = table[3:4, :]
    live = jnp.where(code >= 0.0, 1.0, 0.0)
    energy = jnp.zeros(code.shape, f32)
    for kind in range(atom_ref.shape[0]):
        energy = energy + jnp.where(code == float(kind), atom_ref[kind], 0.0)
    fold = lambda row: sum(row[:, c : c + LANES] for c in range(0, code.shape[1], LANES))
    base[...] = jnp.zeros(base.shape, f32)
    base[0:1, :] = fold(energy)
    base[1:2, :] = fold(live)
    channels, slots = fields_ref.shape[1:]
    entries = feat_ref.shape[1] // slots
    for lanes, edges in lane_parts(slots, entries):
        units = [[geo[U + d, :, edges[k]] for d in range(3)] for k in range(entries)]

        def body(index, carry):
            rows = tile(index)
            degrees = degree_tiles(index, channels)
            fields = [fields_ref[m, rows, lanes] for m in range(9)]
            for k in range(entries):
                h_x, h_y, h_z, one, two = direction_terms(fields, units[k])
                feat = feat_ref[rows, edges[k]]
                r1, r2 = [rad_ref[d, edges[k]] * feat for d in degrees[1:]]
                d0, d1, d2 = [slope_ref[d, edges[k]] for d in degrees]
                factors[0, rows, edges[k]] = feat * (d0 + d1 * one + d2 * two)
                factors[1, rows, edges[k]] = r1 * fields[0] + r2 * h_x
                factors[2, rows, edges[k]] = r1 * fields[1] + r2 * h_y
                factors[3, rows, edges[k]] = r1 * fields[2] + r2 * h_z
            return carry

        lax.fori_loop(0, channels // ROWS, body, 0)


def second_layer_kernel(
    base, table, h_one, got_gx, got_core, got_chip, onehot, y_ref, rad_ref, weights, reads,
    feat_ref, fields_ref, g_ref, g_own, tally,
    inv_ref,
):
    slots = table.shape[1]
    h_local = h_one[...]
    channels = h_local.shape[0]
    h_ext = jnp.concatenate([h_local, got_gx[...], faces_yz(got_core[...], got_chip[...])], axis=1)
    projected = matmul(weights[1], stacked_right(h_ext))
    both = matmul(jnp.concatenate(split2(projected), axis=0), onehot[...])
    feat_ref[...] = both[0:channels] + both[channels : 2 * channels]
    gather_sums(y_ref, rad_ref, feat_ref, fields_ref, inv_ref)
    mixed = matmul(weights[2], stacked_right(inv_ref[...]))
    live = jnp.where(table[3:4, :] >= 0.0, 1.0, 0.0)
    value, slope = silu_and_slope(mixed)
    h_two = live * (h_local + value)
    energy = jnp.sum(reads[0] * h_local + reads[1] * h_two, axis=0, keepdims=True)
    tally[...] = base[...]
    tally[0:1, :] += sum(energy[:, c : c + LANES] for c in range(0, slots, LANES))
    g_ref[...] = matmul(weights[3], stacked_right((live * reads[1]) * slope))
    g_own[...] = live * (reads[0] + reads[1])


def second_gradient_kernel(
    geo, rad_ref, slope_ref, feat_ref, fields_ref, g_ref, g_own, onehot_t, weights,
    g_h, send_gx, send_yz, g_pos,
    g_feat, g_off,
):
    channels, slots = g_ref.shape
    wide = onehot_t.shape[1]
    edge_count = feat_ref.shape[1]
    entries = edge_count // slots
    g_off[...] = jnp.zeros(g_off.shape, f32)
    for lanes, edges in lane_parts(slots, entries):
        units = [[geo[U + d, :, edges[k]] for d in range(3)] for k in range(entries)]

        def body(index, carry):
            rows = tile(index)
            degrees = degree_tiles(index, channels)
            g = g_ref[rows, lanes]
            fields = [g * fields_ref[m, rows, lanes] for m in range(9)]
            found = []
            for k in range(entries):
                h_x, h_y, h_z, one, two = direction_terms(fields, units[k])
                feat = feat_ref[rows, edges[k]]
                r0, r1, r2 = [rad_ref[d, edges[k]] for d in degrees]
                d0, d1, d2 = [slope_ref[d, edges[k]] for d in degrees]
                g_feat[rows, edges[k]] = g * r0 + r1 * one + r2 * two
                q1, q2 = feat * r1, feat * r2
                found += [
                    carry[4 * k] + feat * (g * d0 + d1 * one + d2 * two),
                    carry[4 * k + 1] + (q1 * fields[0] + q2 * h_x),
                    carry[4 * k + 2] + (q1 * fields[1] + q2 * h_y),
                    carry[4 * k + 3] + (q1 * fields[2] + q2 * h_z),
                ]
            return tuple(found)

        zero = jnp.zeros((ROWS, LANES), f32)
        found = lax.fori_loop(0, channels // ROWS, body, (zero,) * (4 * entries))
        for k in range(entries):
            for d, item in enumerate(offset_gradients(found[4 * k : 4 * k + 4], geo, edges[k])):
                g_off[d : d + 1, edges[k]] = item
    high, low = split2(g_feat[...])
    left = jnp.concatenate([high, low, pieces(g_off[...])], axis=0)
    scattered = matmul(left, onehot_t[...])
    g_proj = scattered[0:channels] + scattered[channels : 2 * channels]
    g_ext = whole(scattered[2 * channels : 2 * channels + 3 * ROWS])
    g_all = matmul(weights[4], stacked_right(g_proj))
    g_h[...] = g_all[:, 0:slots] + g_own[...]
    send_gx[...] = g_all[:, slots : slots + LANES]
    send_yz[...] = g_all[:, slots + LANES : slots + 2 * LANES]
    own = sum(g_off[:, k * slots : (k + 1) * slots] for k in range(entries))
    g_pos[:, 0:slots] = g_ext[:, 0:slots] - own
    g_pos[:, slots:wide] = g_ext[:, slots:wide]


def first_gradient_kernel(
    g_h, got_gx, got_core, got_chip, slope, factors, geo, g_pos_two, onehot_t, send_t, weights,
    g_pos, send_gx, send_yz,
    g_ref, g_off,
):
    channels, slots = slope.shape
    entries = geo.shape[2] // slots
    back = jnp.concatenate([got_gx[...], returned_yz(got_core[...], got_chip[...])], axis=1)
    returned = matmul(jnp.concatenate(split2(back), axis=0), send_t[...])
    g_total = g_h[...] + (returned[0:channels] + returned[channels : 2 * channels])
    g_ref[...] = matmul(weights[5], stacked_right(g_total * slope[...]))
    g_off[...] = jnp.zeros(g_off.shape, f32)
    for lanes, edges in lane_parts(slots, entries):

        def body(index, carry):
            rows = tile(index)
            g = g_ref[rows, lanes]
            return tuple(
                carry[4 * k + m] + g * factors[m, rows, edges[k]] for k in range(entries) for m in range(4)
            )

        zero = jnp.zeros((ROWS, LANES), f32)
        found = lax.fori_loop(0, channels // ROWS, body, (zero,) * (4 * entries), unroll=4)
        for k in range(entries):
            for d, item in enumerate(offset_gradients(found[4 * k : 4 * k + 4], geo, edges[k])):
                g_off[d : d + 1, edges[k]] = item
    g_ext = whole(matmul(pieces(g_off[...]), onehot_t[...])) + g_pos_two[...]
    own = sum(g_off[:, k * slots : (k + 1) * slots] for k in range(entries))
    g_pos[...] = g_ext[:, 0:slots] - own
    send_gx[...] = g_ext[:, slots : slots + LANES]
    send_yz[...] = g_ext[:, slots + LANES : slots + 2 * LANES]


def force_kernel(g_pos, got_gx, got_core, got_chip, send_t, *rest):
    tallies, (forces, energy) = rest[:-2], rest[-2:]
    back = jnp.concatenate([got_gx[...], returned_yz(got_core[...], got_chip[...])], axis=1)
    total = g_pos[...] + whole(matmul(pieces(back), send_t[...]))
    forces[...] = -total[0:3]
    sums = jnp.sum(sum(item[0:2, :] for item in tallies), axis=1, keepdims=True)
    energy[...] = sums[0:1, :] / sums[1:2, :]


def call(kernel, outs, scalars, arrays, scratch=(), name=None, raw=False, us=1.0):
    in_vmem = pl.BlockSpec(memory_space=pltpu.VMEM)
    in_smem = pl.BlockSpec(memory_space=pltpu.SMEM)
    in_hbm = pl.BlockSpec(memory_space=pltpu.HBM)
    shapes = [jax.ShapeDtypeStruct(*item) if isinstance(item[0], tuple) else jax.ShapeDtypeStruct(item, f32) for item in outs]
    return pl.pallas_call(
        kernel,
        out_shape=shapes,
        in_specs=[in_smem] * len(scalars) + [in_hbm if raw else in_vmem] * len(arrays),
        out_specs=[in_vmem] * len(outs),
        scratch_shapes=[pltpu.VMEM(item, f32) if isinstance(item, tuple) else item for item in scratch],
        compiler_params=pltpu.CompilerParams(vmem_limit_bytes=VMEM_BYTES),
        cost_estimate=pl.CostEstimate(flops=int(us * 1e9), bytes_accessed=int(us * 3e6), transcendentals=0),
        name=name,
    )(*scalars, *arrays)


def swap_core(value):
    size = lax.axis_size("yz")
    return lax.ppermute(value, "yz", [(i, i ^ 1) for i in range(size)])


def swap_chip(value):
    size = lax.axis_size("yz")
    return lax.ppermute(value, "yz", [(i, (i + 1 if i % 2 else i - 1) % size) for i in range(size)])


def shift(value, axis, by):
    size = lax.axis_size(axis)
    return lax.ppermute(value, axis, [(i, (i + by) % size) for i in range(size)])


def swap_gx(value):
    size = lax.axis_size("gx")
    if size == 2:
        return shift(value, "gx", 1)
    half = value.shape[1] // 2
    return jnp.concatenate(
        [shift(value[:, :half], "gx", 1), shift(value[:, half:], "gx", -1)], axis=1
    )


def return_gx(value):
    size = lax.axis_size("gx")
    if size == 2:
        return shift(value, "gx", 1)
    half = value.shape[1] // 2
    return jnp.concatenate(
        [shift(value[:, :half], "gx", -1), shift(value[:, half:], "gx", 1)], axis=1
    )


def group_parts(value, axis, bits):
    size = lax.axis_size(axis)
    steps = [0]
    for bit in bits:
        steps += [step ^ (1 << bit) for step in steps]
    return [lax.ppermute(value, axis, [(i, i ^ step) for i in range(size)]) if step else value for step in steps]


def shards(
    old_pos,
    old_species,
    block_dest,
    block_count,
    send_list,
    neighbours,
    embed,
    atom_ref,
    w_up,
    gammas,
    w_rad,
    w_mix,
    readout,
):
    entries, slots = neighbours.shape
    blocks = block_dest.shape[0]
    width = old_species.shape[0] // blocks
    channels = w_up.shape[1]
    ghosts = send_list.size
    wide = slots + ghosts
    edges = entries * slots
    rows = w_rad.shape[2]
    species = old_species.reshape(blocks, width)
    i32 = jnp.int32

    (packed,) = call(
        pack_kernel,
        [(3 * ROWS, width)],
        [],
        [block_dest.T, block_count, old_pos, species],
        [
            pltpu.SMEM((1, blocks), i32),
            pltpu.SMEM((blocks,), i32),
            old_pos.shape,
            pltpu.VMEM(species.shape, i32),
            pltpu.SemaphoreType.DMA((4,)),
        ],
        name="pack",
        raw=True,
    )
    got_chip = swap_chip(packed)
    got_core = swap_core(packed)
    onehot, send, gamma, radials, species_up, species_in, weights, reads, onehot_t, send_t = call(
        prepare_kernel,
        [
            ((wide, edges), bf16),
            ((slots, ghosts), bf16),
            (2, ROWS, edges),
            ((2, rows, 3 * ROWS), bf16),
            ((channels, 3 * ROWS), bf16),
            ((channels, 3 * ROWS), bf16),
            ((6, channels, 3 * channels), bf16),
            (2, channels, slots),
            ((edges, wide), bf16),
            ((ghosts, slots), bf16),
        ],
        [],
        [gammas, neighbours, send_list, embed, w_up, w_rad, w_mix, readout],
        [
            pltpu.SMEM(gammas.shape, f32),
            pltpu.VMEM(neighbours.shape, i32),
            pltpu.VMEM(send_list.shape, i32),
            embed.shape,
            w_up.shape,
            w_rad.shape,
            w_mix.shape,
            readout.shape,
            (ROWS, channels),
            pltpu.SemaphoreType.DMA((8,)),
        ],
        name="prepare",
        raw=True,
        us=3.0,
    )
    small = (ROWS, LANES)
    table, pick_gx, pick_yz = call(
        assemble_kernel,
        [(ROWS, slots), small, small],
        [],
        [packed, got_core, got_chip, send],
        name="assemble",
        us=0.2,
    )
    got_chip = swap_chip(pick_yz)
    got_gx = swap_gx(pick_gx)
    got_core = swap_core(pick_yz)
    flat = (channels, slots)
    square = (channels, LANES)
    fields_shape = (9, channels, slots)
    h_one, slope, send_gx, send_yz, geo, angular, rad_one, feat_one, fields_one = call(
        first_layer_kernel,
        [flat, flat, square, square, (8, ROWS, edges), (8, ROWS, edges), (rows, edges), (channels, edges), fields_shape],
        [],
        [table, got_gx, got_core, got_chip, onehot, send, gamma, radials, species_up, species_in, weights],
        [flat],
        name="first_layer",
        us=2.5,
    )
    got_chip = swap_chip(send_yz)
    got_gx = swap_gx(send_gx)
    got_core = swap_core(send_yz)
    factors, rad_two, slope_two, base = call(
        factor_kernel,
        [(4, channels, edges), (rows, edges), (rows, edges), small],
        [atom_ref],
        [geo, gamma, radials, table, rad_one, feat_one, fields_one],
        [(rows, edges)],
        name="factors",
        us=3.5,
    )
    feat_two, fields_two, g_two, g_own, tally = call(
        second_layer_kernel,
        [(channels, edges), fields_shape, flat, flat, small],
        [],
        [base, table, h_one, got_gx, got_core, got_chip, onehot, angular, rad_two, weights, reads],
        [flat],
        name="second_layer",
        us=2.5,
    )
    bits = (lax.axis_size("yz") - 1).bit_length()
    early = sorted({1, bits - 1} - {0})
    tally = sum(group_parts(tally, "yz", early))
    g_h, send_gx, send_yz, g_pos_two = call(
        second_gradient_kernel,
        [flat, square, square, (ROWS, wide)],
        [],
        [geo, rad_two, slope_two, feat_two, fields_two, g_two, g_own, onehot_t, weights],
        [(channels, edges), (ROWS, edges)],
        name="second_gradient",
        us=3.5,
    )
    got_chip = swap_chip(send_yz)
    got_gx = return_gx(send_gx)
    got_core = swap_core(send_yz)
    tally = tally + swap_core(tally)
    g_pos, send_gx, send_yz = call(
        first_gradient_kernel,
        [(ROWS, slots), small, small],
        [],
        [g_h, got_gx, got_core, got_chip, slope, factors, geo, g_pos_two, onehot_t, send_t, weights],
        [flat, (ROWS, edges)],
        name="first_gradient",
        us=1.2,
    )
    tally = sum(group_parts(tally, "yz", [bit for bit in range(1, bits) if bit not in early]))
    got_chip = swap_chip(send_yz)
    got_gx = return_gx(send_gx)
    got_core = swap_core(send_yz)
    tallies = group_parts(tally, "gx", range((lax.axis_size("gx") - 1).bit_length()))
    forces, energy = call(
        force_kernel,
        [(3, slots), (1, 1)],
        [],
        [g_pos, got_gx, got_core, got_chip, send_t] + tallies,
        name="forces",
    )
    return (forces, energy.reshape(()))


def solution(mesh):
    return jax.shard_map(
        shards,
        mesh=mesh,
        in_specs=(
            P(None, ("gx", "yz")),
            P(("gx", "yz")),
            P(("gx", "yz"), None),
            P(("gx", "yz")),
            P(("gx", "yz"), None),
            P(None, ("gx", "yz")),
            P(),
            P(),
            P(),
            P(),
            P(),
            P(),
            P(),
        ),
        out_specs=(P(None, ("gx", "yz")), P()),
        check_vma=False,
    )
```

```python
import functools
import math

import jax
import jax.numpy as jnp
from jax import lax
from jax.experimental import pallas as pl
from jax.experimental.pallas import tpu as pltpu
from jax.sharding import PartitionSpec as P

root_three = math.sqrt(3.0)
root_five = math.sqrt(5.0)
root_fifteen = math.sqrt(15.0)
f32 = jnp.float32
bf16 = jnp.bfloat16
ROWS = 8
LANES = 128
TALL = 64
CHIP_ROWS = 32
VMEM_BYTES = 16 * 1024 * 1024


def split2(value):
    high = value.astype(bf16)
    return high, (value - high.astype(f32)).astype(bf16)


def split3(value):
    high = value.astype(bf16)
    rest = value - high.astype(f32)
    mid = rest.astype(bf16)
    return high, mid, (rest - mid.astype(f32)).astype(bf16)


def dot(left, right, left_dim, right_dim):
    return lax.dot_general(
        left, right, (((left_dim,), (right_dim,)), ((), ())), preferred_element_type=f32
    )


def dot3(left, right, left_dim, right_dim):
    lh, ll = split2(left)
    rh, rl = split2(right)
    return (
        dot(lh, rh, left_dim, right_dim)
        + dot(lh, rl, left_dim, right_dim)
        + dot(ll, rh, left_dim, right_dim)
    )


def pieces(table):
    high = table.astype(bf16).astype(f32)
    rest = table - high
    mid = rest.astype(bf16).astype(f32)
    return jnp.concatenate([high, mid, rest - mid], axis=0).astype(bf16)


def pieces_f32(table):
    high = table.astype(bf16).astype(f32)
    rest = table - high
    mid = rest.astype(bf16).astype(f32)
    return jnp.concatenate([high, mid, rest - mid], axis=0)


def whole(stack):
    return stack[0:ROWS] + stack[ROWS : 2 * ROWS] + stack[2 * ROWS : 3 * ROWS]


def onehot_rows(count, row):
    places = lax.broadcasted_iota(jnp.int32, (count, row.shape[1]), 0)
    return jnp.where(places == row, 1.0, 0.0).astype(bf16)


def column(row):
    n = row.shape[1]
    down = lax.broadcasted_iota(jnp.int32, (n, n), 0)
    across = lax.broadcasted_iota(jnp.int32, (n, n), 1)
    return jnp.sum(jnp.where(down == across, jnp.broadcast_to(row, (n, n)), 0.0), axis=1, keepdims=True)


def left_half(shape):
    return lax.broadcasted_iota(jnp.int32, shape, 1) < shape[1] // 2


def is_even():
    return lax.rem(lax.axis_index("yz"), 2) == 0


def previous_and_next(core, chip):
    even = is_even()
    return jnp.where(even, chip, core), jnp.where(even, core, chip)


def faces_yz(core, chip):
    before, after = previous_and_next(core, chip)
    return jnp.where(left_half(core.shape), before, after)


def returned_yz(core, chip):
    before, after = previous_and_next(core, chip)
    return jnp.where(left_half(core.shape), after, before)


def pack_halves(value):
    half = value.shape[0] // 2
    top, bottom = value[0:half], value[half:]
    left = left_half(top.shape)
    turned_top, turned_bottom = pltpu.roll(top, LANES // 2, 1), pltpu.roll(bottom, LANES // 2, 1)
    return jnp.where(left, top, turned_bottom), jnp.where(left, turned_top, bottom)


def join_halves(left_columns, right_columns):
    left = left_half(left_columns.shape)
    top = jnp.where(left, left_columns, pltpu.roll(right_columns, LANES // 2, 1))
    bottom = jnp.where(left, pltpu.roll(left_columns, LANES // 2, 1), right_columns)
    return jnp.concatenate([top, bottom], axis=0)


def stacked_left(weights):
    high, low = split2(weights)
    return jnp.concatenate([high, high, low], axis=1)


def stacked_right(value):
    high, low = split2(value)
    return jnp.concatenate([high, low, high], axis=0)


def stacked_rows(value):
    high = value.astype(bf16).astype(f32)
    return jnp.concatenate([high, high, value - high], axis=0).astype(bf16)


def stacked_rows_left(value):
    high = value.astype(bf16).astype(f32)
    low = value - high
    return jnp.concatenate([high, low, high], axis=0)


def species_onehot(code, count):
    places = lax.rem(lax.broadcasted_iota(jnp.int32, (3 * count, code.shape[1]), 0), count)
    return jnp.where(places == code.astype(jnp.int32), 1.0, 0.0).astype(bf16)


def matmul(left, right):
    return dot(left, right, 1, 0)


def repeat(row, times):
    return jnp.concatenate([row] * times, axis=1)


def tile(index):
    return pl.ds(pl.multiple_of(index * ROWS, ROWS), ROWS)


def degree_tiles(index, channels):
    return [pl.ds(pl.multiple_of(degree * channels + index * ROWS, ROWS), ROWS) for degree in range(3)]


def lane_parts(slots, entries):
    for part in range(slots // LANES):
        yield pl.ds(part * LANES, LANES), [pl.ds(k * slots + part * LANES, LANES) for k in range(entries)]


U, R, SCALE, SQUARE = 0, 3, 6, 7


def gather_sums(y_ref, rad_ref, feat_ref, fields_ref, invariant_ref):
    channels, slots = invariant_ref.shape
    entries = feat_ref.shape[1] // slots
    for lanes, edges in lane_parts(slots, entries):
        angular = [[y_ref[m, :, edges[k]] for m in range(8)] for k in range(entries)]

        def body(index, carry):
            rows = tile(index)
            degrees = degree_tiles(index, channels)
            sums = None
            for k in range(entries):
                feat = feat_ref[rows, edges[k]]
                weighted = [rad_ref[degree, edges[k]] * feat for degree in degrees]
                terms = [weighted[0]] + [angular[k][m] * weighted[1 if m < 3 else 2] for m in range(8)]
                sums = terms if k == 0 else [old + new for old, new in zip(sums, terms)]
            total = sums[0]
            for item in sums[1:]:
                total = total + item * item
            invariant_ref[rows, lanes] = total
            a1, a2, a3, a4, a5, a6, a7, a8 = sums[1:]
            c6, c8 = (2.0 * root_five) * a6, (2.0 * root_fifteen) * a8
            fields = [(2.0 * root_three) * a for a in (a1, a2, a3)]
            fields += [(2.0 * root_fifteen) * a for a in (a4, a5, a7)]
            fields += [c8 - c6, c8 + c6, c6 + c6]
            for number, field in enumerate(fields):
                fields_ref[number, rows, lanes] = field
            return carry

        lax.fori_loop(0, channels // ROWS, body, 0, unroll=2)


def direction_terms(fields, unit):
    b1, b2, b3, c4, c5, c7, minus, plus, twice = fields
    ux, uy, uz = unit
    h_x = uy * c4 + uz * c7 + ux * minus
    h_y = ux * c4 + uz * c5 - uy * plus
    h_z = uy * c5 + ux * c7 + uz * twice
    one = ux * b1 + uy * b2 + uz * b3
    two = 0.5 * (ux * h_x + uy * h_y + uz * h_z)
    return h_x, h_y, h_z, one, two


def offset_gradients(found, geo_ref, edges):
    g_s, g_x, g_y, g_z = [jnp.sum(item, axis=0, keepdims=True) for item in found]
    rx, ry, rz = [geo_ref[R + d, 0:1, edges] for d in range(3)]
    scale = geo_ref[SCALE, 0:1, edges]
    along = g_x * rx + g_y * ry + g_z * rz
    radial_part = 2.0 * g_s - scale * scale * scale * along
    return scale * g_x + rx * radial_part, scale * g_y + ry * radial_part, scale * g_z + rz * radial_part


def silu_and_slope(mixed):
    sigma = 1.0 / (1.0 + jnp.exp(-mixed))
    return mixed * sigma, sigma * (1.0 + mixed * (1.0 - sigma))


def fetch(pairs, sems):
    copies = [pltpu.make_async_copy(source, target, sems.at[i]) for i, (source, target) in enumerate(pairs)]
    for copy in copies:
        copy.start()
    return copies


def pack_kernel(dest_hbm, count_hbm, pos_hbm, species_hbm, out, dest, count, pos, species, sems):
    copies = fetch(((dest_hbm, dest), (count_hbm, count), (pos_hbm, pos), (species_hbm, species)), sems)
    blocks, width = species.shape
    place = lax.broadcasted_iota(jnp.int32, (1, width), 1)
    out[...] = jnp.zeros(out.shape, f32)
    for copy in copies:
        copy.wait()
    for group in range(3):
        coords = jnp.zeros((3, width), f32)
        code = jnp.full((1, width), -1.0, f32)
        for b in range(blocks):
            hit = dest[0, b] == group
            coords = jnp.where(hit, pos[:, b * width : (b + 1) * width], coords)
            alive = jnp.where(place < count[b], species[b : b + 1, :].astype(f32), -1.0)
            code = jnp.where(hit, alive, code)
        out[group * ROWS : group * ROWS + 3, :] = coords
        out[group * ROWS + 3 : group * ROWS + 4, :] = code


def prepare_kernel(
    gammas_hbm, nbr_hbm, lists_hbm, embed_hbm, w_up_hbm, w_rad_hbm, w_mix_hbm, readout_hbm,
    onehot, send, gamma, radials, species_up, species_in, weights, reads, onehot_t, send_t,
    gammas, nbr, lists, embed, w_up, w_rad, w_mix, readout, padded, sems,
):
    copies = fetch(
        (
            (nbr_hbm, nbr),
            (lists_hbm, lists),
            (gammas_hbm, gammas),
            (w_rad_hbm, w_rad),
            (embed_hbm, embed),
            (w_up_hbm, w_up),
            (w_mix_hbm, w_mix),
            (readout_hbm, readout),
        ),
        sems,
    )
    entries, slots = nbr.shape
    for copy in copies:
        copy.wait()
    wide = onehot.shape[0]
    for k in range(entries):
        onehot[:, k * slots : (k + 1) * slots] = onehot_rows(wide, nbr[k : k + 1, :])
    faces, ghosts = lists.shape
    for face in range(faces):
        send[:, face * ghosts : (face + 1) * ghosts] = onehot_rows(slots, lists[face : face + 1, :])
    count = w_rad.shape[1]
    which = lax.broadcasted_iota(jnp.int32, gamma.shape[1:], 0)
    for layer in range(2):
        value = jnp.zeros(which.shape, f32)
        for q in range(count):
            value = jnp.where(which == q, gammas[layer, q], value)
        gamma[layer] = value
        radials[layer] = stacked_rows_left(w_rad[layer] * (1.0 / entries)).T.astype(bf16)
    padded[...] = jnp.zeros(padded.shape, f32)
    padded[0 : embed.shape[0], :] = embed[...]
    species = padded[...]
    species_up[...] = pieces_f32(dot3(species, w_up[0], 1, 0)).T.astype(bf16)
    species_in[...] = pieces_f32(species).T.astype(bf16)
    for number, item in enumerate(
        (w_mix[0].T, w_up[1].T, w_mix[1].T, w_mix[1], w_up[1], w_mix[0])
    ):
        weights[number] = stacked_left(item)
    for layer in range(2):
        reads[layer] = jnp.broadcast_to(column(readout[layer : layer + 1, :]), reads.shape[1:])
    index_rows = jnp.concatenate([nbr[...].astype(f32), jnp.zeros((ROWS - entries, slots), f32)], axis=0)
    index_columns = index_rows.T
    across = lax.broadcasted_iota(jnp.int32, (slots, wide), 1).astype(f32)
    for k in range(entries):
        onehot_t[k * slots : (k + 1) * slots, :] = jnp.where(
            across == index_columns[:, k : k + 1], 1.0, 0.0
        ).astype(bf16)
    list_rows = jnp.concatenate([lists[...].astype(f32), jnp.zeros((ROWS - faces, ghosts), f32)], axis=0)
    list_columns = list_rows.T
    across = lax.broadcasted_iota(jnp.int32, (ghosts, slots), 1).astype(f32)
    for face in range(faces):
        send_t[face * ghosts : (face + 1) * ghosts, :] = jnp.where(
            across == list_columns[:, face : face + 1], 1.0, 0.0
        ).astype(bf16)


def assemble_kernel(own, core, chip, send, table, pick_gx, pick_core, pick_chip):
    before, after = previous_and_next(core[...], chip[...])
    blocks = [after[0:ROWS], own[ROWS : 2 * ROWS, :], before[2 * ROWS : 3 * ROWS]]
    slots = jnp.concatenate(blocks, axis=1)
    table[...] = slots
    picked = whole(matmul(pieces(slots), send[...]))
    pick_gx[...] = picked[:, 0:LANES]
    pick_core[...] = picked[:, LANES : 2 * LANES]
    pick_chip[...] = jnp.zeros(pick_chip.shape, f32)
    pick_chip[0:ROWS, :] = picked[:, LANES : 2 * LANES]


def first_layer_kernel(
    table, got_gx, got_core, got_chip, onehot, send, gamma, radials, species_up, species_in, weights,
    h_out, slope_out, send_gx, send_core, send_chip, geo, y_ref, rad_ref, feat_ref, fields_ref,
    inv_ref,
):
    slots = table.shape[1]
    edges = onehot.shape[1]
    entries = edges // slots
    ext = jnp.concatenate([table[...], got_gx[...], faces_yz(got_core[...], got_chip[0:ROWS, :])], axis=1)
    found = whole(matmul(pieces(ext), onehot[...]))
    feat_ref[...] = matmul(species_up[...], species_onehot(found[3:4], ROWS))
    spread = lambda row: jnp.broadcast_to(row, (ROWS, edges))
    rx, ry, rz = [
        spread(found[d : d + 1] - repeat(ext[d : d + 1, 0:slots], entries)) for d in range(3)
    ]
    square = rx * rx + ry * ry + rz * rz
    basis = jnp.exp(-gamma[0] * square)
    rad_ref[...] = matmul(radials[0], stacked_rows(basis))
    scale = lax.rsqrt(1.0 + square)
    ux, uy, uz = rx * scale, ry * scale, rz * scale
    for number, item in enumerate((ux, uy, uz, rx, ry, rz, scale, square)):
        geo[number] = item
    unit_square = ux * ux + uy * uy + uz * uz
    y_ref[0] = root_three * ux
    y_ref[1] = root_three * uy
    y_ref[2] = root_three * uz
    y_ref[3] = root_fifteen * ux * uy
    y_ref[4] = root_fifteen * uy * uz
    y_ref[5] = 0.5 * root_five * (3.0 * uz * uz - unit_square)
    y_ref[6] = root_fifteen * ux * uz
    y_ref[7] = 0.5 * root_fifteen * (ux * ux - uy * uy)
    gather_sums(y_ref, rad_ref, feat_ref, fields_ref, inv_ref)
    mixed = matmul(weights[0], stacked_right(inv_ref[...]))
    code = ext[3:4, 0:slots]
    live = jnp.where(code >= 0.0, 1.0, 0.0)
    h_zero = matmul(species_in[...], species_onehot(code, ROWS))
    value, slope = silu_and_slope(mixed)
    h_one = live * (h_zero + value)
    h_out[...] = h_one
    slope_out[...] = live * slope
    channels = h_one.shape[0]
    picked = matmul(jnp.concatenate(split2(h_one), axis=0), send[...])
    picked = picked[0:channels] + picked[channels : 2 * channels]
    send_gx[...] = picked[:, 0:LANES]
    to_next, to_previous = pack_halves(picked[:, LANES : 2 * LANES])
    even = is_even()
    send_core[...] = jnp.where(even, to_next, to_previous)
    send_chip[...] = jnp.where(even, to_previous, to_next)


def factor_kernel(
    atom_ref, geo, gamma, radials, table, rad_ref, feat_ref, fields_ref,
    factors, rad_two, slope_two, base,
    slope_ref,
):
    square = geo[SQUARE]
    basis = jnp.exp(-gamma[1] * square)
    rad_two[...] = matmul(radials[1], stacked_rows(basis))
    slope_two[...] = matmul(radials[1], stacked_rows(-gamma[1] * basis))
    slope_ref[...] = matmul(radials[0], stacked_rows(-gamma[0] * jnp.exp(-gamma[0] * square)))
    code = table[3:4, :]
    live = jnp.where(code >= 0.0, 1.0, 0.0)
    energy = jnp.zeros(code.shape, f32)
    for kind in range(atom_ref.shape[0]):
        energy = energy + jnp.where(code == float(kind), atom_ref[kind], 0.0)
    fold = lambda row: sum(row[:, c : c + LANES] for c in range(0, code.shape[1], LANES))
    base[...] = jnp.zeros(base.shape, f32)
    base[0:1, :] = fold(energy)
    base[1:2, :] = fold(live)
    channels, slots = fields_ref.shape[1:]
    entries = feat_ref.shape[1] // slots
    for lanes, edges in lane_parts(slots, entries):
        units = [[geo[U + d, :, edges[k]] for d in range(3)] for k in range(entries)]

        def body(index, carry):
            rows = tile(index)
            degrees = degree_tiles(index, channels)
            fields = [fields_ref[m, rows, lanes] for m in range(9)]
            for k in range(entries):
                h_x, h_y, h_z, one, two = direction_terms(fields, units[k])
                feat = feat_ref[rows, edges[k]]
                r1, r2 = [rad_ref[d, edges[k]] * feat for d in degrees[1:]]
                d0, d1, d2 = [slope_ref[d, edges[k]] for d in degrees]
                factors[0, rows, edges[k]] = feat * (d0 + d1 * one + d2 * two)
                factors[1, rows, edges[k]] = r1 * fields[0] + r2 * h_x
                factors[2, rows, edges[k]] = r1 * fields[1] + r2 * h_y
                factors[3, rows, edges[k]] = r1 * fields[2] + r2 * h_z
            return carry

        lax.fori_loop(0, channels // ROWS, body, 0)


def second_layer_kernel(
    base, table, h_one, got_gx, got_core, got_chip, onehot, y_ref, rad_ref, weights, reads,
    feat_ref, fields_ref, g_ref, g_own, tally,
    inv_ref,
):
    slots = table.shape[1]
    h_local = h_one[...]
    channels = h_local.shape[0]
    before, after = previous_and_next(got_core[...], got_chip[...])
    h_ext = jnp.concatenate([h_local, got_gx[...], join_halves(before, after)], axis=1)
    projected = matmul(weights[1], stacked_right(h_ext))
    both = matmul(jnp.concatenate(split2(projected), axis=0), onehot[...])
    feat_ref[...] = both[0:channels] + both[channels : 2 * channels]
    gather_sums(y_ref, rad_ref, feat_ref, fields_ref, inv_ref)
    mixed = matmul(weights[2], stacked_right(inv_ref[...]))
    live = jnp.where(table[3:4, :] >= 0.0, 1.0, 0.0)
    value, slope = silu_and_slope(mixed)
    h_two = live * (h_local + value)
    energy = jnp.sum(reads[0] * h_local + reads[1] * h_two, axis=0, keepdims=True)
    tally[...] = base[...]
    tally[0:1, :] += sum(energy[:, c : c + LANES] for c in range(0, slots, LANES))
    g_ref[...] = matmul(weights[3], stacked_right((live * reads[1]) * slope))
    g_own[...] = live * (reads[0] + reads[1])


def second_gradient_kernel(
    geo, rad_ref, slope_ref, feat_ref, fields_ref, g_ref, g_own, onehot_t, weights,
    g_h, send_gx, send_core, send_chip, g_pos,
    g_feat, g_off,
):
    channels, slots = g_ref.shape
    wide = onehot_t.shape[1]
    edge_count = feat_ref.shape[1]
    entries = edge_count // slots
    g_off[...] = jnp.zeros(g_off.shape, f32)
    for lanes, edges in lane_parts(slots, entries):
        units = [[geo[U + d, :, edges[k]] for d in range(3)] for k in range(entries)]

        def body(index, carry):
            rows = tile(index)
            degrees = degree_tiles(index, channels)
            g = g_ref[rows, lanes]
            fields = [g * fields_ref[m, rows, lanes] for m in range(9)]
            found = []
            for k in range(entries):
                h_x, h_y, h_z, one, two = direction_terms(fields, units[k])
                feat = feat_ref[rows, edges[k]]
                r0, r1, r2 = [rad_ref[d, edges[k]] for d in degrees]
                d0, d1, d2 = [slope_ref[d, edges[k]] for d in degrees]
                g_feat[rows, edges[k]] = g * r0 + r1 * one + r2 * two
                q1, q2 = feat * r1, feat * r2
                found += [
                    carry[4 * k] + feat * (g * d0 + d1 * one + d2 * two),
                    carry[4 * k + 1] + (q1 * fields[0] + q2 * h_x),
                    carry[4 * k + 2] + (q1 * fields[1] + q2 * h_y),
                    carry[4 * k + 3] + (q1 * fields[2] + q2 * h_z),
                ]
            return tuple(found)

        zero = jnp.zeros((ROWS, LANES), f32)
        found = lax.fori_loop(0, channels // ROWS, body, (zero,) * (4 * entries))
        for k in range(entries):
            for d, item in enumerate(offset_gradients(found[4 * k : 4 * k + 4], geo, edges[k])):
                g_off[d : d + 1, edges[k]] = item
    high, low = split2(g_feat[...])
    left = jnp.concatenate([high, low, pieces(g_off[...])], axis=0)
    scattered = matmul(left, onehot_t[...])
    g_proj = scattered[0:channels] + scattered[channels : 2 * channels]
    g_ext = whole(scattered[2 * channels : 2 * channels + 3 * ROWS])
    g_all = matmul(weights[4], stacked_right(g_proj))
    g_h[...] = g_all[:, 0:slots] + g_own[...]
    send_gx[...] = g_all[:, slots : slots + LANES]
    to_previous, to_next = pack_halves(g_all[:, slots + LANES : slots + 2 * LANES])
    even = is_even()
    send_core[...] = jnp.where(even, to_next, to_previous)
    send_chip[...] = jnp.where(even, to_previous, to_next)
    own = sum(g_off[:, k * slots : (k + 1) * slots] for k in range(entries))
    g_pos[:, 0:slots] = g_ext[:, 0:slots] - own
    g_pos[:, slots:wide] = g_ext[:, slots:wide]


def first_gradient_kernel(
    g_h, got_gx, got_core, got_chip, slope, factors, geo, g_pos_two, onehot_t, send_t, weights,
    g_pos, send_gx, send_core, send_chip,
    g_ref, g_off,
):
    channels, slots = slope.shape
    entries = geo.shape[2] // slots
    before, after = previous_and_next(got_core[...], got_chip[...])
    back = jnp.concatenate([got_gx[...], join_halves(after, before)], axis=1)
    returned = matmul(jnp.concatenate(split2(back), axis=0), send_t[...])
    g_total = g_h[...] + (returned[0:channels] + returned[channels : 2 * channels])
    g_ref[...] = matmul(weights[5], stacked_right(g_total * slope[...]))
    g_off[...] = jnp.zeros(g_off.shape, f32)
    for lanes, edges in lane_parts(slots, entries):

        def body(index, carry):
            rows = tile(index)
            g = g_ref[rows, lanes]
            return tuple(
                carry[4 * k + m] + g * factors[m, rows, edges[k]] for k in range(entries) for m in range(4)
            )

        zero = jnp.zeros((ROWS, LANES), f32)
        found = lax.fori_loop(0, channels // ROWS, body, (zero,) * (4 * entries), unroll=4)
        for k in range(entries):
            for d, item in enumerate(offset_gradients(found[4 * k : 4 * k + 4], geo, edges[k])):
                g_off[d : d + 1, edges[k]] = item
    g_ext = whole(matmul(pieces(g_off[...]), onehot_t[...])) + g_pos_two[...]
    own = sum(g_off[:, k * slots : (k + 1) * slots] for k in range(entries))
    g_pos[...] = g_ext[:, 0:slots] - own
    send_gx[...] = g_ext[:, slots : slots + LANES]
    send_core[...] = g_ext[:, slots + LANES : slots + 2 * LANES]
    send_chip[...] = jnp.zeros(send_chip.shape, f32)
    send_chip[0:ROWS, :] = g_ext[:, slots + LANES : slots + 2 * LANES]


def force_kernel(g_pos, got_gx, got_core, got_chip, send_t, *rest):
    tallies, (forces, energy) = rest[:-2], rest[-2:]
    back = jnp.concatenate([got_gx[...], returned_yz(got_core[...], got_chip[0:ROWS, :])], axis=1)
    total = g_pos[...] + whole(matmul(pieces(back), send_t[...]))
    forces[...] = -total[0:3]
    sums = jnp.sum(sum(item[0:2, :] for item in tallies), axis=1, keepdims=True)
    energy[...] = sums[0:1, :] / sums[1:2, :]


def call(kernel, outs, scalars, arrays, scratch=(), name=None, raw=False, us=1.0):
    in_vmem = pl.BlockSpec(memory_space=pltpu.VMEM)
    in_smem = pl.BlockSpec(memory_space=pltpu.SMEM)
    in_hbm = pl.BlockSpec(memory_space=pltpu.HBM)
    shapes = [jax.ShapeDtypeStruct(*item) if isinstance(item[0], tuple) else jax.ShapeDtypeStruct(item, f32) for item in outs]
    return pl.pallas_call(
        kernel,
        out_shape=shapes,
        in_specs=[in_smem] * len(scalars) + [in_hbm if raw else in_vmem] * len(arrays),
        out_specs=[in_vmem] * len(outs),
        scratch_shapes=[pltpu.VMEM(item, f32) if isinstance(item, tuple) else item for item in scratch],
        compiler_params=pltpu.CompilerParams(vmem_limit_bytes=VMEM_BYTES),
        cost_estimate=pl.CostEstimate(flops=int(us * 1e9), bytes_accessed=int(us * 3e6), transcendentals=0),
        name=name,
    )(*scalars, *[pltpu.with_memory_space_constraint(item, pltpu.HBM) if raw else item for item in arrays])


def swap_core(value):
    size = lax.axis_size("yz")
    return lax.ppermute(value, "yz", [(i, i ^ 1) for i in range(size)])


def swap_chip(value):
    size = lax.axis_size("yz")
    return lax.ppermute(value, "yz", [(i, (i + 1 if i % 2 else i - 1) % size) for i in range(size)])


def shift(value, axis, by):
    size = lax.axis_size(axis)
    return lax.ppermute(value, axis, [(i, (i + by) % size) for i in range(size)])


def swap_gx(value):
    size = lax.axis_size("gx")
    if size == 2:
        return shift(value, "gx", 1)
    half = value.shape[1] // 2
    return jnp.concatenate(
        [shift(value[:, :half], "gx", 1), shift(value[:, half:], "gx", -1)], axis=1
    )


def return_gx(value):
    size = lax.axis_size("gx")
    if size == 2:
        return shift(value, "gx", 1)
    half = value.shape[1] // 2
    return jnp.concatenate(
        [shift(value[:, :half], "gx", -1), shift(value[:, half:], "gx", 1)], axis=1
    )


def partners(value, axis, bits):
    size = lax.axis_size(axis)
    steps = [0]
    for bit in bits:
        steps += [step ^ (1 << bit) for step in steps]
    return [lax.ppermute(value, axis, [(i, i ^ step) for i in range(size)]) for step in steps[1:]]


def together(values, other):
    *values, other = lax.optimization_barrier((*values, other))
    return values, other


def shards(
    old_pos,
    old_species,
    block_dest,
    block_count,
    send_list,
    neighbours,
    embed,
    atom_ref,
    w_up,
    gammas,
    w_rad,
    w_mix,
    readout,
):
    entries, slots = neighbours.shape
    blocks = block_dest.shape[0]
    width = old_species.shape[0] // blocks
    channels = w_up.shape[1]
    ghosts = send_list.size
    wide = slots + ghosts
    edges = entries * slots
    rows = w_rad.shape[2]
    species = old_species.reshape(blocks, width)
    i32 = jnp.int32

    (packed,) = call(
        pack_kernel,
        [(3 * ROWS, width)],
        [],
        [block_dest.T, block_count, old_pos, species],
        [
            pltpu.SMEM((1, blocks), i32),
            pltpu.SMEM((blocks,), i32),
            old_pos.shape,
            pltpu.VMEM(species.shape, i32),
            pltpu.SemaphoreType.DMA((4,)),
        ],
        name="pack",
        raw=True,
    )
    got_chip = swap_chip(packed)
    got_core = swap_core(packed)
    onehot, send, gamma, radials, species_up, species_in, weights, reads, onehot_t, send_t = call(
        prepare_kernel,
        [
            ((wide, edges), bf16),
            ((slots, ghosts), bf16),
            (2, ROWS, edges),
            ((2, rows, 3 * ROWS), bf16),
            ((channels, 3 * ROWS), bf16),
            ((channels, 3 * ROWS), bf16),
            ((6, channels, 3 * channels), bf16),
            (2, channels, slots),
            ((edges, wide), bf16),
            ((ghosts, slots), bf16),
        ],
        [],
        [gammas, neighbours, send_list, embed, w_up, w_rad, w_mix, readout],
        [
            pltpu.SMEM(gammas.shape, f32),
            pltpu.VMEM(neighbours.shape, i32),
            pltpu.VMEM(send_list.shape, i32),
            embed.shape,
            w_up.shape,
            w_rad.shape,
            w_mix.shape,
            readout.shape,
            (ROWS, channels),
            pltpu.SemaphoreType.DMA((8,)),
        ],
        name="prepare",
        raw=True,
        us=3.0,
    )
    small = (ROWS, LANES)
    tall = (CHIP_ROWS, LANES)
    table, pick_gx, pick_core, pick_chip = call(
        assemble_kernel,
        [(ROWS, slots), small, small, tall],
        [],
        [packed, got_core, got_chip, send],
        name="assemble",
        us=0.2,
    )
    got_chip = swap_chip(pick_chip)
    got_gx = swap_gx(pick_gx)
    got_core = swap_core(pick_core)
    flat = (channels, slots)
    square = (channels, LANES)
    half = (channels // 2, LANES)
    fields_shape = (9, channels, slots)
    h_one, slope, send_gx, send_core, send_chip, geo, angular, rad_one, feat_one, fields_one = call(
        first_layer_kernel,
        [flat, flat, square, half, half, (8, ROWS, edges), (8, ROWS, edges), (rows, edges), (channels, edges), fields_shape],
        [],
        [table, got_gx, got_core, got_chip, onehot, send, gamma, radials, species_up, species_in, weights],
        [flat],
        name="first_layer",
        us=2.5,
    )
    got_chip = swap_chip(send_chip)
    got_gx = swap_gx(send_gx)
    got_core = swap_core(send_core)
    factors, rad_two, slope_two, base = call(
        factor_kernel,
        [(4, channels, edges), (rows, edges), (rows, edges), (TALL, LANES)],
        [atom_ref],
        [geo, gamma, radials, table, rad_one, feat_one, fields_one],
        [(rows, edges)],
        name="factors",
        us=3.5,
    )
    feat_two, fields_two, g_two, g_own, tally = call(
        second_layer_kernel,
        [(channels, edges), fields_shape, flat, flat, (TALL, LANES)],
        [],
        [base, table, h_one, got_gx, got_core, got_chip, onehot, angular, rad_two, weights, reads],
        [flat],
        name="second_layer",
        us=2.5,
    )
    bits = (lax.axis_size("yz") - 1).bit_length()
    got_sums = partners(tally, "yz", [bits - 1] if bits > 1 else [])
    g_h, send_gx, send_core, send_chip, g_pos_two = call(
        second_gradient_kernel,
        [flat, square, half, half, (ROWS, wide)],
        [],
        [geo, rad_two, slope_two, feat_two, fields_two, g_two, g_own, onehot_t, weights],
        [(channels, edges), (ROWS, edges)],
        name="second_gradient",
        us=3.5,
    )
    got_sums, g_pos_two = together(got_sums, g_pos_two)
    tally = sum(got_sums, tally)
    got_chip = swap_chip(send_chip)
    got_gx = return_gx(send_gx)
    got_core = swap_core(send_core)
    tally = sum(partners(tally, "yz", [0]), tally)
    got_sums = partners(tally, "yz", [1] if bits > 2 else [])
    got_sums, got_chip = together(got_sums, got_chip)
    tally = sum(got_sums, tally)
    got_sums = partners(tally, "yz", range(2, bits - 1))
    g_pos, send_gx, send_core, send_chip = call(
        first_gradient_kernel,
        [(ROWS, slots), small, small, tall],
        [],
        [g_h, got_gx, got_core, got_chip, slope, factors, geo, g_pos_two, onehot_t, send_t, weights],
        [flat, (ROWS, edges)],
        name="first_gradient",
        us=1.2,
    )
    got_sums, g_pos = together(got_sums, g_pos)
    tally = sum(got_sums, tally)
    got_chip = swap_chip(send_chip)
    got_gx = return_gx(send_gx)
    got_core = swap_core(send_core)
    tally = tally[:ROWS]
    tallies = [tally] + partners(tally, "gx", range((lax.axis_size("gx") - 1).bit_length()))
    forces, energy = call(
        force_kernel,
        [(3, slots), (1, 1)],
        [],
        [g_pos, got_gx, got_core, got_chip, send_t] + tallies,
        name="forces",
    )
    return (forces, energy.reshape(()))


def solution(mesh):
    return jax.shard_map(
        shards,
        mesh=mesh,
        in_specs=(
            P(None, ("gx", "yz")),
            P(("gx", "yz")),
            P(("gx", "yz"), None),
            P(("gx", "yz")),
            P(("gx", "yz"), None),
            P(None, ("gx", "yz")),
            P(),
            P(),
            P(),
            P(),
            P(),
            P(),
            P(),
        ),
        out_specs=(P(None, ("gx", "yz")), P()),
        check_vma=False,
    )
```

```python
import functools
import math

import jax
import jax.numpy as jnp
from jax import lax
from jax.experimental import pallas as pl
from jax.experimental.pallas import tpu as pltpu
from jax.sharding import PartitionSpec as P

root_three = math.sqrt(3.0)
root_five = math.sqrt(5.0)
root_fifteen = math.sqrt(15.0)
f32 = jnp.float32
bf16 = jnp.bfloat16
ROWS = 8
LANES = 128
TALL = 64
CHIP_ROWS = 32
VMEM_BYTES = 16 * 1024 * 1024


def split2(value):
    high = value.astype(bf16)
    return high, (value - high.astype(f32)).astype(bf16)


def split3(value):
    high = value.astype(bf16)
    rest = value - high.astype(f32)
    mid = rest.astype(bf16)
    return high, mid, (rest - mid.astype(f32)).astype(bf16)


def dot(left, right, left_dim, right_dim):
    return lax.dot_general(
        left, right, (((left_dim,), (right_dim,)), ((), ())), preferred_element_type=f32
    )


def dot3(left, right, left_dim, right_dim):
    lh, ll = split2(left)
    rh, rl = split2(right)
    return (
        dot(lh, rh, left_dim, right_dim)
        + dot(lh, rl, left_dim, right_dim)
        + dot(ll, rh, left_dim, right_dim)
    )


def pieces(table):
    high = table.astype(bf16).astype(f32)
    rest = table - high
    mid = rest.astype(bf16).astype(f32)
    return jnp.concatenate([high, mid, rest - mid], axis=0).astype(bf16)


def pieces_f32(table):
    high = table.astype(bf16).astype(f32)
    rest = table - high
    mid = rest.astype(bf16).astype(f32)
    return jnp.concatenate([high, mid, rest - mid], axis=0)


def whole(stack):
    return stack[0:ROWS] + stack[ROWS : 2 * ROWS] + stack[2 * ROWS : 3 * ROWS]


def onehot_rows(count, row):
    places = lax.broadcasted_iota(jnp.int32, (count, row.shape[1]), 0)
    return jnp.where(places == row, 1.0, 0.0).astype(bf16)


def column(row):
    n = row.shape[1]
    down = lax.broadcasted_iota(jnp.int32, (n, n), 0)
    across = lax.broadcasted_iota(jnp.int32, (n, n), 1)
    return jnp.sum(jnp.where(down == across, jnp.broadcast_to(row, (n, n)), 0.0), axis=1, keepdims=True)


def left_half(shape):
    return lax.broadcasted_iota(jnp.int32, shape, 1) < shape[1] // 2


def is_even():
    return lax.rem(lax.axis_index("yz"), 2) == 0


def previous_and_next(core, chip):
    even = is_even()
    return jnp.where(even, chip, core), jnp.where(even, core, chip)


def faces_yz(core, chip):
    before, after = previous_and_next(core, chip)
    return jnp.where(left_half(core.shape), before, after)


def pack_halves(value):
    half = value.shape[0] // 2
    top, bottom = value[0:half], value[half:]
    left = left_half(top.shape)
    turned_top, turned_bottom = pltpu.roll(top, LANES // 2, 1), pltpu.roll(bottom, LANES // 2, 1)
    return jnp.where(left, top, turned_bottom), jnp.where(left, turned_top, bottom)


def join_halves(left_columns, right_columns):
    left = left_half(left_columns.shape)
    top = jnp.where(left, left_columns, pltpu.roll(right_columns, LANES // 2, 1))
    bottom = jnp.where(left, pltpu.roll(left_columns, LANES // 2, 1), right_columns)
    return jnp.concatenate([top, bottom], axis=0)


def stacked_left(weights):
    high, low = split2(weights)
    return jnp.concatenate([high, high, low], axis=1)


def stacked_right(value):
    high, low = split2(value)
    return jnp.concatenate([high, low, high], axis=0)


def stacked_rows(value):
    high = value.astype(bf16).astype(f32)
    return jnp.concatenate([high, high, value - high], axis=0).astype(bf16)


def stacked_rows_left(value):
    high = value.astype(bf16).astype(f32)
    low = value - high
    return jnp.concatenate([high, low, high], axis=0)


def species_onehot(code, count):
    places = lax.rem(lax.broadcasted_iota(jnp.int32, (3 * count, code.shape[1]), 0), count)
    return jnp.where(places == code.astype(jnp.int32), 1.0, 0.0).astype(bf16)


def matmul(left, right):
    return dot(left, right, 1, 0)


def repeat(row, times):
    return jnp.concatenate([row] * times, axis=1)


def tile(index):
    return pl.ds(pl.multiple_of(index * ROWS, ROWS), ROWS)


def degree_tiles(index, channels):
    return [pl.ds(pl.multiple_of(degree * channels + index * ROWS, ROWS), ROWS) for degree in range(3)]


def lane_parts(slots, entries):
    for part in range(slots // LANES):
        yield pl.ds(part * LANES, LANES), [pl.ds(k * slots + part * LANES, LANES) for k in range(entries)]


U, R, SCALE, SQUARE = 0, 3, 6, 7


def gather_sums(y_ref, rad_ref, feat_ref, fields_ref, invariant_ref):
    channels, slots = invariant_ref.shape
    entries = feat_ref.shape[1] // slots
    for lanes, edges in lane_parts(slots, entries):
        angular = [[y_ref[m, :, edges[k]] for m in range(8)] for k in range(entries)]

        def body(index, carry):
            rows = tile(index)
            degrees = degree_tiles(index, channels)
            sums = None
            for k in range(entries):
                feat = feat_ref[rows, edges[k]]
                weighted = [rad_ref[degree, edges[k]] * feat for degree in degrees]
                terms = [weighted[0]] + [angular[k][m] * weighted[1 if m < 3 else 2] for m in range(8)]
                sums = terms if k == 0 else [old + new for old, new in zip(sums, terms)]
            total = sums[0]
            for item in sums[1:]:
                total = total + item * item
            invariant_ref[rows, lanes] = total
            a1, a2, a3, a4, a5, a6, a7, a8 = sums[1:]
            c6, c8 = (2.0 * root_five) * a6, (2.0 * root_fifteen) * a8
            fields = [(2.0 * root_three) * a for a in (a1, a2, a3)]
            fields += [(2.0 * root_fifteen) * a for a in (a4, a5, a7)]
            fields += [c8 - c6, c8 + c6, c6 + c6]
            for number, field in enumerate(fields):
                fields_ref[number, rows, lanes] = field
            return carry

        lax.fori_loop(0, channels // ROWS, body, 0, unroll=2)


def direction_terms(fields, unit):
    b1, b2, b3, c4, c5, c7, minus, plus, twice = fields
    ux, uy, uz = unit
    h_x = uy * c4 + uz * c7 + ux * minus
    h_y = ux * c4 + uz * c5 - uy * plus
    h_z = uy * c5 + ux * c7 + uz * twice
    one = ux * b1 + uy * b2 + uz * b3
    two = 0.5 * (ux * h_x + uy * h_y + uz * h_z)
    return h_x, h_y, h_z, one, two


def offset_gradients(found, geo_ref, edges):
    g_s, g_x, g_y, g_z = [jnp.sum(item, axis=0, keepdims=True) for item in found]
    rx, ry, rz = [geo_ref[R + d, 0:1, edges] for d in range(3)]
    scale = geo_ref[SCALE, 0:1, edges]
    along = g_x * rx + g_y * ry + g_z * rz
    radial_part = 2.0 * g_s - scale * scale * scale * along
    return scale * g_x + rx * radial_part, scale * g_y + ry * radial_part, scale * g_z + rz * radial_part


def silu_and_slope(mixed):
    sigma = 1.0 / (1.0 + jnp.exp(-mixed))
    return mixed * sigma, sigma * (1.0 + mixed * (1.0 - sigma))


def fetch(pairs, sems):
    copies = [pltpu.make_async_copy(source, target, sems.at[i]) for i, (source, target) in enumerate(pairs)]
    for copy in copies:
        copy.start()
    return copies


def pack_kernel(dest_hbm, count_hbm, pos_hbm, species_hbm, out, dest, count, pos, species, sems):
    copies = fetch(((dest_hbm, dest), (count_hbm, count), (pos_hbm, pos), (species_hbm, species)), sems)
    blocks, width = species.shape
    place = lax.broadcasted_iota(jnp.int32, (1, width), 1)
    out[...] = jnp.zeros(out.shape, f32)
    for copy in copies:
        copy.wait()
    for group in range(3):
        coords = jnp.zeros((3, width), f32)
        code = jnp.full((1, width), -1.0, f32)
        for b in range(blocks):
            hit = dest[0, b] == group
            coords = jnp.where(hit, pos[:, b * width : (b + 1) * width], coords)
            alive = jnp.where(place < count[b], species[b : b + 1, :].astype(f32), -1.0)
            code = jnp.where(hit, alive, code)
        out[group * ROWS : group * ROWS + 3, :] = coords
        out[group * ROWS + 3 : group * ROWS + 4, :] = code


def prepare_kernel(
    gammas_hbm, nbr_hbm, lists_hbm, embed_hbm, w_up_hbm, w_rad_hbm, w_mix_hbm, readout_hbm,
    onehot, send, gamma, radials, species_up, species_in, weights, reads, onehot_t, send_t,
    gammas, nbr, lists, embed, w_up, w_rad, w_mix, readout, padded, sems,
):
    copies = fetch(
        (
            (nbr_hbm, nbr),
            (lists_hbm, lists),
            (gammas_hbm, gammas),
            (w_rad_hbm, w_rad),
            (embed_hbm, embed),
            (w_up_hbm, w_up),
            (w_mix_hbm, w_mix),
            (readout_hbm, readout),
        ),
        sems,
    )
    entries, slots = nbr.shape
    for copy in copies:
        copy.wait()
    wide = onehot.shape[0]
    for k in range(entries):
        onehot[:, k * slots : (k + 1) * slots] = onehot_rows(wide, nbr[k : k + 1, :])
    faces, ghosts = lists.shape
    for face in range(faces):
        send[:, face * ghosts : (face + 1) * ghosts] = onehot_rows(slots, lists[face : face + 1, :])
    count = w_rad.shape[1]
    which = lax.broadcasted_iota(jnp.int32, gamma.shape[1:], 0)
    for layer in range(2):
        value = jnp.zeros(which.shape, f32)
        for q in range(count):
            value = jnp.where(which == q, gammas[layer, q], value)
        gamma[layer] = value
        radials[layer] = stacked_rows_left(w_rad[layer] * (1.0 / entries)).T.astype(bf16)
    padded[...] = jnp.zeros(padded.shape, f32)
    padded[0 : embed.shape[0], :] = embed[...]
    species = padded[...]
    species_up[...] = pieces_f32(dot3(species, w_up[0], 1, 0)).T.astype(bf16)
    species_in[...] = pieces_f32(species).T.astype(bf16)
    for number, item in enumerate(
        (w_mix[0].T, w_up[1].T, w_mix[1].T, w_mix[1], w_up[1], w_mix[0])
    ):
        weights[number] = stacked_left(item)
    for layer in range(2):
        reads[layer] = jnp.broadcast_to(column(readout[layer : layer + 1, :]), reads.shape[1:])
    index_rows = jnp.concatenate([nbr[...].astype(f32), jnp.zeros((ROWS - entries, slots), f32)], axis=0)
    index_columns = index_rows.T
    across = lax.broadcasted_iota(jnp.int32, (slots, wide), 1).astype(f32)
    for k in range(entries):
        onehot_t[k * slots : (k + 1) * slots, :] = jnp.where(
            across == index_columns[:, k : k + 1], 1.0, 0.0
        ).astype(bf16)
    list_rows = jnp.concatenate([lists[...].astype(f32), jnp.zeros((ROWS - faces, ghosts), f32)], axis=0)
    list_columns = list_rows.T
    across = lax.broadcasted_iota(jnp.int32, (ghosts, slots), 1).astype(f32)
    for face in range(faces):
        send_t[face * ghosts : (face + 1) * ghosts, :] = jnp.where(
            across == list_columns[:, face : face + 1], 1.0, 0.0
        ).astype(bf16)


def assemble_kernel(own, core, chip, send, table, pick_gx, pick_core, pick_chip):
    before, after = previous_and_next(core[...], chip[...])
    blocks = [after[0:ROWS], own[ROWS : 2 * ROWS, :], before[2 * ROWS : 3 * ROWS]]
    slots = jnp.concatenate(blocks, axis=1)
    table[...] = slots
    picked = whole(matmul(pieces(slots), send[...]))
    pick_gx[...] = picked[:, 0:LANES]
    pick_core[...] = picked[:, LANES : 2 * LANES]
    pick_chip[...] = jnp.zeros(pick_chip.shape, f32)
    pick_chip[0:ROWS, :] = picked[:, LANES : 2 * LANES]


def first_layer_kernel(
    table, got_gx, got_core, got_chip, onehot, send, gamma, radials, species_up, species_in, weights,
    h_out, slope_out, send_gx, send_core, send_chip, geo, y_ref, rad_ref, feat_ref, fields_ref,
    inv_ref,
):
    slots = table.shape[1]
    edges = onehot.shape[1]
    entries = edges // slots
    ext = jnp.concatenate([table[...], got_gx[...], faces_yz(got_core[...], got_chip[0:ROWS, :])], axis=1)
    found = whole(matmul(pieces(ext), onehot[...]))
    feat_ref[...] = matmul(species_up[...], species_onehot(found[3:4], ROWS))
    spread = lambda row: jnp.broadcast_to(row, (ROWS, edges))
    rx, ry, rz = [
        spread(found[d : d + 1] - repeat(ext[d : d + 1, 0:slots], entries)) for d in range(3)
    ]
    square = rx * rx + ry * ry + rz * rz
    basis = jnp.exp(-gamma[0] * square)
    rad_ref[...] = matmul(radials[0], stacked_rows(basis))
    scale = lax.rsqrt(1.0 + square)
    ux, uy, uz = rx * scale, ry * scale, rz * scale
    for number, item in enumerate((ux, uy, uz, rx, ry, rz, scale, square)):
        geo[number] = item
    unit_square = ux * ux + uy * uy + uz * uz
    y_ref[0] = root_three * ux
    y_ref[1] = root_three * uy
    y_ref[2] = root_three * uz
    y_ref[3] = root_fifteen * ux * uy
    y_ref[4] = root_fifteen * uy * uz
    y_ref[5] = 0.5 * root_five * (3.0 * uz * uz - unit_square)
    y_ref[6] = root_fifteen * ux * uz
    y_ref[7] = 0.5 * root_fifteen * (ux * ux - uy * uy)
    gather_sums(y_ref, rad_ref, feat_ref, fields_ref, inv_ref)
    mixed = matmul(weights[0], stacked_right(inv_ref[...]))
    code = ext[3:4, 0:slots]
    live = jnp.where(code >= 0.0, 1.0, 0.0)
    h_zero = matmul(species_in[...], species_onehot(code, ROWS))
    value, slope = silu_and_slope(mixed)
    h_one = live * (h_zero + value)
    h_out[...] = h_one
    slope_out[...] = live * slope
    channels = h_one.shape[0]
    picked = matmul(jnp.concatenate(split2(h_one), axis=0), send[...])
    picked = picked[0:channels] + picked[channels : 2 * channels]
    send_gx[...] = picked[:, 0:LANES]
    to_next, to_previous = pack_halves(picked[:, LANES : 2 * LANES])
    even = is_even()
    send_core[...] = jnp.where(even, to_next, to_previous)
    send_chip[...] = jnp.where(even, to_previous, to_next)


def radial_kernel(
    atom_ref, geo, gamma, radials, table, h_one, onehot, weights,
    rad_two, slope_one, slope_two, base, found_two,
):
    square = geo[SQUARE]
    basis = jnp.exp(-gamma[1] * square)
    rad_two[...] = matmul(radials[1], stacked_rows(basis))
    slope_two[...] = matmul(radials[1], stacked_rows(-gamma[1] * basis))
    slope_one[...] = matmul(radials[0], stacked_rows(-gamma[0] * jnp.exp(-gamma[0] * square)))
    code = table[3:4, :]
    live = jnp.where(code >= 0.0, 1.0, 0.0)
    energy = jnp.zeros(code.shape, f32)
    for kind in range(atom_ref.shape[0]):
        energy = energy + jnp.where(code == float(kind), atom_ref[kind], 0.0)
    fold = lambda row: sum(row[:, c : c + LANES] for c in range(0, code.shape[1], LANES))
    base[...] = jnp.zeros(base.shape, f32)
    base[0:1, :] = fold(energy)
    base[1:2, :] = fold(live)
    channels, slots = h_one.shape
    projected = matmul(weights[1], stacked_right(h_one[...]))
    both = matmul(jnp.concatenate(split2(projected), axis=0), onehot[0:slots, :])
    found_two[...] = both[0:channels] + both[channels : 2 * channels]


def factor_kernel(
    geo, rad_ref, slope_ref, feat_ref, fields_ref, left, onehot_t, weights, g_own,
    factors, g_h, g_pos,
):
    channels, slots = fields_ref.shape[1:]
    entries = feat_ref.shape[1] // slots
    scattered = matmul(left[...], onehot_t[:, 0:slots])
    g_proj = scattered[0:channels] + scattered[channels : 2 * channels]
    g_pos[...] = whole(scattered[2 * channels : 2 * channels + 3 * ROWS])
    g_h[...] = matmul(weights[4], stacked_right(g_proj)) + g_own[...]
    for lanes, edges in lane_parts(slots, entries):
        units = [[geo[U + d, :, edges[k]] for d in range(3)] for k in range(entries)]

        def body(index, carry):
            rows = tile(index)
            degrees = degree_tiles(index, channels)
            fields = [fields_ref[m, rows, lanes] for m in range(9)]
            for k in range(entries):
                h_x, h_y, h_z, one, two = direction_terms(fields, units[k])
                feat = feat_ref[rows, edges[k]]
                r1, r2 = [rad_ref[d, edges[k]] * feat for d in degrees[1:]]
                d0, d1, d2 = [slope_ref[d, edges[k]] for d in degrees]
                factors[0, rows, edges[k]] = feat * (d0 + d1 * one + d2 * two)
                factors[1, rows, edges[k]] = r1 * fields[0] + r2 * h_x
                factors[2, rows, edges[k]] = r1 * fields[1] + r2 * h_y
                factors[3, rows, edges[k]] = r1 * fields[2] + r2 * h_z
            return carry

        lax.fori_loop(0, channels // ROWS, body, 0)


def second_layer_kernel(
    base, table, h_one, got_gx, got_core, got_chip, onehot, y_ref, rad_ref, weights, reads, found_two,
    feat_ref, fields_ref, g_ref, g_own, tally,
    inv_ref,
):
    h_local = h_one[...]
    channels, slots = h_local.shape
    before, after = previous_and_next(got_core[...], got_chip[...])
    ghosts = jnp.concatenate([got_gx[...], join_halves(before, after)], axis=1)
    projected = matmul(weights[1], stacked_right(ghosts))
    both = matmul(jnp.concatenate(split2(projected), axis=0), onehot[slots:, :])
    feat_ref[...] = found_two[...] + (both[0:channels] + both[channels : 2 * channels])
    gather_sums(y_ref, rad_ref, feat_ref, fields_ref, inv_ref)
    mixed = matmul(weights[2], stacked_right(inv_ref[...]))
    live = jnp.where(table[3:4, :] >= 0.0, 1.0, 0.0)
    value, slope = silu_and_slope(mixed)
    h_two = live * (h_local + value)
    energy = jnp.sum(reads[0] * h_local + reads[1] * h_two, axis=0, keepdims=True)
    tally[...] = base[...]
    tally[0:1, :] += sum(energy[:, c : c + LANES] for c in range(0, slots, LANES))
    g_ref[...] = matmul(weights[3], stacked_right((live * reads[1]) * slope))
    g_own[...] = live * (reads[0] + reads[1])


def second_gradient_kernel(
    geo, rad_ref, slope_ref, feat_ref, fields_ref, g_ref,
    g_feat, g_off,
):
    channels, slots = g_ref.shape
    entries = feat_ref.shape[1] // slots
    g_off[...] = jnp.zeros(g_off.shape, f32)
    for lanes, edges in lane_parts(slots, entries):
        units = [[geo[U + d, :, edges[k]] for d in range(3)] for k in range(entries)]

        def body(index, carry):
            rows = tile(index)
            degrees = degree_tiles(index, channels)
            g = g_ref[rows, lanes]
            fields = [g * fields_ref[m, rows, lanes] for m in range(9)]
            found = []
            for k in range(entries):
                h_x, h_y, h_z, one, two = direction_terms(fields, units[k])
                feat = feat_ref[rows, edges[k]]
                r0, r1, r2 = [rad_ref[d, edges[k]] for d in degrees]
                d0, d1, d2 = [slope_ref[d, edges[k]] for d in degrees]
                g_feat[rows, edges[k]] = g * r0 + r1 * one + r2 * two
                q1, q2 = feat * r1, feat * r2
                found += [
                    carry[4 * k] + feat * (g * d0 + d1 * one + d2 * two),
                    carry[4 * k + 1] + (q1 * fields[0] + q2 * h_x),
                    carry[4 * k + 2] + (q1 * fields[1] + q2 * h_y),
                    carry[4 * k + 3] + (q1 * fields[2] + q2 * h_z),
                ]
            return tuple(found)

        zero = jnp.zeros((ROWS, LANES), f32)
        found = lax.fori_loop(0, channels // ROWS, body, (zero,) * (4 * entries))
        for k in range(entries):
            for d, item in enumerate(offset_gradients(found[4 * k : 4 * k + 4], geo, edges[k])):
                g_off[d : d + 1, edges[k]] = item


def ghost_gradient_kernel(g_feat, g_off, onehot_t, weights, left, send_gx, send_core, send_chip, g_ghost, g_target):
    channels, edge_count = g_feat.shape
    wide = onehot_t.shape[1]
    slots = g_target.shape[1]
    entries = edge_count // slots
    stacked = jnp.concatenate([*split2(g_feat[...]), pieces(g_off[...])], axis=0)
    left[...] = stacked
    scattered = matmul(stacked, onehot_t[:, slots:wide])
    g_proj = scattered[0:channels] + scattered[channels : 2 * channels]
    g_ghost[...] = whole(scattered[2 * channels : 2 * channels + 3 * ROWS])
    g_all = matmul(weights[4], stacked_right(g_proj))
    send_gx[...] = g_all[:, 0:LANES]
    to_previous, to_next = pack_halves(g_all[:, LANES : 2 * LANES])
    even = is_even()
    send_core[...] = jnp.where(even, to_next, to_previous)
    send_chip[...] = jnp.where(even, to_previous, to_next)
    g_target[...] = sum(g_off[:, k * slots : (k + 1) * slots] for k in range(entries))


def first_gradient_kernel(
    g_h, got_gx, got_core, got_chip, slope, factors, geo, g_ghost, onehot_t, send_t, weights,
    left, g_target, send_gx, send_core, send_chip,
    g_ref, g_off,
):
    channels, slots = slope.shape
    entries = geo.shape[2] // slots
    before, after = previous_and_next(got_core[...], got_chip[...])
    back = jnp.concatenate([got_gx[...], join_halves(after, before)], axis=1)
    returned = matmul(jnp.concatenate(split2(back), axis=0), send_t[...])
    g_total = g_h[...] + (returned[0:channels] + returned[channels : 2 * channels])
    g_ref[...] = matmul(weights[5], stacked_right(g_total * slope[...]))
    g_off[...] = jnp.zeros(g_off.shape, f32)
    for lanes, edges in lane_parts(slots, entries):

        def body(index, carry):
            rows = tile(index)
            g = g_ref[rows, lanes]
            return tuple(
                carry[4 * k + m] + g * factors[m, rows, edges[k]] for k in range(entries) for m in range(4)
            )

        zero = jnp.zeros((ROWS, LANES), f32)
        found = lax.fori_loop(0, channels // ROWS, body, (zero,) * (4 * entries), unroll=4)
        for k in range(entries):
            for d, item in enumerate(offset_gradients(found[4 * k : 4 * k + 4], geo, edges[k])):
                g_off[d : d + 1, edges[k]] = item
    wide = onehot_t.shape[1]
    stacked = pieces(g_off[...])
    left[...] = stacked
    g_ext = whole(matmul(stacked, onehot_t[:, slots:wide])) + g_ghost[...]
    for out, piece in ((send_gx, 0), (send_core, 1), (send_chip, 1)):
        out[...] = jnp.zeros(out.shape, f32)
        out[0:ROWS, :] = g_ext[:, piece * LANES : (piece + 1) * LANES]
    g_target[...] = sum(g_off[:, k * slots : (k + 1) * slots] for k in range(entries))


def local_kernel(left, onehot_t, g_local_two, g_target_two, g_target_one, g_pos):
    slots = g_pos.shape[1]
    g_pos[...] = whole(matmul(left[...], onehot_t[:, 0:slots])) + g_local_two[...] - g_target_two[...] - g_target_one[...]


def chip_force_kernel(g_pos, got_chip, send_t, g_sum):
    half = left_half((ROWS, LANES))
    wanted = jnp.where(is_even(), 1.0, 0.0)
    kept = got_chip[0:ROWS, :] * jnp.where(half, 1.0 - wanted, wanted)
    ghosts = send_t.shape[0]
    g_sum[...] = g_pos[...] + whole(matmul(pieces(kept), send_t[ghosts - LANES : ghosts, :]))


def force_kernel(g_sum, got_gx, got_core, send_t, *rest):
    tallies, (forces, energy) = rest[:-2], rest[-2:]
    half = left_half((ROWS, LANES))
    wanted = jnp.where(is_even(), 0.0, 1.0)
    kept = got_core[0:ROWS, :] * jnp.where(half, 1.0 - wanted, wanted)
    back = jnp.concatenate([got_gx[0:ROWS, :], kept], axis=1)
    forces[...] = -(g_sum[...] + whole(matmul(pieces(back), send_t[...])))[0:3]
    sums = jnp.sum(sum(item[0:2, :] for item in tallies), axis=1, keepdims=True)
    energy[...] = sums[0:1, :] / sums[1:2, :]


def call(kernel, outs, scalars, arrays, scratch=(), name=None, raw=False, us=1.0):
    in_vmem = pl.BlockSpec(memory_space=pltpu.VMEM)
    in_smem = pl.BlockSpec(memory_space=pltpu.SMEM)
    in_hbm = pl.BlockSpec(memory_space=pltpu.HBM)
    shapes = [jax.ShapeDtypeStruct(*item) if isinstance(item[0], tuple) else jax.ShapeDtypeStruct(item, f32) for item in outs]
    return pl.pallas_call(
        kernel,
        out_shape=shapes,
        in_specs=[in_smem] * len(scalars) + [in_hbm if raw else in_vmem] * len(arrays),
        out_specs=[in_vmem] * len(outs),
        scratch_shapes=[pltpu.VMEM(item, f32) if isinstance(item, tuple) else item for item in scratch],
        compiler_params=pltpu.CompilerParams(vmem_limit_bytes=VMEM_BYTES),
        cost_estimate=pl.CostEstimate(flops=int(us * 1e9), bytes_accessed=int(us * 3e6), transcendentals=0),
        name=name,
    )(*scalars, *[pltpu.with_memory_space_constraint(item, pltpu.HBM) if raw else item for item in arrays])


def swap_core(value):
    size = lax.axis_size("yz")
    return lax.ppermute(value, "yz", [(i, i ^ 1) for i in range(size)])


def swap_chip(value):
    size = lax.axis_size("yz")
    return lax.ppermute(value, "yz", [(i, (i + 1 if i % 2 else i - 1) % size) for i in range(size)])


def shift(value, axis, by):
    size = lax.axis_size(axis)
    return lax.ppermute(value, axis, [(i, (i + by) % size) for i in range(size)])


def swap_gx(value):
    size = lax.axis_size("gx")
    if size == 2:
        return shift(value, "gx", 1)
    half = value.shape[1] // 2
    return jnp.concatenate(
        [shift(value[:, :half], "gx", 1), shift(value[:, half:], "gx", -1)], axis=1
    )


def return_gx(value):
    size = lax.axis_size("gx")
    if size == 2:
        return shift(value, "gx", 1)
    half = value.shape[1] // 2
    return jnp.concatenate(
        [shift(value[:, :half], "gx", -1), shift(value[:, half:], "gx", 1)], axis=1
    )


def partners(value, axis, bits):
    size = lax.axis_size(axis)
    steps = [0]
    for bit in bits:
        steps += [step ^ (1 << bit) for step in steps]
    return [lax.ppermute(value, axis, [(i, i ^ step) for i in range(size)]) for step in steps[1:]]


def together(values, other):
    *values, other = lax.optimization_barrier((*values, other))
    return values, other


def shards(
    old_pos,
    old_species,
    block_dest,
    block_count,
    send_list,
    neighbours,
    embed,
    atom_ref,
    w_up,
    gammas,
    w_rad,
    w_mix,
    readout,
):
    entries, slots = neighbours.shape
    blocks = block_dest.shape[0]
    width = old_species.shape[0] // blocks
    channels = w_up.shape[1]
    ghosts = send_list.size
    wide = slots + ghosts
    edges = entries * slots
    rows = w_rad.shape[2]
    species = old_species.reshape(blocks, width)
    i32 = jnp.int32

    (packed,) = call(
        pack_kernel,
        [(3 * ROWS, width)],
        [],
        [block_dest.T, block_count, old_pos, species],
        [
            pltpu.SMEM((1, blocks), i32),
            pltpu.SMEM((blocks,), i32),
            old_pos.shape,
            pltpu.VMEM(species.shape, i32),
            pltpu.SemaphoreType.DMA((4,)),
        ],
        name="pack",
        raw=True,
    )
    got_chip = swap_chip(packed)
    got_core = swap_core(packed)
    onehot, send, gamma, radials, species_up, species_in, weights, reads, onehot_t, send_t = call(
        prepare_kernel,
        [
            ((wide, edges), bf16),
            ((slots, ghosts), bf16),
            (2, ROWS, edges),
            ((2, rows, 3 * ROWS), bf16),
            ((channels, 3 * ROWS), bf16),
            ((channels, 3 * ROWS), bf16),
            ((6, channels, 3 * channels), bf16),
            (2, channels, slots),
            ((edges, wide), bf16),
            ((ghosts, slots), bf16),
        ],
        [],
        [gammas, neighbours, send_list, embed, w_up, w_rad, w_mix, readout],
        [
            pltpu.SMEM(gammas.shape, f32),
            pltpu.VMEM(neighbours.shape, i32),
            pltpu.VMEM(send_list.shape, i32),
            embed.shape,
            w_up.shape,
            w_rad.shape,
            w_mix.shape,
            readout.shape,
            (ROWS, channels),
            pltpu.SemaphoreType.DMA((8,)),
        ],
        name="prepare",
        raw=True,
        us=3.0,
    )
    small = (ROWS, LANES)
    tall = (CHIP_ROWS, LANES)
    table, pick_gx, pick_core, pick_chip = call(
        assemble_kernel,
        [(ROWS, slots), small, small, tall],
        [],
        [packed, got_core, got_chip, send],
        name="assemble",
        us=0.2,
    )
    got_chip = swap_chip(pick_chip)
    got_gx = swap_gx(pick_gx)
    got_core = swap_core(pick_core)
    flat = (channels, slots)
    square = (channels, LANES)
    half = (channels // 2, LANES)
    fields_shape = (9, channels, slots)
    h_one, slope, send_gx, send_core, send_chip, geo, angular, rad_one, feat_one, fields_one = call(
        first_layer_kernel,
        [flat, flat, square, half, half, (8, ROWS, edges), (8, ROWS, edges), (rows, edges), (channels, edges), fields_shape],
        [],
        [table, got_gx, got_core, got_chip, onehot, send, gamma, radials, species_up, species_in, weights],
        [flat],
        name="first_layer",
        us=2.5,
    )
    got_chip = swap_chip(send_chip)
    got_gx = swap_gx(send_gx)
    got_core = swap_core(send_core)
    rad_two, slope_one, slope_two, base, found_two = call(
        radial_kernel,
        [(rows, edges), (rows, edges), (rows, edges), (TALL, LANES), (channels, edges)],
        [atom_ref],
        [geo, gamma, radials, table, h_one, onehot, weights],
        name="radials",
        us=2.0,
    )
    feat_two, fields_two, g_two, g_own, tally = call(
        second_layer_kernel,
        [(channels, edges), fields_shape, flat, flat, (TALL, LANES)],
        [],
        [base, table, h_one, got_gx, got_core, got_chip, onehot, angular, rad_two, weights, reads, found_two],
        [flat],
        name="second_layer",
        us=2.5,
    )
    bits = (lax.axis_size("yz") - 1).bit_length()
    got_sums = partners(tally, "yz", [0])
    g_feat, g_off = call(
        second_gradient_kernel,
        [(channels, edges), (ROWS, edges)],
        [],
        [geo, rad_two, slope_two, feat_two, fields_two, g_two],
        name="second_gradient",
        us=2.5,
    )
    got_sums, g_off = together(got_sums, g_off)
    tally = sum(got_sums, tally)
    got_sums = partners(tally, "yz", [bits - 1] if bits > 1 else [])
    left, send_gx, send_core, send_chip, g_ghost, g_target_two = call(
        ghost_gradient_kernel,
        [((2 * channels + 3 * ROWS, edges), bf16), square, half, half, (ROWS, ghosts), (ROWS, slots)],
        [],
        [g_feat, g_off, onehot_t, weights],
        name="ghost_gradient",
        us=1.5,
    )
    got_sums, g_ghost = together(got_sums, g_ghost)
    tally = sum(got_sums, tally)
    got_chip = swap_chip(send_chip)
    got_gx = return_gx(send_gx)
    got_core = swap_core(send_core)
    tally = tally[:ROWS]
    got_sums = partners(tally, "yz", [1] if bits > 2 else [])
    factors, g_h, g_local_two = call(
        factor_kernel,
        [(4, channels, edges), flat, (ROWS, slots)],
        [],
        [geo, rad_one, slope_one, feat_one, fields_one, left, onehot_t, weights, g_own],
        name="factors",
        us=3.0,
    )
    got_sums, got_chip = together(got_sums, got_chip)
    tally = sum(got_sums, tally)
    tally = jnp.pad(tally, ((0, TALL - ROWS), (0, 0)))
    got_sums = partners(tally, "yz", range(2, bits - 1))
    left, g_target_one, send_gx, send_core, send_chip = call(
        first_gradient_kernel,
        [((3 * ROWS, edges), bf16), (ROWS, slots), (8, LANES), (8, LANES), (8, LANES)],
        [],
        [g_h, got_gx, got_core, got_chip, slope, factors, geo, g_ghost, onehot_t, send_t, weights],
        [flat, (ROWS, edges)],
        name="first_gradient",
        us=1.2,
    )
    got_sums, left = together(got_sums, left)
    tally = sum(got_sums, tally)
    got_chip = swap_chip(send_chip)
    got_gx = return_gx(send_gx)
    got_core = swap_core(send_core)
    (g_pos,) = call(
        local_kernel,
        [(ROWS, slots)],
        [],
        [left, onehot_t, g_local_two, g_target_two, g_target_one],
        name="local",
        us=0.5,
    )
    tally = tally[:ROWS]
    tallies = [tally] + partners(tally, "gx", range((lax.axis_size("gx") - 1).bit_length()))
    (g_sum,) = call(
        chip_force_kernel, [(ROWS, slots)], [], [g_pos, got_chip, send_t], name="chip_forces", us=0.1
    )
    forces, energy = call(
        force_kernel,
        [(3, slots), (1, 1)],
        [],
        [g_sum, got_gx, got_core, send_t] + tallies,
        name="forces",
    )
    return (forces, energy.reshape(()))


def solution(mesh):
    return jax.shard_map(
        shards,
        mesh=mesh,
        in_specs=(
            P(None, ("gx", "yz")),
            P(("gx", "yz")),
            P(("gx", "yz"), None),
            P(("gx", "yz")),
            P(("gx", "yz"), None),
            P(None, ("gx", "yz")),
            P(),
            P(),
            P(),
            P(),
            P(),
            P(),
            P(),
        ),
        out_specs=(P(None, ("gx", "yz")), P()),
        check_vma=False,
    )
```

```python
import functools
import math

import jax
import jax.numpy as jnp
from jax import lax
from jax.experimental import pallas as pl
from jax.experimental.pallas import tpu as pltpu
from jax.sharding import PartitionSpec as P

root_three = math.sqrt(3.0)
root_five = math.sqrt(5.0)
root_fifteen = math.sqrt(15.0)
f32 = jnp.float32
bf16 = jnp.bfloat16
ROWS = 8
LANES = 128
TALL = 64
CHIP_ROWS = 16
SUMS_UNROLL = 16
EDGE_UNROLL = 16
FORCE_UNROLL = 16
VMEM_BYTES = 16 * 1024 * 1024


def split2(value):
    high = value.astype(bf16)
    return high, (value - high.astype(f32)).astype(bf16)


def split3(value):
    high = value.astype(bf16)
    rest = value - high.astype(f32)
    mid = rest.astype(bf16)
    return high, mid, (rest - mid.astype(f32)).astype(bf16)


def dot(left, right, left_dim, right_dim):
    return lax.dot_general(
        left, right, (((left_dim,), (right_dim,)), ((), ())), preferred_element_type=f32
    )


def dot3(left, right, left_dim, right_dim):
    lh, ll = split2(left)
    rh, rl = split2(right)
    return (
        dot(lh, rh, left_dim, right_dim)
        + dot(lh, rl, left_dim, right_dim)
        + dot(ll, rh, left_dim, right_dim)
    )


def pieces(table):
    high = table.astype(bf16).astype(f32)
    rest = table - high
    mid = rest.astype(bf16).astype(f32)
    return jnp.concatenate([high, mid, rest - mid], axis=0).astype(bf16)


def pieces_f32(table):
    high = table.astype(bf16).astype(f32)
    rest = table - high
    mid = rest.astype(bf16).astype(f32)
    return jnp.concatenate([high, mid, rest - mid], axis=0)


def whole(stack):
    return stack[0:ROWS] + stack[ROWS : 2 * ROWS] + stack[2 * ROWS : 3 * ROWS]


def onehot_rows(count, row):
    places = lax.broadcasted_iota(jnp.int32, (count, row.shape[1]), 0)
    return jnp.where(places == row, 1.0, 0.0).astype(bf16)


def column(row):
    n = row.shape[1]
    down = lax.broadcasted_iota(jnp.int32, (n, n), 0)
    across = lax.broadcasted_iota(jnp.int32, (n, n), 1)
    return jnp.sum(jnp.where(down == across, jnp.broadcast_to(row, (n, n)), 0.0), axis=1, keepdims=True)


def left_half(shape):
    return lax.broadcasted_iota(jnp.int32, shape, 1) < shape[1] // 2


def is_even():
    return lax.rem(lax.axis_index("yz"), 2) == 0


def previous_and_next(core, chip):
    even = is_even()
    return jnp.where(even, chip, core), jnp.where(even, core, chip)


def faces_yz(core, chip):
    before, after = previous_and_next(core, chip)
    return jnp.where(left_half(core.shape), before, after)


def pack_halves(value):
    half = value.shape[0] // 2
    top, bottom = value[0:half], value[half:]
    left = left_half(top.shape)
    turned_top, turned_bottom = pltpu.roll(top, LANES // 2, 1), pltpu.roll(bottom, LANES // 2, 1)
    return jnp.where(left, top, turned_bottom), jnp.where(left, turned_top, bottom)


def join_halves(left_columns, right_columns):
    left = left_half(left_columns.shape)
    top = jnp.where(left, left_columns, pltpu.roll(right_columns, LANES // 2, 1))
    bottom = jnp.where(left, pltpu.roll(left_columns, LANES // 2, 1), right_columns)
    return jnp.concatenate([top, bottom], axis=0)


def stacked_left(weights):
    high, low = split2(weights)
    return jnp.concatenate([high, high, low], axis=1)


def stacked_right(value):
    high, low = split2(value)
    return jnp.concatenate([high, low, high], axis=0)


def stacked_rows(value):
    high = value.astype(bf16).astype(f32)
    return jnp.concatenate([high, high, value - high], axis=0).astype(bf16)


def stacked_rows_left(value):
    high = value.astype(bf16).astype(f32)
    low = value - high
    return jnp.concatenate([high, low, high], axis=0)


def species_onehot(code, count):
    places = lax.rem(lax.broadcasted_iota(jnp.int32, (3 * count, code.shape[1]), 0), count)
    return jnp.where(places == code.astype(jnp.int32), 1.0, 0.0).astype(bf16)


def matmul(left, right):
    return dot(left, right, 1, 0)


def repeat(row, times):
    return jnp.concatenate([row] * times, axis=1)


def tile(index):
    return pl.ds(pl.multiple_of(index * ROWS, ROWS), ROWS)


def degree_tiles(index, channels):
    return [pl.ds(pl.multiple_of(degree * channels + index * ROWS, ROWS), ROWS) for degree in range(3)]


def lane_parts(slots, entries):
    for part in range(slots // LANES):
        yield pl.ds(part * LANES, LANES), [pl.ds(k * slots + part * LANES, LANES) for k in range(entries)]


U, R, SCALE, SQUARE = 0, 3, 6, 7


def gather_sums(geo, y_ref, rad_ref, feat_ref, fields_ref, invariant_ref):
    channels, slots = invariant_ref.shape
    entries = feat_ref.shape[1] // slots
    for lanes, edges in lane_parts(slots, entries):
        first = [[geo[U + d, :, edges[k]] for d in range(3)] for k in range(entries)]
        second = [[y_ref[m, :, edges[k]] for m in range(5)] for k in range(entries)]

        def body(index, carry):
            rows = tile(index)
            degrees = degree_tiles(index, channels)
            sums = None
            for k in range(entries):
                feat = feat_ref[rows, edges[k]]
                zero, one, two = [rad_ref[degree, edges[k]] * feat for degree in degrees]
                terms = [zero] + [item * one for item in first[k]] + [item * two for item in second[k]]
                sums = terms if k == 0 else [old + new for old, new in zip(sums, terms)]
            total = sums[0]
            for item in sums[1:]:
                total = total + item * item
            invariant_ref[rows, lanes] = total
            a1, a2, a3, a4, a5, a6, a7, a8 = sums[1:]
            c6 = (1.0 / root_three) * a6
            for number, field in enumerate((a1, a2, a3, a4, a5, a7, a8 - c6, a8 + c6, c6 + c6)):
                fields_ref[number, rows, lanes] = field
            return carry

        lax.fori_loop(0, channels // ROWS, body, 0, unroll=SUMS_UNROLL)


def direction_terms(fields, unit):
    a1, a2, a3, a4, a5, a7, minus, plus, twice = fields
    ux, uy, uz = unit
    h_x = uy * a4 + uz * a7 + ux * minus
    h_y = ux * a4 + uz * a5 - uy * plus
    h_z = uy * a5 + ux * a7 + uz * twice
    one = ux * a1 + uy * a2 + uz * a3
    two = 0.5 * (ux * h_x + uy * h_y + uz * h_z)
    return h_x, h_y, h_z, one, two


def offset_gradients(found, geo_ref, edges):
    g_s, g_x, g_y, g_z = [jnp.sum(item, axis=0, keepdims=True) for item in found]
    rx, ry, rz = [geo_ref[R + d, 0:1, edges] for d in range(3)]
    scale = geo_ref[SCALE, 0:1, edges]
    along = g_x * rx + g_y * ry + g_z * rz
    radial_part = 2.0 * g_s - scale * scale * scale * along
    return scale * g_x + rx * radial_part, scale * g_y + ry * radial_part, scale * g_z + rz * radial_part


def silu_and_slope(mixed):
    sigma = 1.0 / (1.0 + jnp.exp(-mixed))
    return mixed * sigma, sigma * (1.0 + mixed * (1.0 - sigma))


def fetch(pairs, sems):
    copies = [pltpu.make_async_copy(source, target, sems.at[i]) for i, (source, target) in enumerate(pairs)]
    for copy in copies:
        copy.start()
    return copies


def pack_kernel(dest_hbm, count_hbm, pos_hbm, species_hbm, out, dest, count, pos, species, sems):
    copies = fetch(((dest_hbm, dest), (count_hbm, count), (pos_hbm, pos), (species_hbm, species)), sems)
    blocks, width = species.shape
    place = lax.broadcasted_iota(jnp.int32, (1, width), 1)
    out[...] = jnp.zeros(out.shape, f32)
    for copy in copies:
        copy.wait()
    for group in range(3):
        coords = jnp.zeros((3, width), f32)
        code = jnp.full((1, width), -1.0, f32)
        for b in range(blocks):
            hit = dest[0, b] == group
            coords = jnp.where(hit, pos[:, b * width : (b + 1) * width], coords)
            alive = jnp.where(place < count[b], species[b : b + 1, :].astype(f32), -1.0)
            code = jnp.where(hit, alive, code)
        out[group * ROWS : group * ROWS + 3, :] = coords
        out[group * ROWS + 3 : group * ROWS + 4, :] = code


def prepare_kernel(
    gammas_hbm, nbr_hbm, lists_hbm, embed_hbm, w_up_hbm, w_rad_hbm, w_mix_hbm, readout_hbm,
    onehot, send, gamma, radials, species_up, species_in, weights, reads, onehot_t, send_t,
    gammas, nbr, lists, embed, w_up, w_rad, w_mix, readout, padded, sems,
):
    copies = fetch(
        (
            (nbr_hbm, nbr),
            (lists_hbm, lists),
            (gammas_hbm, gammas),
            (w_rad_hbm, w_rad),
            (embed_hbm, embed),
            (w_up_hbm, w_up),
            (w_mix_hbm, w_mix),
            (readout_hbm, readout),
        ),
        sems,
    )
    entries, slots = nbr.shape
    for copy in copies:
        copy.wait()
    wide = onehot.shape[0]
    for k in range(entries):
        onehot[:, k * slots : (k + 1) * slots] = onehot_rows(wide, nbr[k : k + 1, :])
    faces, ghosts = lists.shape
    for face in range(faces):
        send[:, face * ghosts : (face + 1) * ghosts] = onehot_rows(slots, lists[face : face + 1, :])
    count = w_rad.shape[1]
    which = lax.broadcasted_iota(jnp.int32, gamma.shape[1:], 0)
    channels = w_up.shape[1]
    place = lax.broadcasted_iota(jnp.int32, w_rad.shape[1:], 1)
    scales = jnp.where(place < channels, 1.0, jnp.where(place < 2 * channels, root_three, root_fifteen)) * (1.0 / entries)
    for layer in range(2):
        value = jnp.zeros(which.shape, f32)
        for q in range(count):
            value = jnp.where(which == q, gammas[layer, q], value)
        gamma[layer] = value
        radials[layer] = stacked_rows_left(w_rad[layer] * scales).T.astype(bf16)
    padded[...] = jnp.zeros(padded.shape, f32)
    padded[0 : embed.shape[0], :] = embed[...]
    species = padded[...]
    species_up[...] = pieces_f32(dot3(species, w_up[0], 1, 0)).T.astype(bf16)
    species_in[...] = pieces_f32(species).T.astype(bf16)
    for number, item in enumerate(
        (w_mix[0].T, w_up[1].T, w_mix[1].T, w_mix[1], w_up[1], w_mix[0])
    ):
        weights[number] = stacked_left(item)
    for layer in range(2):
        reads[layer] = jnp.broadcast_to(column(readout[layer : layer + 1, :]), reads.shape[1:])
    index_rows = jnp.concatenate([nbr[...].astype(f32), jnp.zeros((ROWS - entries, slots), f32)], axis=0)
    index_columns = index_rows.T
    across = lax.broadcasted_iota(jnp.int32, (slots, wide), 1).astype(f32)
    for k in range(entries):
        onehot_t[k * slots : (k + 1) * slots, :] = jnp.where(
            across == index_columns[:, k : k + 1], 1.0, 0.0
        ).astype(bf16)
    list_rows = jnp.concatenate([lists[...].astype(f32), jnp.zeros((ROWS - faces, ghosts), f32)], axis=0)
    list_columns = list_rows.T
    across = lax.broadcasted_iota(jnp.int32, (ghosts, slots), 1).astype(f32)
    for face in range(faces):
        send_t[face * ghosts : (face + 1) * ghosts, :] = jnp.where(
            across == list_columns[:, face : face + 1], 1.0, 0.0
        ).astype(bf16)


def assemble_kernel(own, core, chip, send, table, pick_gx, pick_core, pick_chip):
    before, after = previous_and_next(core[...], chip[...])
    blocks = [after[0:ROWS], own[ROWS : 2 * ROWS, :], before[2 * ROWS : 3 * ROWS]]
    slots = jnp.concatenate(blocks, axis=1)
    table[...] = slots
    picked = whole(matmul(pieces(slots), send[...]))
    pick_gx[...] = picked[:, 0:LANES]
    pick_core[...] = picked[:, LANES : 2 * LANES]
    pick_chip[...] = jnp.zeros(pick_chip.shape, f32)
    pick_chip[0:ROWS, :] = picked[:, LANES : 2 * LANES]


def own_positions_kernel(table, onehot, found):
    found[...] = whole(matmul(pieces(table[...]), onehot[0 : table.shape[1], :]))


def first_layer_kernel(
    found_own, table, got_gx, got_core, got_chip, onehot, send, gamma, radials, species_up, species_in, weights,
    h_out, slope_out, send_gx, send_core, send_chip, geo, y_ref, rad_ref, feat_ref, fields_ref,
    inv_ref,
):
    slots = table.shape[1]
    edges = onehot.shape[1]
    entries = edges // slots
    ghosts = jnp.concatenate([got_gx[...], faces_yz(got_core[...], got_chip[0:ROWS, :])], axis=1)
    found = found_own[...] + whole(matmul(pieces(ghosts), onehot[slots:, :]))
    feat_ref[...] = matmul(species_up[...], species_onehot(found[3:4], ROWS))
    spread = lambda row: jnp.broadcast_to(row, (ROWS, edges))
    rx, ry, rz = [
        spread(found[d : d + 1] - repeat(table[d : d + 1, :], entries)) for d in range(3)
    ]
    square = rx * rx + ry * ry + rz * rz
    basis = jnp.exp(-gamma[0] * square)
    rad_ref[...] = matmul(radials[0], stacked_rows(basis))
    scale = lax.rsqrt(1.0 + square)
    ux, uy, uz = rx * scale, ry * scale, rz * scale
    for number, item in enumerate((ux, uy, uz, rx, ry, rz, scale, square)):
        geo[number] = item
    xx, yy, zz = ux * ux, uy * uy, uz * uz
    for number, item in enumerate(
        (ux * uy, uy * uz, (0.5 / root_three) * (2.0 * zz - xx - yy), ux * uz, 0.5 * (xx - yy))
    ):
        y_ref[number] = item
    gather_sums(geo, y_ref, rad_ref, feat_ref, fields_ref, inv_ref)
    mixed = matmul(weights[0], stacked_right(inv_ref[...]))
    code = table[3:4, :]
    live = jnp.where(code >= 0.0, 1.0, 0.0)
    h_zero = matmul(species_in[...], species_onehot(code, ROWS))
    value, slope = silu_and_slope(mixed)
    h_one = live * (h_zero + value)
    h_out[...] = h_one
    slope_out[...] = live * slope
    channels = h_one.shape[0]
    picked = matmul(jnp.concatenate(split2(h_one), axis=0), send[...])
    picked = picked[0:channels] + picked[channels : 2 * channels]
    send_gx[...] = picked[:, 0:LANES]
    to_next, to_previous = pack_halves(picked[:, LANES : 2 * LANES])
    even = is_even()
    send_core[...] = jnp.where(even, to_next, to_previous)
    send_chip[...] = jnp.where(even, to_previous, to_next)


def radial_kernel(
    atom_ref, geo, gamma, radials, table, h_one, onehot, weights,
    rad_two, slope_one, slope_two, base, found_two,
):
    square = geo[SQUARE]
    basis = jnp.exp(-gamma[1] * square)
    rad_two[...] = matmul(radials[1], stacked_rows(basis))
    slope_two[...] = matmul(radials[1], stacked_rows(-gamma[1] * basis))
    slope_one[...] = matmul(radials[0], stacked_rows(-gamma[0] * jnp.exp(-gamma[0] * square)))
    code = table[3:4, :]
    live = jnp.where(code >= 0.0, 1.0, 0.0)
    energy = jnp.zeros(code.shape, f32)
    for kind in range(atom_ref.shape[0]):
        energy = energy + jnp.where(code == float(kind), atom_ref[kind], 0.0)
    fold = lambda row: sum(row[:, c : c + LANES] for c in range(0, code.shape[1], LANES))
    base[...] = jnp.zeros(base.shape, f32)
    base[0:1, :] = fold(energy)
    base[1:2, :] = fold(live)
    channels, slots = h_one.shape
    projected = matmul(weights[1], stacked_right(h_one[...]))
    both = matmul(jnp.concatenate(split2(projected), axis=0), onehot[0:slots, :])
    found_two[...] = both[0:channels] + both[channels : 2 * channels]


def factor_kernel(
    geo, rad_ref, slope_ref, feat_ref, fields_ref, left, onehot_t, weights, g_own,
    factors, g_h, g_pos,
):
    channels, slots = fields_ref.shape[1:]
    entries = feat_ref.shape[1] // slots
    scattered = matmul(left[...], onehot_t[:, 0:slots])
    g_proj = scattered[0:channels] + scattered[channels : 2 * channels]
    g_pos[...] = whole(scattered[2 * channels : 2 * channels + 3 * ROWS])
    g_h[...] = matmul(weights[4], stacked_right(g_proj)) + g_own[...]
    for lanes, edges in lane_parts(slots, entries):
        units = [[geo[U + d, :, edges[k]] for d in range(3)] for k in range(entries)]

        def body(index, carry):
            rows = tile(index)
            degrees = degree_tiles(index, channels)
            fields = [fields_ref[m, rows, lanes] for m in range(9)]
            for k in range(entries):
                h_x, h_y, h_z, one, two = direction_terms(fields, units[k])
                feat = feat_ref[rows, edges[k]]
                r1, r2 = [rad_ref[d, edges[k]] * feat for d in degrees[1:]]
                d0, d1, d2 = [slope_ref[d, edges[k]] for d in degrees]
                factors[0, rows, edges[k]] = feat * (0.5 * d0 + d1 * one + d2 * two)
                factors[1, rows, edges[k]] = r1 * fields[0] + r2 * h_x
                factors[2, rows, edges[k]] = r1 * fields[1] + r2 * h_y
                factors[3, rows, edges[k]] = r1 * fields[2] + r2 * h_z
            return carry

        lax.fori_loop(0, channels // ROWS, body, 0, unroll=2)


def second_layer_kernel(
    base, table, h_one, got_gx, got_core, got_chip, onehot, geo, y_ref, rad_ref, weights, reads, found_two,
    feat_ref, fields_ref, g_ref, g_own, tally,
    inv_ref,
):
    h_local = h_one[...]
    channels, slots = h_local.shape
    before, after = previous_and_next(got_core[...], got_chip[...])
    ghosts = jnp.concatenate([got_gx[...], join_halves(before, after)], axis=1)
    projected = matmul(weights[1], stacked_right(ghosts))
    both = matmul(jnp.concatenate(split2(projected), axis=0), onehot[slots:, :])
    feat_ref[...] = found_two[...] + (both[0:channels] + both[channels : 2 * channels])
    gather_sums(geo, y_ref, rad_ref, feat_ref, fields_ref, inv_ref)
    mixed = matmul(weights[2], stacked_right(inv_ref[...]))
    live = jnp.where(table[3:4, :] >= 0.0, 1.0, 0.0)
    value, slope = silu_and_slope(mixed)
    h_two = live * (h_local + value)
    energy = jnp.sum(reads[0] * h_local + reads[1] * h_two, axis=0, keepdims=True)
    tally[...] = base[...]
    tally[0:1, :] += sum(energy[:, c : c + LANES] for c in range(0, slots, LANES))
    g_ref[...] = matmul(weights[3], stacked_right((live * reads[1]) * slope))
    g_own[...] = live * (reads[0] + reads[1])


def second_gradient_kernel(
    geo, rad_ref, slope_ref, feat_ref, fields_ref, g_ref,
    g_feat, g_off,
):
    channels, slots = g_ref.shape
    entries = feat_ref.shape[1] // slots
    g_off[...] = jnp.zeros(g_off.shape, f32)
    for lanes, edges in lane_parts(slots, entries):
        units = [[geo[U + d, :, edges[k]] for d in range(3)] for k in range(entries)]

        def body(index, carry):
            rows = tile(index)
            degrees = degree_tiles(index, channels)
            g = g_ref[rows, lanes]
            fields = [(g + g) * fields_ref[m, rows, lanes] for m in range(9)]
            found = []
            for k in range(entries):
                h_x, h_y, h_z, one, two = direction_terms(fields, units[k])
                feat = feat_ref[rows, edges[k]]
                r0, r1, r2 = [rad_ref[d, edges[k]] for d in degrees]
                d0, d1, d2 = [slope_ref[d, edges[k]] for d in degrees]
                g_feat[rows, edges[k]] = g * r0 + r1 * one + r2 * two
                q1, q2 = feat * r1, feat * r2
                found += [
                    carry[4 * k] + feat * (g * d0 + d1 * one + d2 * two),
                    carry[4 * k + 1] + (q1 * fields[0] + q2 * h_x),
                    carry[4 * k + 2] + (q1 * fields[1] + q2 * h_y),
                    carry[4 * k + 3] + (q1 * fields[2] + q2 * h_z),
                ]
            return tuple(found)

        zero = jnp.zeros((ROWS, LANES), f32)
        found = lax.fori_loop(0, channels // ROWS, body, (zero,) * (4 * entries), unroll=EDGE_UNROLL)
        for k in range(entries):
            for d, item in enumerate(offset_gradients(found[4 * k : 4 * k + 4], geo, edges[k])):
                g_off[d : d + 1, edges[k]] = item


def ghost_gradient_kernel(g_feat, g_off, onehot_t, weights, left, send_gx, send_core, send_chip, g_ghost, g_target):
    channels, edge_count = g_feat.shape
    wide = onehot_t.shape[1]
    slots = g_target.shape[1]
    entries = edge_count // slots
    stacked = jnp.concatenate([*split2(g_feat[...]), pieces(g_off[...])], axis=0)
    left[...] = stacked
    scattered = matmul(stacked, onehot_t[:, slots:wide])
    g_proj = scattered[0:channels] + scattered[channels : 2 * channels]
    g_ghost[...] = whole(scattered[2 * channels : 2 * channels + 3 * ROWS])
    g_all = matmul(weights[4], stacked_right(g_proj))
    send_gx[...] = g_all[:, 0:LANES]
    to_previous, to_next = pack_halves(g_all[:, LANES : 2 * LANES])
    even = is_even()
    send_core[...] = jnp.where(even, to_next, to_previous)
    send_chip[...] = jnp.where(even, to_previous, to_next)
    g_target[...] = sum(g_off[:, k * slots : (k + 1) * slots] for k in range(entries))


def first_gradient_kernel(
    g_h, got_gx, got_core, got_chip, slope, factors, geo, g_ghost, onehot_t, send_t, weights,
    left, g_target, send_gx, send_core, send_chip,
    g_ref, g_off,
):
    channels, slots = slope.shape
    entries = geo.shape[2] // slots
    before, after = previous_and_next(got_core[...], got_chip[...])
    back = jnp.concatenate([got_gx[...], join_halves(after, before)], axis=1)
    returned = matmul(jnp.concatenate(split2(back), axis=0), send_t[...])
    g_total = g_h[...] + (returned[0:channels] + returned[channels : 2 * channels])
    g_ref[...] = matmul(weights[5], stacked_right(g_total * (2.0 * slope[...])))
    g_off[...] = jnp.zeros(g_off.shape, f32)
    for lanes, edges in lane_parts(slots, entries):

        def body(index, carry):
            rows = tile(index)
            g = g_ref[rows, lanes]
            return tuple(
                carry[4 * k + m] + g * factors[m, rows, edges[k]] for k in range(entries) for m in range(4)
            )

        zero = jnp.zeros((ROWS, LANES), f32)
        found = lax.fori_loop(0, channels // ROWS, body, (zero,) * (4 * entries), unroll=FORCE_UNROLL)
        for k in range(entries):
            for d, item in enumerate(offset_gradients(found[4 * k : 4 * k + 4], geo, edges[k])):
                g_off[d : d + 1, edges[k]] = item
    wide = onehot_t.shape[1]
    stacked = pieces(g_off[...])
    left[...] = stacked
    g_ext = whole(matmul(stacked, onehot_t[:, slots:wide])) + g_ghost[...]
    for out, piece in ((send_gx, 0), (send_core, 1), (send_chip, 1)):
        out[...] = jnp.zeros(out.shape, f32)
        out[0:ROWS, :] = g_ext[:, piece * LANES : (piece + 1) * LANES]
    g_target[...] = sum(g_off[:, k * slots : (k + 1) * slots] for k in range(entries))


def local_kernel(left, onehot_t, g_local_two, g_target_two, g_target_one, g_pos):
    slots = g_pos.shape[1]
    g_pos[...] = whole(matmul(left[...], onehot_t[:, 0:slots])) + g_local_two[...] - g_target_two[...] - g_target_one[...]


def chip_force_kernel(g_pos, got_chip, send_t, g_sum):
    half = left_half((ROWS, LANES))
    wanted = jnp.where(is_even(), 1.0, 0.0)
    kept = got_chip[0:ROWS, :] * jnp.where(half, 1.0 - wanted, wanted)
    ghosts = send_t.shape[0]
    g_sum[...] = g_pos[...] + whole(matmul(pieces(kept), send_t[ghosts - LANES : ghosts, :]))


def force_kernel(g_sum, got_gx, got_core, send_t, *rest):
    tallies, (forces, energy) = rest[:-2], rest[-2:]
    half = left_half((ROWS, LANES))
    wanted = jnp.where(is_even(), 0.0, 1.0)
    kept = got_core[0:ROWS, :] * jnp.where(half, 1.0 - wanted, wanted)
    back = jnp.concatenate([got_gx[0:ROWS, :], kept], axis=1)
    forces[...] = -(g_sum[...] + whole(matmul(pieces(back), send_t[...])))[0:3]
    sums = jnp.sum(sum(item[0:2, :] for item in tallies), axis=1, keepdims=True)
    energy[...] = sums[0:1, :] / sums[1:2, :]


def call(kernel, outs, scalars, arrays, scratch=(), name=None, raw=False, us=1.0):
    in_vmem = pl.BlockSpec(memory_space=pltpu.VMEM)
    in_smem = pl.BlockSpec(memory_space=pltpu.SMEM)
    in_hbm = pl.BlockSpec(memory_space=pltpu.HBM)
    shapes = [jax.ShapeDtypeStruct(*item) if isinstance(item[0], tuple) else jax.ShapeDtypeStruct(item, f32) for item in outs]
    return pl.pallas_call(
        kernel,
        out_shape=shapes,
        in_specs=[in_smem] * len(scalars) + [in_hbm if raw else in_vmem] * len(arrays),
        out_specs=[in_vmem] * len(outs),
        scratch_shapes=[pltpu.VMEM(item, f32) if isinstance(item, tuple) else item for item in scratch],
        compiler_params=pltpu.CompilerParams(vmem_limit_bytes=VMEM_BYTES),
        cost_estimate=pl.CostEstimate(flops=int(us * 1e9), bytes_accessed=int(us * 3e6), transcendentals=0),
        name=name,
    )(*scalars, *[pltpu.with_memory_space_constraint(item, pltpu.HBM) if raw else item for item in arrays])


def swap_core(value):
    size = lax.axis_size("yz")
    return lax.ppermute(value, "yz", [(i, i ^ 1) for i in range(size)])


def swap_chip(value):
    size = lax.axis_size("yz")
    return lax.ppermute(value, "yz", [(i, (i + 1 if i % 2 else i - 1) % size) for i in range(size)])


def shift(value, axis, by):
    size = lax.axis_size(axis)
    return lax.ppermute(value, axis, [(i, (i + by) % size) for i in range(size)])


def swap_gx(value):
    size = lax.axis_size("gx")
    if size == 2:
        return shift(value, "gx", 1)
    half = value.shape[1] // 2
    return jnp.concatenate(
        [shift(value[:, :half], "gx", 1), shift(value[:, half:], "gx", -1)], axis=1
    )


def return_gx(value):
    size = lax.axis_size("gx")
    if size == 2:
        return shift(value, "gx", 1)
    half = value.shape[1] // 2
    return jnp.concatenate(
        [shift(value[:, :half], "gx", -1), shift(value[:, half:], "gx", 1)], axis=1
    )


def partners(value, axis, bits):
    size = lax.axis_size(axis)
    steps = [0]
    for bit in bits:
        steps += [step ^ (1 << bit) for step in steps]
    return [lax.ppermute(value, axis, [(i, i ^ step) for i in range(size)]) for step in steps[1:]]


def together(values, other):
    *values, other = lax.optimization_barrier((*values, other))
    return values, other


def shards(
    old_pos,
    old_species,
    block_dest,
    block_count,
    send_list,
    neighbours,
    embed,
    atom_ref,
    w_up,
    gammas,
    w_rad,
    w_mix,
    readout,
):
    entries, slots = neighbours.shape
    blocks = block_dest.shape[0]
    width = old_species.shape[0] // blocks
    channels = w_up.shape[1]
    ghosts = send_list.size
    wide = slots + ghosts
    edges = entries * slots
    rows = w_rad.shape[2]
    species = old_species.reshape(blocks, width)
    i32 = jnp.int32

    (packed,) = call(
        pack_kernel,
        [(3 * ROWS, width)],
        [],
        [block_dest.T, block_count, old_pos, species],
        [
            pltpu.SMEM((1, blocks), i32),
            pltpu.SMEM((blocks,), i32),
            old_pos.shape,
            pltpu.VMEM(species.shape, i32),
            pltpu.SemaphoreType.DMA((4,)),
        ],
        name="pack",
        raw=True,
    )
    got_chip = swap_chip(packed)
    got_core = swap_core(packed)
    onehot, send, gamma, radials, species_up, species_in, weights, reads, onehot_t, send_t = call(
        prepare_kernel,
        [
            ((wide, edges), bf16),
            ((slots, ghosts), bf16),
            (2, ROWS, edges),
            ((2, rows, 3 * ROWS), bf16),
            ((channels, 3 * ROWS), bf16),
            ((channels, 3 * ROWS), bf16),
            ((6, channels, 3 * channels), bf16),
            (2, channels, slots),
            ((edges, wide), bf16),
            ((ghosts, slots), bf16),
        ],
        [],
        [gammas, neighbours, send_list, embed, w_up, w_rad, w_mix, readout],
        [
            pltpu.SMEM(gammas.shape, f32),
            pltpu.VMEM(neighbours.shape, i32),
            pltpu.VMEM(send_list.shape, i32),
            embed.shape,
            w_up.shape,
            w_rad.shape,
            w_mix.shape,
            readout.shape,
            (ROWS, channels),
            pltpu.SemaphoreType.DMA((8,)),
        ],
        name="prepare",
        raw=True,
        us=3.0,
    )
    small = (ROWS, LANES)
    tall = (CHIP_ROWS, LANES)
    table, pick_gx, pick_core, pick_chip = call(
        assemble_kernel,
        [(ROWS, slots), small, small, tall],
        [],
        [packed, got_core, got_chip, send],
        name="assemble",
        us=0.2,
    )
    got_chip = swap_chip(pick_chip)
    got_gx = swap_gx(pick_gx)
    got_core = swap_core(pick_core)
    (found_own,) = call(
        own_positions_kernel, [(ROWS, edges)], [], [table, onehot], name="own_positions", us=0.02
    )
    flat = (channels, slots)
    square = (channels, LANES)
    half = (channels // 2, LANES)
    fields_shape = (9, channels, slots)
    h_one, slope, send_gx, send_core, send_chip, geo, angular, rad_one, feat_one, fields_one = call(
        first_layer_kernel,
        [flat, flat, square, half, half, (8, ROWS, edges), (5, ROWS, edges), (rows, edges), (channels, edges), fields_shape],
        [],
        [found_own, table, got_gx, got_core, got_chip, onehot, send, gamma, radials, species_up, species_in, weights],
        [flat],
        name="first_layer",
        us=2.5,
    )
    got_chip = swap_chip(send_chip)
    got_gx = swap_gx(send_gx)
    got_core = swap_core(send_core)
    rad_two, slope_one, slope_two, base, found_two = call(
        radial_kernel,
        [(rows, edges), (rows, edges), (rows, edges), (TALL, LANES), (channels, edges)],
        [atom_ref],
        [geo, gamma, radials, table, h_one, onehot, weights],
        name="radials",
        us=2.0,
    )
    feat_two, fields_two, g_two, g_own, tally = call(
        second_layer_kernel,
        [(channels, edges), fields_shape, flat, flat, (TALL, LANES)],
        [],
        [base, table, h_one, got_gx, got_core, got_chip, onehot, geo, angular, rad_two, weights, reads, found_two],
        [flat],
        name="second_layer",
        us=2.5,
    )
    bits = (lax.axis_size("yz") - 1).bit_length()
    got_sums = partners(tally, "yz", [0])
    g_feat, g_off = call(
        second_gradient_kernel,
        [(channels, edges), (ROWS, edges)],
        [],
        [geo, rad_two, slope_two, feat_two, fields_two, g_two],
        name="second_gradient",
        us=2.5,
    )
    got_sums, g_off = together(got_sums, g_off)
    tally = sum(got_sums, tally)
    got_sums = partners(tally, "yz", [bits - 1] if bits > 1 else [])
    left, send_gx, send_core, send_chip, g_ghost, g_target_two = call(
        ghost_gradient_kernel,
        [((2 * channels + 3 * ROWS, edges), bf16), square, half, half, (ROWS, ghosts), (ROWS, slots)],
        [],
        [g_feat, g_off, onehot_t, weights],
        name="ghost_gradient",
        us=1.5,
    )
    got_sums, g_ghost = together(got_sums, g_ghost)
    tally = sum(got_sums, tally)
    got_chip = swap_chip(send_chip)
    got_gx = return_gx(send_gx)
    got_core = swap_core(send_core)
    tally = tally[:ROWS]
    got_sums = partners(tally, "yz", [1] if bits > 2 else [])
    factors, g_h, g_local_two = call(
        factor_kernel,
        [(4, channels, edges), flat, (ROWS, slots)],
        [],
        [geo, rad_one, slope_one, feat_one, fields_one, left, onehot_t, weights, g_own],
        name="factors",
        us=3.0,
    )
    got_sums, got_chip = together(got_sums, got_chip)
    tally = sum(got_sums, tally)
    tally = jnp.pad(tally, ((0, TALL - ROWS), (0, 0)))
    got_sums = partners(tally, "yz", range(2, bits - 1))
    left, g_target_one, send_gx, send_core, send_chip = call(
        first_gradient_kernel,
        [((3 * ROWS, edges), bf16), (ROWS, slots), (8, LANES), (8, LANES), (8, LANES)],
        [],
        [g_h, got_gx, got_core, got_chip, slope, factors, geo, g_ghost, onehot_t, send_t, weights],
        [flat, (ROWS, edges)],
        name="first_gradient",
        us=1.2,
    )
    got_sums, left = together(got_sums, left)
    tally = sum(got_sums, tally)
    got_chip = swap_chip(send_chip)
    got_gx = return_gx(send_gx)
    got_core = swap_core(send_core)
    (g_pos,) = call(
        local_kernel,
        [(ROWS, slots)],
        [],
        [left, onehot_t, g_local_two, g_target_two, g_target_one],
        name="local",
        us=0.5,
    )
    tally = tally[:ROWS]
    tallies = [tally] + partners(tally, "gx", range((lax.axis_size("gx") - 1).bit_length()))
    (g_sum,) = call(
        chip_force_kernel, [(ROWS, slots)], [], [g_pos, got_chip, send_t], name="chip_forces", us=0.1
    )
    forces, energy = call(
        force_kernel,
        [(3, slots), (1, 1)],
        [],
        [g_sum, got_gx, got_core, send_t] + tallies,
        name="forces",
    )
    return (forces, energy.reshape(()))


def solution(mesh):
    return jax.shard_map(
        shards,
        mesh=mesh,
        in_specs=(
            P(None, ("gx", "yz")),
            P(("gx", "yz")),
            P(("gx", "yz"), None),
            P(("gx", "yz")),
            P(("gx", "yz"), None),
            P(None, ("gx", "yz")),
            P(),
            P(),
            P(),
            P(),
            P(),
            P(),
            P(),
        ),
        out_specs=(P(None, ("gx", "yz")), P()),
        check_vma=False,
    )
```

```python
import functools
import math

import jax
import jax.numpy as jnp
from jax import lax
from jax.experimental import pallas as pl
from jax.experimental.pallas import tpu as pltpu
from jax.sharding import PartitionSpec as P

root_three = math.sqrt(3.0)
root_five = math.sqrt(5.0)
root_fifteen = math.sqrt(15.0)
f32 = jnp.float32
bf16 = jnp.bfloat16
ROWS = 8
LANES = 128
TALL = 8
CHIP_ROWS = 16
SUMS_UNROLL = 16
EDGE_UNROLL = 16
FORCE_UNROLL = 16
VMEM_BYTES = 16 * 1024 * 1024


def split2(value):
    high = value.astype(bf16)
    return high, (value - high.astype(f32)).astype(bf16)


def split3(value):
    high = value.astype(bf16)
    rest = value - high.astype(f32)
    mid = rest.astype(bf16)
    return high, mid, (rest - mid.astype(f32)).astype(bf16)


def dot(left, right, left_dim, right_dim):
    return lax.dot_general(
        left, right, (((left_dim,), (right_dim,)), ((), ())), preferred_element_type=f32
    )


def dot3(left, right, left_dim, right_dim):
    lh, ll = split2(left)
    rh, rl = split2(right)
    return (
        dot(lh, rh, left_dim, right_dim)
        + dot(lh, rl, left_dim, right_dim)
        + dot(ll, rh, left_dim, right_dim)
    )


def pieces(table):
    high = table.astype(bf16).astype(f32)
    rest = table - high
    mid = rest.astype(bf16).astype(f32)
    return jnp.concatenate([high, mid, rest - mid], axis=0).astype(bf16)


def pieces_f32(table):
    high = table.astype(bf16).astype(f32)
    rest = table - high
    mid = rest.astype(bf16).astype(f32)
    return jnp.concatenate([high, mid, rest - mid], axis=0)


def whole(stack):
    return stack[0:ROWS] + stack[ROWS : 2 * ROWS] + stack[2 * ROWS : 3 * ROWS]


def onehot_rows(count, row):
    places = lax.broadcasted_iota(jnp.int32, (count, row.shape[1]), 0)
    return jnp.where(places == row, 1.0, 0.0).astype(bf16)


def column(row):
    n = row.shape[1]
    down = lax.broadcasted_iota(jnp.int32, (n, n), 0)
    across = lax.broadcasted_iota(jnp.int32, (n, n), 1)
    return jnp.sum(jnp.where(down == across, jnp.broadcast_to(row, (n, n)), 0.0), axis=1, keepdims=True)


def left_half(shape):
    return lax.broadcasted_iota(jnp.int32, shape, 1) < shape[1] // 2


def is_even():
    return lax.rem(lax.axis_index("yz"), 2) == 0


def previous_and_next(core, chip):
    even = is_even()
    return jnp.where(even, chip, core), jnp.where(even, core, chip)


def faces_yz(core, chip):
    before, after = previous_and_next(core, chip)
    return jnp.where(left_half(core.shape), before, after)


def pack_halves(value):
    half = value.shape[0] // 2
    top, bottom = value[0:half], value[half:]
    left = left_half(top.shape)
    turned_top, turned_bottom = pltpu.roll(top, LANES // 2, 1), pltpu.roll(bottom, LANES // 2, 1)
    return jnp.where(left, top, turned_bottom), jnp.where(left, turned_top, bottom)


def join_halves(left_columns, right_columns):
    left = left_half(left_columns.shape)
    top = jnp.where(left, left_columns, pltpu.roll(right_columns, LANES // 2, 1))
    bottom = jnp.where(left, pltpu.roll(left_columns, LANES // 2, 1), right_columns)
    return jnp.concatenate([top, bottom], axis=0)


def stacked_left(weights):
    high, low = split2(weights)
    return jnp.concatenate([high, high, low], axis=1)


def stacked_right(value):
    high, low = split2(value)
    return jnp.concatenate([high, low, high], axis=0)


def stacked_rows(value):
    high = value.astype(bf16).astype(f32)
    return jnp.concatenate([high, high, value - high], axis=0).astype(bf16)


def stacked_rows_left(value):
    high = value.astype(bf16).astype(f32)
    low = value - high
    return jnp.concatenate([high, low, high], axis=0)


def species_onehot(code, count):
    places = lax.rem(lax.broadcasted_iota(jnp.int32, (3 * count, code.shape[1]), 0), count)
    return jnp.where(places == code.astype(jnp.int32), 1.0, 0.0).astype(bf16)


def matmul(left, right):
    return dot(left, right, 1, 0)


def repeat(row, times):
    return jnp.concatenate([row] * times, axis=1)


def tile(index):
    return pl.ds(pl.multiple_of(index * ROWS, ROWS), ROWS)


def degree_tiles(index, channels):
    return [pl.ds(pl.multiple_of(degree * channels + index * ROWS, ROWS), ROWS) for degree in range(3)]


def lane_parts(slots, entries):
    for part in range(slots // LANES):
        yield pl.ds(part * LANES, LANES), [pl.ds(k * slots + part * LANES, LANES) for k in range(entries)]


U, R, SCALE, SQUARE = 0, 3, 6, 7


def gather_sums(geo, y_ref, rad_ref, feat_ref, fields_ref, invariant_ref):
    channels, slots = invariant_ref.shape
    entries = feat_ref.shape[1] // slots
    for lanes, edges in lane_parts(slots, entries):
        first = [[geo[U + d, :, edges[k]] for d in range(3)] for k in range(entries)]
        second = [[y_ref[m, :, edges[k]] for m in range(5)] for k in range(entries)]

        def body(index, carry):
            rows = tile(index)
            degrees = degree_tiles(index, channels)
            sums = None
            for k in range(entries):
                feat = feat_ref[rows, edges[k]]
                zero, one, two = [rad_ref[degree, edges[k]] * feat for degree in degrees]
                terms = [zero] + [item * one for item in first[k]] + [item * two for item in second[k]]
                sums = terms if k == 0 else [old + new for old, new in zip(sums, terms)]
            total = sums[0]
            for item in sums[1:]:
                total = total + item * item
            invariant_ref[rows, lanes] = total
            a1, a2, a3, a4, a5, a6, a7, a8 = sums[1:]
            c6 = (1.0 / root_three) * a6
            for number, field in enumerate((a1, a2, a3, a4, a5, a7, a8 - c6, a8 + c6, c6 + c6)):
                fields_ref[number, rows, lanes] = field
            return carry

        lax.fori_loop(0, channels // ROWS, body, 0, unroll=SUMS_UNROLL)


def direction_terms(fields, unit):
    a1, a2, a3, a4, a5, a7, minus, plus, twice = fields
    ux, uy, uz = unit
    h_x = uy * a4 + uz * a7 + ux * minus
    h_y = ux * a4 + uz * a5 - uy * plus
    h_z = uy * a5 + ux * a7 + uz * twice
    one = ux * a1 + uy * a2 + uz * a3
    two = 0.5 * (ux * h_x + uy * h_y + uz * h_z)
    return h_x, h_y, h_z, one, two


def offset_gradients(found, geo_ref, edges):
    g_s, g_x, g_y, g_z = [jnp.sum(item, axis=0, keepdims=True) for item in found]
    rx, ry, rz = [geo_ref[R + d, 0:1, edges] for d in range(3)]
    scale = geo_ref[SCALE, 0:1, edges]
    along = g_x * rx + g_y * ry + g_z * rz
    radial_part = 2.0 * g_s - scale * scale * scale * along
    return scale * g_x + rx * radial_part, scale * g_y + ry * radial_part, scale * g_z + rz * radial_part


def silu_and_slope(mixed):
    sigma = 1.0 / (1.0 + jnp.exp(-mixed))
    return mixed * sigma, sigma * (1.0 + mixed * (1.0 - sigma))


def fetch(pairs, sems):
    copies = [pltpu.make_async_copy(source, target, sems.at[i]) for i, (source, target) in enumerate(pairs)]
    for copy in copies:
        copy.start()
    return copies


def pack_kernel(dest_hbm, count_hbm, pos_hbm, species_hbm, out, dest, count, pos, species, sems):
    copies = fetch(((dest_hbm, dest), (count_hbm, count), (pos_hbm, pos), (species_hbm, species)), sems)
    blocks, width = species.shape
    place = lax.broadcasted_iota(jnp.int32, (1, width), 1)
    out[...] = jnp.zeros(out.shape, f32)
    for copy in copies:
        copy.wait()
    for group in range(3):
        coords = jnp.zeros((3, width), f32)
        code = jnp.full((1, width), -1.0, f32)
        for b in range(blocks):
            hit = dest[0, b] == group
            coords = jnp.where(hit, pos[:, b * width : (b + 1) * width], coords)
            alive = jnp.where(place < count[b], species[b : b + 1, :].astype(f32), -1.0)
            code = jnp.where(hit, alive, code)
        out[group * ROWS : group * ROWS + 3, :] = coords
        out[group * ROWS + 3 : group * ROWS + 4, :] = code


def prepare_kernel(
    gammas_hbm, nbr_hbm, lists_hbm, embed_hbm, w_up_hbm, w_rad_hbm, w_mix_hbm, readout_hbm,
    onehot, send, gamma, radials, species_up, species_in, weights, reads, onehot_t, send_t,
    gammas, nbr, lists, embed, w_up, w_rad, w_mix, readout, padded, sems,
):
    copies = fetch(
        (
            (nbr_hbm, nbr),
            (lists_hbm, lists),
            (gammas_hbm, gammas),
            (w_rad_hbm, w_rad),
            (embed_hbm, embed),
            (w_up_hbm, w_up),
            (w_mix_hbm, w_mix),
            (readout_hbm, readout),
        ),
        sems,
    )
    entries, slots = nbr.shape
    for copy in copies:
        copy.wait()
    wide = onehot.shape[0]
    for k in range(entries):
        onehot[:, k * slots : (k + 1) * slots] = onehot_rows(wide, nbr[k : k + 1, :])
    faces, ghosts = lists.shape
    for face in range(faces):
        send[:, face * ghosts : (face + 1) * ghosts] = onehot_rows(slots, lists[face : face + 1, :])
    count = w_rad.shape[1]
    which = lax.broadcasted_iota(jnp.int32, gamma.shape[1:], 0)
    channels = w_up.shape[1]
    place = lax.broadcasted_iota(jnp.int32, w_rad.shape[1:], 1)
    scales = jnp.where(place < channels, 1.0, jnp.where(place < 2 * channels, root_three, root_fifteen)) * (1.0 / entries)
    for layer in range(2):
        value = jnp.zeros(which.shape, f32)
        for q in range(count):
            value = jnp.where(which == q, gammas[layer, q], value)
        gamma[layer] = value
        radials[layer] = stacked_rows_left(w_rad[layer] * scales).T.astype(bf16)
    padded[...] = jnp.zeros(padded.shape, f32)
    padded[0 : embed.shape[0], :] = embed[...]
    species = padded[...]
    species_up[...] = pieces_f32(dot3(species, w_up[0], 1, 0)).T.astype(bf16)
    species_in[...] = pieces_f32(species).T.astype(bf16)
    for number, item in enumerate(
        (w_mix[0].T, w_up[1].T, w_mix[1].T, w_mix[1], w_up[1], w_mix[0])
    ):
        weights[number] = stacked_left(item)
    for layer in range(2):
        reads[layer] = jnp.broadcast_to(column(readout[layer : layer + 1, :]), reads.shape[1:])
    index_rows = jnp.concatenate([nbr[...].astype(f32), jnp.zeros((ROWS - entries, slots), f32)], axis=0)
    index_columns = index_rows.T
    across = lax.broadcasted_iota(jnp.int32, (slots, wide), 1).astype(f32)
    for k in range(entries):
        onehot_t[k * slots : (k + 1) * slots, :] = jnp.where(
            across == index_columns[:, k : k + 1], 1.0, 0.0
        ).astype(bf16)
    list_rows = jnp.concatenate([lists[...].astype(f32), jnp.zeros((ROWS - faces, ghosts), f32)], axis=0)
    list_columns = list_rows.T
    across = lax.broadcasted_iota(jnp.int32, (ghosts, slots), 1).astype(f32)
    for face in range(faces):
        send_t[face * ghosts : (face + 1) * ghosts, :] = jnp.where(
            across == list_columns[:, face : face + 1], 1.0, 0.0
        ).astype(bf16)


def assemble_kernel(own, core, chip, send, table, pick_gx, pick_core, pick_chip):
    before, after = previous_and_next(core[...], chip[...])
    blocks = [after[0:ROWS], own[ROWS : 2 * ROWS, :], before[2 * ROWS : 3 * ROWS]]
    slots = jnp.concatenate(blocks, axis=1)
    table[...] = slots
    picked = whole(matmul(pieces(slots), send[...]))
    pick_gx[...] = picked[:, 0:LANES]
    pick_core[...] = picked[:, LANES : 2 * LANES]
    pick_chip[...] = jnp.zeros(pick_chip.shape, f32)
    pick_chip[0:ROWS, :] = picked[:, LANES : 2 * LANES]


def own_positions_kernel(table, onehot, found):
    found[...] = whole(matmul(pieces(table[...]), onehot[0 : table.shape[1], :]))


def first_layer_kernel(
    found_own, table, got_gx, got_core, got_chip, onehot, send, gamma, radials, species_up, species_in, weights,
    h_out, slope_out, send_gx, send_core, send_chip, geo, y_ref, rad_ref, feat_ref, fields_ref,
    inv_ref,
):
    slots = table.shape[1]
    edges = onehot.shape[1]
    entries = edges // slots
    ghosts = jnp.concatenate([got_gx[...], faces_yz(got_core[...], got_chip[0:ROWS, :])], axis=1)
    found = found_own[...] + whole(matmul(pieces(ghosts), onehot[slots:, :]))
    feat_ref[...] = matmul(species_up[...], species_onehot(found[3:4], ROWS))
    spread = lambda row: jnp.broadcast_to(row, (ROWS, edges))
    rx, ry, rz = [
        spread(found[d : d + 1] - repeat(table[d : d + 1, :], entries)) for d in range(3)
    ]
    square = rx * rx + ry * ry + rz * rz
    basis = jnp.exp(-gamma[0] * square)
    rad_ref[...] = matmul(radials[0], stacked_rows(basis))
    scale = lax.rsqrt(1.0 + square)
    ux, uy, uz = rx * scale, ry * scale, rz * scale
    for number, item in enumerate((ux, uy, uz, rx, ry, rz, scale, square)):
        geo[number] = item
    xx, yy, zz = ux * ux, uy * uy, uz * uz
    for number, item in enumerate(
        (ux * uy, uy * uz, (0.5 / root_three) * (2.0 * zz - xx - yy), ux * uz, 0.5 * (xx - yy))
    ):
        y_ref[number] = item
    gather_sums(geo, y_ref, rad_ref, feat_ref, fields_ref, inv_ref)
    mixed = matmul(weights[0], stacked_right(inv_ref[...]))
    code = table[3:4, :]
    live = jnp.where(code >= 0.0, 1.0, 0.0)
    h_zero = matmul(species_in[...], species_onehot(code, ROWS))
    value, slope = silu_and_slope(mixed)
    h_one = live * (h_zero + value)
    h_out[...] = h_one
    slope_out[...] = live * slope
    channels = h_one.shape[0]
    picked = matmul(jnp.concatenate(split2(h_one), axis=0), send[...])
    picked = picked[0:channels] + picked[channels : 2 * channels]
    send_gx[...] = picked[:, 0:LANES]
    to_next, to_previous = pack_halves(picked[:, LANES : 2 * LANES])
    even = is_even()
    send_core[...] = jnp.where(even, to_next, to_previous)
    send_chip[...] = jnp.where(even, to_previous, to_next)


def radial_kernel(
    atom_ref, geo, gamma, radials, table, h_one, onehot, weights,
    rad_two, slope_one, slope_two, base, found_two,
):
    square = geo[SQUARE]
    basis = jnp.exp(-gamma[1] * square)
    rad_two[...] = matmul(radials[1], stacked_rows(basis))
    slope_two[...] = matmul(radials[1], stacked_rows(-gamma[1] * basis))
    slope_one[...] = matmul(radials[0], stacked_rows(-gamma[0] * jnp.exp(-gamma[0] * square)))
    code = table[3:4, :]
    live = jnp.where(code >= 0.0, 1.0, 0.0)
    energy = jnp.zeros(code.shape, f32)
    for kind in range(atom_ref.shape[0]):
        energy = energy + jnp.where(code == float(kind), atom_ref[kind], 0.0)
    fold = lambda row: sum(row[:, c : c + LANES] for c in range(0, code.shape[1], LANES))
    base[...] = jnp.zeros(base.shape, f32)
    base[0:1, :] = fold(energy)
    base[1:2, :] = fold(live)
    channels, slots = h_one.shape
    projected = matmul(weights[1], stacked_right(h_one[...]))
    both = matmul(jnp.concatenate(split2(projected), axis=0), onehot[0:slots, :])
    found_two[...] = both[0:channels] + both[channels : 2 * channels]


def factor_kernel(
    geo, rad_ref, slope_ref, feat_ref, fields_ref, left, onehot_t, weights, g_own,
    factors, g_h, g_pos,
):
    channels, slots = fields_ref.shape[1:]
    entries = feat_ref.shape[1] // slots
    scattered = matmul(left[...], onehot_t[:, 0:slots])
    g_proj = scattered[0:channels] + scattered[channels : 2 * channels]
    g_pos[...] = whole(scattered[2 * channels : 2 * channels + 3 * ROWS])
    g_h[...] = matmul(weights[4], stacked_right(g_proj)) + g_own[...]
    for lanes, edges in lane_parts(slots, entries):
        units = [[geo[U + d, :, edges[k]] for d in range(3)] for k in range(entries)]

        def body(index, carry):
            rows = tile(index)
            degrees = degree_tiles(index, channels)
            fields = [fields_ref[m, rows, lanes] for m in range(9)]
            for k in range(entries):
                h_x, h_y, h_z, one, two = direction_terms(fields, units[k])
                feat = feat_ref[rows, edges[k]]
                r1, r2 = [rad_ref[d, edges[k]] * feat for d in degrees[1:]]
                d0, d1, d2 = [slope_ref[d, edges[k]] for d in degrees]
                factors[0, rows, edges[k]] = feat * (0.5 * d0 + d1 * one + d2 * two)
                factors[1, rows, edges[k]] = r1 * fields[0] + r2 * h_x
                factors[2, rows, edges[k]] = r1 * fields[1] + r2 * h_y
                factors[3, rows, edges[k]] = r1 * fields[2] + r2 * h_z
            return carry

        lax.fori_loop(0, channels // ROWS, body, 0, unroll=2)


def second_layer_kernel(
    base, table, h_one, got_gx, got_core, got_chip, onehot, geo, y_ref, rad_ref, weights, reads, found_two,
    feat_ref, fields_ref, g_ref, g_own, tally,
    inv_ref,
):
    h_local = h_one[...]
    channels, slots = h_local.shape
    before, after = previous_and_next(got_core[...], got_chip[...])
    ghosts = jnp.concatenate([got_gx[...], join_halves(before, after)], axis=1)
    projected = matmul(weights[1], stacked_right(ghosts))
    both = matmul(jnp.concatenate(split2(projected), axis=0), onehot[slots:, :])
    feat_ref[...] = found_two[...] + (both[0:channels] + both[channels : 2 * channels])
    gather_sums(geo, y_ref, rad_ref, feat_ref, fields_ref, inv_ref)
    mixed = matmul(weights[2], stacked_right(inv_ref[...]))
    live = jnp.where(table[3:4, :] >= 0.0, 1.0, 0.0)
    value, slope = silu_and_slope(mixed)
    h_two = live * (h_local + value)
    energy = jnp.sum(reads[0] * h_local + reads[1] * h_two, axis=0, keepdims=True)
    tally[...] = base[...]
    tally[0:1, :] += sum(energy[:, c : c + LANES] for c in range(0, slots, LANES))
    g_ref[...] = matmul(weights[3], stacked_right((live * reads[1]) * slope))
    g_own[...] = live * (reads[0] + reads[1])


def second_gradient_kernel(
    geo, rad_ref, slope_ref, feat_ref, fields_ref, g_ref,
    g_feat, g_off,
):
    channels, slots = g_ref.shape
    entries = feat_ref.shape[1] // slots
    g_off[...] = jnp.zeros(g_off.shape, f32)
    for lanes, edges in lane_parts(slots, entries):
        units = [[geo[U + d, :, edges[k]] for d in range(3)] for k in range(entries)]

        def body(index, carry):
            rows = tile(index)
            degrees = degree_tiles(index, channels)
            g = g_ref[rows, lanes]
            fields = [(g + g) * fields_ref[m, rows, lanes] for m in range(9)]
            found = []
            for k in range(entries):
                h_x, h_y, h_z, one, two = direction_terms(fields, units[k])
                feat = feat_ref[rows, edges[k]]
                r0, r1, r2 = [rad_ref[d, edges[k]] for d in degrees]
                d0, d1, d2 = [slope_ref[d, edges[k]] for d in degrees]
                g_feat[rows, edges[k]] = g * r0 + r1 * one + r2 * two
                q1, q2 = feat * r1, feat * r2
                found += [
                    carry[4 * k] + feat * (g * d0 + d1 * one + d2 * two),
                    carry[4 * k + 1] + (q1 * fields[0] + q2 * h_x),
                    carry[4 * k + 2] + (q1 * fields[1] + q2 * h_y),
                    carry[4 * k + 3] + (q1 * fields[2] + q2 * h_z),
                ]
            return tuple(found)

        zero = jnp.zeros((ROWS, LANES), f32)
        found = lax.fori_loop(0, channels // ROWS, body, (zero,) * (4 * entries), unroll=EDGE_UNROLL)
        for k in range(entries):
            for d, item in enumerate(offset_gradients(found[4 * k : 4 * k + 4], geo, edges[k])):
                g_off[d : d + 1, edges[k]] = item


def ghost_gradient_kernel(g_feat, g_off, onehot_t, weights, left, send_gx, send_core, send_chip, g_ghost, g_target):
    channels, edge_count = g_feat.shape
    wide = onehot_t.shape[1]
    slots = g_target.shape[1]
    entries = edge_count // slots
    stacked = jnp.concatenate([*split2(g_feat[...]), pieces(g_off[...])], axis=0)
    left[...] = stacked
    scattered = matmul(stacked, onehot_t[:, slots:wide])
    g_proj = scattered[0:channels] + scattered[channels : 2 * channels]
    g_ghost[...] = whole(scattered[2 * channels : 2 * channels + 3 * ROWS])
    g_all = matmul(weights[4], stacked_right(g_proj))
    send_gx[...] = g_all[:, 0:LANES]
    to_previous, to_next = pack_halves(g_all[:, LANES : 2 * LANES])
    even = is_even()
    send_core[...] = jnp.where(even, to_next, to_previous)
    send_chip[...] = jnp.where(even, to_previous, to_next)
    g_target[...] = sum(g_off[:, k * slots : (k + 1) * slots] for k in range(entries))


def first_gradient_kernel(
    g_h, got_gx, got_core, got_chip, slope, factors, geo, g_ghost, onehot_t, send_t, weights,
    left, g_target, send_gx, send_core, send_chip,
    g_ref, g_off,
):
    channels, slots = slope.shape
    entries = geo.shape[2] // slots
    before, after = previous_and_next(got_core[...], got_chip[...])
    back = jnp.concatenate([got_gx[...], join_halves(after, before)], axis=1)
    returned = matmul(jnp.concatenate(split2(back), axis=0), send_t[...])
    g_total = g_h[...] + (returned[0:channels] + returned[channels : 2 * channels])
    g_ref[...] = matmul(weights[5], stacked_right(g_total * (2.0 * slope[...])))
    g_off[...] = jnp.zeros(g_off.shape, f32)
    for lanes, edges in lane_parts(slots, entries):

        def body(index, carry):
            rows = tile(index)
            g = g_ref[rows, lanes]
            return tuple(
                carry[4 * k + m] + g * factors[m, rows, edges[k]] for k in range(entries) for m in range(4)
            )

        zero = jnp.zeros((ROWS, LANES), f32)
        found = lax.fori_loop(0, channels // ROWS, body, (zero,) * (4 * entries), unroll=FORCE_UNROLL)
        for k in range(entries):
            for d, item in enumerate(offset_gradients(found[4 * k : 4 * k + 4], geo, edges[k])):
                g_off[d : d + 1, edges[k]] = item
    wide = onehot_t.shape[1]
    stacked = pieces(g_off[...])
    left[...] = stacked
    g_ext = whole(matmul(stacked, onehot_t[:, slots:wide])) + g_ghost[...]
    for out, piece in ((send_gx, 0), (send_core, 1), (send_chip, 1)):
        out[...] = jnp.zeros(out.shape, f32)
        out[0:ROWS, :] = g_ext[:, piece * LANES : (piece + 1) * LANES]
    g_target[...] = sum(g_off[:, k * slots : (k + 1) * slots] for k in range(entries))


def local_kernel(left, onehot_t, g_local_two, g_target_two, g_target_one, g_pos):
    slots = g_pos.shape[1]
    g_pos[...] = whole(matmul(left[...], onehot_t[:, 0:slots])) + g_local_two[...] - g_target_two[...] - g_target_one[...]


def chip_force_kernel(g_pos, got_chip, send_t, g_sum):
    half = left_half((ROWS, LANES))
    wanted = jnp.where(is_even(), 1.0, 0.0)
    kept = got_chip[0:ROWS, :] * jnp.where(half, 1.0 - wanted, wanted)
    ghosts = send_t.shape[0]
    g_sum[...] = g_pos[...] + whole(matmul(pieces(kept), send_t[ghosts - LANES : ghosts, :]))


def force_kernel(g_sum, got_gx, got_core, send_t, *rest):
    tallies, (forces, energy) = rest[:-2], rest[-2:]
    half = left_half((ROWS, LANES))
    wanted = jnp.where(is_even(), 0.0, 1.0)
    kept = got_core[0:ROWS, :] * jnp.where(half, 1.0 - wanted, wanted)
    back = jnp.concatenate([got_gx[0:ROWS, :], kept], axis=1)
    forces[...] = -(g_sum[...] + whole(matmul(pieces(back), send_t[...])))[0:3]
    sums = jnp.sum(sum(item[0:2, :] for item in tallies), axis=1, keepdims=True)
    energy[...] = sums[0:1, :] / sums[1:2, :]


def call(kernel, outs, scalars, arrays, scratch=(), name=None, raw=False, us=1.0):
    in_vmem = pl.BlockSpec(memory_space=pltpu.VMEM)
    in_smem = pl.BlockSpec(memory_space=pltpu.SMEM)
    in_hbm = pl.BlockSpec(memory_space=pltpu.HBM)
    shapes = [jax.ShapeDtypeStruct(*item) if isinstance(item[0], tuple) else jax.ShapeDtypeStruct(item, f32) for item in outs]
    return pl.pallas_call(
        kernel,
        out_shape=shapes,
        in_specs=[in_smem] * len(scalars) + [in_hbm if raw else in_vmem] * len(arrays),
        out_specs=[in_vmem] * len(outs),
        scratch_shapes=[pltpu.VMEM(item, f32) if isinstance(item, tuple) else item for item in scratch],
        compiler_params=pltpu.CompilerParams(vmem_limit_bytes=VMEM_BYTES),
        cost_estimate=pl.CostEstimate(flops=int(us * 1e9), bytes_accessed=int(us * 3e6), transcendentals=0),
        name=name,
    )(*scalars, *[pltpu.with_memory_space_constraint(item, pltpu.HBM) if raw else item for item in arrays])


def swap_core(value):
    size = lax.axis_size("yz")
    return lax.ppermute(value, "yz", [(i, i ^ 1) for i in range(size)])


def swap_chip(value):
    size = lax.axis_size("yz")
    return lax.ppermute(value, "yz", [(i, (i + 1 if i % 2 else i - 1) % size) for i in range(size)])


def shift(value, axis, by):
    size = lax.axis_size(axis)
    return lax.ppermute(value, axis, [(i, (i + by) % size) for i in range(size)])


def swap_gx(value):
    size = lax.axis_size("gx")
    if size == 2:
        return shift(value, "gx", 1)
    half = value.shape[1] // 2
    return jnp.concatenate(
        [shift(value[:, :half], "gx", 1), shift(value[:, half:], "gx", -1)], axis=1
    )


def return_gx(value):
    size = lax.axis_size("gx")
    if size == 2:
        return shift(value, "gx", 1)
    half = value.shape[1] // 2
    return jnp.concatenate(
        [shift(value[:, :half], "gx", -1), shift(value[:, half:], "gx", 1)], axis=1
    )


def partners(value, bits):
    axes = ("gx", "yz")
    size = lax.axis_size(axes)
    steps = [0]
    for bit in bits:
        steps += [step ^ (1 << bit) for step in steps]
    return [lax.ppermute(value, axes, [(i, i ^ step) for i in range(size)]) for step in steps[1:]]


def together(values, other):
    *values, other = lax.optimization_barrier((*values, other))
    return values, other


def shards(
    old_pos,
    old_species,
    block_dest,
    block_count,
    send_list,
    neighbours,
    embed,
    atom_ref,
    w_up,
    gammas,
    w_rad,
    w_mix,
    readout,
):
    entries, slots = neighbours.shape
    blocks = block_dest.shape[0]
    width = old_species.shape[0] // blocks
    channels = w_up.shape[1]
    ghosts = send_list.size
    wide = slots + ghosts
    edges = entries * slots
    rows = w_rad.shape[2]
    species = old_species.reshape(blocks, width)
    i32 = jnp.int32

    (packed,) = call(
        pack_kernel,
        [(3 * ROWS, width)],
        [],
        [block_dest.T, block_count, old_pos, species],
        [
            pltpu.SMEM((1, blocks), i32),
            pltpu.SMEM((blocks,), i32),
            old_pos.shape,
            pltpu.VMEM(species.shape, i32),
            pltpu.SemaphoreType.DMA((4,)),
        ],
        name="pack",
        raw=True,
    )
    got_chip = swap_chip(packed)
    got_core = swap_core(packed)
    onehot, send, gamma, radials, species_up, species_in, weights, reads, onehot_t, send_t = call(
        prepare_kernel,
        [
            ((wide, edges), bf16),
            ((slots, ghosts), bf16),
            (2, ROWS, edges),
            ((2, rows, 3 * ROWS), bf16),
            ((channels, 3 * ROWS), bf16),
            ((channels, 3 * ROWS), bf16),
            ((6, channels, 3 * channels), bf16),
            (2, channels, slots),
            ((edges, wide), bf16),
            ((ghosts, slots), bf16),
        ],
        [],
        [gammas, neighbours, send_list, embed, w_up, w_rad, w_mix, readout],
        [
            pltpu.SMEM(gammas.shape, f32),
            pltpu.VMEM(neighbours.shape, i32),
            pltpu.VMEM(send_list.shape, i32),
            embed.shape,
            w_up.shape,
            w_rad.shape,
            w_mix.shape,
            readout.shape,
            (ROWS, channels),
            pltpu.SemaphoreType.DMA((8,)),
        ],
        name="prepare",
        raw=True,
        us=3.0,
    )
    small = (ROWS, LANES)
    tall = (CHIP_ROWS, LANES)
    table, pick_gx, pick_core, pick_chip = call(
        assemble_kernel,
        [(ROWS, slots), small, small, tall],
        [],
        [packed, got_core, got_chip, send],
        name="assemble",
        us=0.2,
    )
    got_chip = swap_chip(pick_chip)
    got_gx = swap_gx(pick_gx)
    got_core = swap_core(pick_core)
    (found_own,) = call(
        own_positions_kernel, [(ROWS, edges)], [], [table, onehot], name="own_positions", us=0.02
    )
    flat = (channels, slots)
    square = (channels, LANES)
    half = (channels // 2, LANES)
    fields_shape = (9, channels, slots)
    h_one, slope, send_gx, send_core, send_chip, geo, angular, rad_one, feat_one, fields_one = call(
        first_layer_kernel,
        [flat, flat, square, half, half, (8, ROWS, edges), (5, ROWS, edges), (rows, edges), (channels, edges), fields_shape],
        [],
        [found_own, table, got_gx, got_core, got_chip, onehot, send, gamma, radials, species_up, species_in, weights],
        [flat],
        name="first_layer",
        us=2.5,
    )
    got_chip = swap_chip(send_chip)
    got_gx = swap_gx(send_gx)
    got_core = swap_core(send_core)
    rad_two, slope_one, slope_two, base, found_two = call(
        radial_kernel,
        [(rows, edges), (rows, edges), (rows, edges), (TALL, LANES), (channels, edges)],
        [atom_ref],
        [geo, gamma, radials, table, h_one, onehot, weights],
        name="radials",
        us=2.0,
    )
    feat_two, fields_two, g_two, g_own, tally = call(
        second_layer_kernel,
        [(channels, edges), fields_shape, flat, flat, (TALL, LANES)],
        [],
        [base, table, h_one, got_gx, got_core, got_chip, onehot, geo, angular, rad_two, weights, reads, found_two],
        [flat],
        name="second_layer",
        us=2.5,
    )
    bits = (lax.axis_size("yz") - 1).bit_length()
    all_bits = (lax.axis_size(("gx", "yz")) - 1).bit_length()
    got_sums = partners(tally, [0])
    g_feat, g_off = call(
        second_gradient_kernel,
        [(channels, edges), (ROWS, edges)],
        [],
        [geo, rad_two, slope_two, feat_two, fields_two, g_two],
        name="second_gradient",
        us=2.5,
    )
    got_sums, g_off = together(got_sums, g_off)
    tally = sum(got_sums, tally)
    got_sums = partners(tally, [bits - 1] if bits > 1 else [])
    left, send_gx, send_core, send_chip, g_ghost, g_target_two = call(
        ghost_gradient_kernel,
        [((2 * channels + 3 * ROWS, edges), bf16), square, half, half, (ROWS, ghosts), (ROWS, slots)],
        [],
        [g_feat, g_off, onehot_t, weights],
        name="ghost_gradient",
        us=1.5,
    )
    got_sums, g_ghost = together(got_sums, g_ghost)
    tally = sum(got_sums, tally)
    got_chip = swap_chip(send_chip)
    got_gx = return_gx(send_gx)
    got_core = swap_core(send_core)
    (slope_one,), tally = together([slope_one], tally)
    got_sums = partners(tally, [bit for bit in range(1, bits - 1) if bit != 2])
    factors, g_h, g_local_two = call(
        factor_kernel,
        [(4, channels, edges), flat, (ROWS, slots)],
        [],
        [geo, rad_one, slope_one, feat_one, fields_one, left, onehot_t, weights, g_own],
        name="factors",
        us=3.0,
    )
    left, g_target_one, send_gx, send_core, send_chip = call(
        first_gradient_kernel,
        [((3 * ROWS, edges), bf16), (ROWS, slots), (8, LANES), (8, LANES), (8, LANES)],
        [],
        [g_h, got_gx, got_core, got_chip, slope, factors, geo, g_ghost, onehot_t, send_t, weights],
        [flat, (ROWS, edges)],
        name="first_gradient",
        us=1.2,
    )
    got_sums, left = together(got_sums, left)
    tally = sum(got_sums, tally)
    got_sums = partners(tally, [2] if bits > 3 else [])
    got_chip = swap_chip(send_chip)
    got_gx = return_gx(send_gx)
    got_core = swap_core(send_core)
    (g_pos,) = call(
        local_kernel,
        [(ROWS, slots)],
        [],
        [left, onehot_t, g_local_two, g_target_two, g_target_one],
        name="local",
        us=0.5,
    )
    tally = sum(got_sums, tally)[:ROWS]
    tallies = [tally] + partners(tally, range(bits, all_bits))
    (g_sum,) = call(
        chip_force_kernel, [(ROWS, slots)], [], [g_pos, got_chip, send_t], name="chip_forces", us=0.1
    )
    forces, energy = call(
        force_kernel,
        [(3, slots), (1, 1)],
        [],
        [g_sum, got_gx, got_core, send_t] + tallies,
        name="forces",
    )
    return (forces, energy.reshape(()))


def solution(mesh):
    return jax.shard_map(
        shards,
        mesh=mesh,
        in_specs=(
            P(None, ("gx", "yz")),
            P(("gx", "yz")),
            P(("gx", "yz"), None),
            P(("gx", "yz")),
            P(("gx", "yz"), None),
            P(None, ("gx", "yz")),
            P(),
            P(),
            P(),
            P(),
            P(),
            P(),
            P(),
        ),
        out_specs=(P(None, ("gx", "yz")), P()),
        check_vma=False,
    )
```

```python
import functools
import math

import jax
import jax.numpy as jnp
from jax import lax
from jax.experimental import pallas as pl
from jax.experimental.pallas import tpu as pltpu
from jax.sharding import PartitionSpec as P

root_three = math.sqrt(3.0)
root_five = math.sqrt(5.0)
root_fifteen = math.sqrt(15.0)
f32 = jnp.float32
bf16 = jnp.bfloat16
ROWS = 8
LANES = 128
TALL = 8
CHIP_ROWS = 16
SUMS_UNROLL = 16
EDGE_UNROLL = 16
FORCE_UNROLL = 16
FACTOR_UNROLL = 16
VMEM_BYTES = 16 * 1024 * 1024


def split2(value):
    high = value.astype(bf16)
    return high, (value - high.astype(f32)).astype(bf16)


def split3(value):
    high = value.astype(bf16)
    rest = value - high.astype(f32)
    mid = rest.astype(bf16)
    return high, mid, (rest - mid.astype(f32)).astype(bf16)


def dot(left, right, left_dim, right_dim):
    return lax.dot_general(
        left, right, (((left_dim,), (right_dim,)), ((), ())), preferred_element_type=f32
    )


def dot3(left, right, left_dim, right_dim):
    lh, ll = split2(left)
    rh, rl = split2(right)
    return (
        dot(lh, rh, left_dim, right_dim)
        + dot(lh, rl, left_dim, right_dim)
        + dot(ll, rh, left_dim, right_dim)
    )


def pieces(table):
    parts = pieces_f32(table)
    return jnp.concatenate([parts, jnp.zeros(table.shape, f32)], axis=0).astype(bf16)


def pieces_f32(table):
    high = table.astype(bf16).astype(f32)
    rest = table - high
    mid = rest.astype(bf16).astype(f32)
    return jnp.concatenate([high, mid, rest - mid], axis=0)


def whole(stack):
    return stack[0:ROWS] + stack[ROWS : 2 * ROWS] + stack[2 * ROWS : 3 * ROWS]


def onehot_rows(count, row):
    places = lax.broadcasted_iota(jnp.int32, (count, row.shape[1]), 0)
    return jnp.where(places == row, 1.0, 0.0).astype(bf16)


def column(row):
    n = row.shape[1]
    down = lax.broadcasted_iota(jnp.int32, (n, n), 0)
    across = lax.broadcasted_iota(jnp.int32, (n, n), 1)
    return jnp.sum(jnp.where(down == across, jnp.broadcast_to(row, (n, n)), 0.0), axis=1, keepdims=True)


def left_half(shape):
    return lax.broadcasted_iota(jnp.int32, shape, 1) < shape[1] // 2


def is_even():
    return lax.rem(lax.axis_index("yz"), 2) == 0


def previous_and_next(core, chip):
    even = is_even()
    return jnp.where(even, chip, core), jnp.where(even, core, chip)


def faces_yz(core, chip):
    before, after = previous_and_next(core, chip)
    return jnp.where(left_half(core.shape), before, after)


def pack_halves(value):
    half = value.shape[0] // 2
    top, bottom = value[0:half], value[half:]
    left = left_half(top.shape)
    turned_top, turned_bottom = pltpu.roll(top, LANES // 2, 1), pltpu.roll(bottom, LANES // 2, 1)
    return jnp.where(left, top, turned_bottom), jnp.where(left, turned_top, bottom)


def join_halves(left_columns, right_columns):
    left = left_half(left_columns.shape)
    top = jnp.where(left, left_columns, pltpu.roll(right_columns, LANES // 2, 1))
    bottom = jnp.where(left, pltpu.roll(left_columns, LANES // 2, 1), right_columns)
    return jnp.concatenate([top, bottom], axis=0)


def stacked_left(weights):
    high, low = split2(weights)
    return jnp.concatenate([high, high, low], axis=1)


def stacked_right(value):
    high, low = split2(value)
    return jnp.concatenate([high, low, high], axis=0)


def stacked_rows(value):
    high = value.astype(bf16).astype(f32)
    return jnp.concatenate([high, high, value - high], axis=0).astype(bf16)


def stacked_rows_left(value):
    high = value.astype(bf16).astype(f32)
    low = value - high
    return jnp.concatenate([high, low, high], axis=0)


def species_onehot(code, count):
    places = lax.rem(lax.broadcasted_iota(jnp.int32, (3 * count, code.shape[1]), 0), count)
    return jnp.where(places == code.astype(jnp.int32), 1.0, 0.0).astype(bf16)


def matmul(left, right):
    return dot(left, right, 1, 0)


def repeat(row, times):
    return jnp.concatenate([row] * times, axis=1)


def tile(index):
    return pl.ds(pl.multiple_of(index * ROWS, ROWS), ROWS)


def degree_tiles(index, channels):
    return [pl.ds(pl.multiple_of(degree * channels + index * ROWS, ROWS), ROWS) for degree in range(3)]


def lane_parts(slots, entries):
    for part in range(slots // LANES):
        yield pl.ds(part * LANES, LANES), [pl.ds(k * slots + part * LANES, LANES) for k in range(entries)]


U, R, SCALE, SQUARE = 0, 3, 6, 7


def gather_sums(geo, y_ref, rad_ref, feat_ref, fields_ref, invariant_ref):
    channels, slots = invariant_ref.shape
    entries = feat_ref.shape[1] // slots
    for lanes, edges in lane_parts(slots, entries):
        first = [[geo[U + d, :, edges[k]] for d in range(3)] for k in range(entries)]
        second = [[y_ref[m, :, edges[k]] for m in range(5)] for k in range(entries)]

        def body(index, carry):
            rows = tile(index)
            degrees = degree_tiles(index, channels)
            sums = None
            for k in range(entries):
                feat = feat_ref[rows, edges[k]]
                zero, one, two = [rad_ref[degree, edges[k]] * feat for degree in degrees]
                terms = [zero] + [item * one for item in first[k]] + [item * two for item in second[k]]
                sums = terms if k == 0 else [old + new for old, new in zip(sums, terms)]
            total = sums[0]
            for item in sums[1:]:
                total = total + item * item
            invariant_ref[rows, lanes] = total
            a1, a2, a3, a4, a5, a6, a7, a8 = sums[1:]
            c6 = (1.0 / root_three) * a6
            for number, field in enumerate((a1, a2, a3, a4, a5, a7, a8 - c6, a8 + c6, c6 + c6)):
                fields_ref[number, rows, lanes] = field
            return carry

        lax.fori_loop(0, channels // ROWS, body, 0, unroll=SUMS_UNROLL)


def direction_terms(fields, unit):
    a1, a2, a3, a4, a5, a7, minus, plus, twice = fields
    ux, uy, uz = unit
    h_x = uy * a4 + uz * a7 + ux * minus
    h_y = ux * a4 + uz * a5 - uy * plus
    h_z = uy * a5 + ux * a7 + uz * twice
    one = ux * a1 + uy * a2 + uz * a3
    two = 0.5 * (ux * h_x + uy * h_y + uz * h_z)
    return h_x, h_y, h_z, one, two


def offset_gradients(found, geo_ref, edges):
    g_s, g_x, g_y, g_z = [jnp.sum(item, axis=0, keepdims=True) for item in found]
    rx, ry, rz = [geo_ref[R + d, 0:1, edges] for d in range(3)]
    scale = geo_ref[SCALE, 0:1, edges]
    along = g_x * rx + g_y * ry + g_z * rz
    radial_part = 2.0 * g_s - scale * scale * scale * along
    return scale * g_x + rx * radial_part, scale * g_y + ry * radial_part, scale * g_z + rz * radial_part


def silu_and_slope(mixed):
    sigma = 1.0 / (1.0 + jnp.exp(-mixed))
    return mixed * sigma, sigma * (1.0 + mixed * (1.0 - sigma))


def fetch(pairs, sems):
    copies = [pltpu.make_async_copy(source, target, sems.at[i]) for i, (source, target) in enumerate(pairs)]
    for copy in copies:
        copy.start()
    return copies


def pack_kernel(dest_hbm, count_hbm, pos_hbm, species_hbm, out, dest, count, pos, species, sems):
    copies = fetch(((dest_hbm, dest), (count_hbm, count), (pos_hbm, pos), (species_hbm, species)), sems)
    blocks, width = species.shape
    place = lax.broadcasted_iota(jnp.int32, (1, width), 1)
    out[...] = jnp.zeros(out.shape, f32)
    for copy in copies:
        copy.wait()
    for group in range(3):
        coords = jnp.zeros((3, width), f32)
        code = jnp.full((1, width), -1.0, f32)
        for b in range(blocks):
            hit = dest[0, b] == group
            coords = jnp.where(hit, pos[:, b * width : (b + 1) * width], coords)
            alive = jnp.where(place < count[b], species[b : b + 1, :].astype(f32), -1.0)
            code = jnp.where(hit, alive, code)
        out[group * ROWS : group * ROWS + 3, :] = coords
        out[group * ROWS + 3 : group * ROWS + 4, :] = code


def prepare_kernel(
    gammas_hbm, nbr_hbm, lists_hbm, embed_hbm, w_up_hbm, w_rad_hbm, w_mix_hbm, readout_hbm,
    onehot, send, gamma, radials, species_up, species_in, weights, reads, onehot_t, send_t,
    gammas, nbr, lists, embed, w_up, w_rad, w_mix, readout, padded, sems,
):
    copies = fetch(
        (
            (nbr_hbm, nbr),
            (lists_hbm, lists),
            (gammas_hbm, gammas),
            (w_rad_hbm, w_rad),
            (embed_hbm, embed),
            (w_up_hbm, w_up),
            (w_mix_hbm, w_mix),
            (readout_hbm, readout),
        ),
        sems,
    )
    entries, slots = nbr.shape
    for copy in copies:
        copy.wait()
    wide = onehot.shape[0]
    for k in range(entries):
        onehot[:, k * slots : (k + 1) * slots] = onehot_rows(wide, nbr[k : k + 1, :])
    faces, ghosts = lists.shape
    for face in range(faces):
        send[:, face * ghosts : (face + 1) * ghosts] = onehot_rows(slots, lists[face : face + 1, :])
    count = w_rad.shape[1]
    which = lax.broadcasted_iota(jnp.int32, gamma.shape[1:], 0)
    channels = w_up.shape[1]
    place = lax.broadcasted_iota(jnp.int32, w_rad.shape[1:], 1)
    scales = jnp.where(place < channels, 1.0, jnp.where(place < 2 * channels, root_three, root_fifteen)) * (1.0 / entries)
    for layer in range(2):
        value = jnp.zeros(which.shape, f32)
        for q in range(count):
            value = jnp.where(which == q, gammas[layer, q], value)
        gamma[layer] = value
        radials[layer] = stacked_rows_left(w_rad[layer] * scales).T.astype(bf16)
    padded[...] = jnp.zeros(padded.shape, f32)
    padded[0 : embed.shape[0], :] = embed[...]
    species = padded[...]
    species_up[...] = pieces_f32(dot3(species, w_up[0], 1, 0)).T.astype(bf16)
    species_in[...] = pieces_f32(species).T.astype(bf16)
    for number, item in enumerate(
        (w_mix[0].T, w_up[1].T, w_mix[1].T, w_mix[1], w_up[1], w_mix[0])
    ):
        weights[number] = stacked_left(item)
    for layer in range(2):
        reads[layer] = jnp.broadcast_to(column(readout[layer : layer + 1, :]), reads.shape[1:])
    index_rows = jnp.concatenate([nbr[...].astype(f32), jnp.zeros((ROWS - entries, slots), f32)], axis=0)
    index_columns = index_rows.T
    across = lax.broadcasted_iota(jnp.int32, (slots, wide), 1).astype(f32)
    for k in range(entries):
        onehot_t[k * slots : (k + 1) * slots, :] = jnp.where(
            across == index_columns[:, k : k + 1], 1.0, 0.0
        ).astype(bf16)
    list_rows = jnp.concatenate([lists[...].astype(f32), jnp.zeros((ROWS - faces, ghosts), f32)], axis=0)
    list_columns = list_rows.T
    across = lax.broadcasted_iota(jnp.int32, (ghosts, slots), 1).astype(f32)
    for face in range(faces):
        send_t[face * ghosts : (face + 1) * ghosts, :] = jnp.where(
            across == list_columns[:, face : face + 1], 1.0, 0.0
        ).astype(bf16)


def assemble_kernel(own, core, chip, send, table, pick_gx, pick_core, pick_chip):
    before, after = previous_and_next(core[...], chip[...])
    blocks = [after[0:ROWS], own[ROWS : 2 * ROWS, :], before[2 * ROWS : 3 * ROWS]]
    slots = jnp.concatenate(blocks, axis=1)
    table[...] = slots
    picked = whole(matmul(pieces(slots), send[...]))
    pick_gx[...] = picked[:, 0:LANES]
    pick_core[...] = picked[:, LANES : 2 * LANES]
    pick_chip[...] = jnp.zeros(pick_chip.shape, f32)
    pick_chip[0:ROWS, :] = picked[:, LANES : 2 * LANES]


def own_positions_kernel(table, onehot, found):
    found[...] = whole(matmul(pieces(table[...]), onehot[0 : table.shape[1], :]))


def first_layer_kernel(
    found_own, table, got_gx, got_core, got_chip, onehot, send, gamma, radials, species_up, species_in, weights,
    h_out, slope_out, send_gx, send_core, send_chip, geo, y_ref, rad_ref, feat_ref, fields_ref,
    inv_ref,
):
    slots = table.shape[1]
    edges = onehot.shape[1]
    entries = edges // slots
    ghosts = jnp.concatenate([got_gx[...], faces_yz(got_core[...], got_chip[0:ROWS, :])], axis=1)
    found = found_own[...] + whole(matmul(pieces(ghosts), onehot[slots:, :]))
    feat_ref[...] = matmul(species_up[...], species_onehot(found[3:4], ROWS))
    spread = lambda row: jnp.broadcast_to(row, (ROWS, edges))
    rx, ry, rz = [
        spread(found[d : d + 1] - repeat(table[d : d + 1, :], entries)) for d in range(3)
    ]
    square = rx * rx + ry * ry + rz * rz
    basis = jnp.exp(-gamma[0] * square)
    rad_ref[...] = matmul(radials[0], stacked_rows(basis))
    scale = lax.rsqrt(1.0 + square)
    ux, uy, uz = rx * scale, ry * scale, rz * scale
    for number, item in enumerate((ux, uy, uz, rx, ry, rz, scale, square)):
        geo[number] = item
    xx, yy, zz = ux * ux, uy * uy, uz * uz
    for number, item in enumerate(
        (ux * uy, uy * uz, (0.5 / root_three) * (2.0 * zz - xx - yy), ux * uz, 0.5 * (xx - yy))
    ):
        y_ref[number] = item
    gather_sums(geo, y_ref, rad_ref, feat_ref, fields_ref, inv_ref)
    mixed = matmul(weights[0], stacked_right(inv_ref[...]))
    code = table[3:4, :]
    live = jnp.where(code >= 0.0, 1.0, 0.0)
    h_zero = matmul(species_in[...], species_onehot(code, ROWS))
    value, slope = silu_and_slope(mixed)
    h_one = live * (h_zero + value)
    h_out[...] = h_one
    slope_out[...] = live * slope
    channels = h_one.shape[0]
    picked = matmul(jnp.concatenate(split2(h_one), axis=0), send[...])
    picked = picked[0:channels] + picked[channels : 2 * channels]
    send_gx[...] = picked[:, 0:LANES]
    to_next, to_previous = pack_halves(picked[:, LANES : 2 * LANES])
    even = is_even()
    send_core[...] = jnp.where(even, to_next, to_previous)
    send_chip[...] = jnp.where(even, to_previous, to_next)


def radial_kernel(
    atom_ref, geo, gamma, radials, table, h_one, onehot, weights,
    rad_two, slope_one, slope_two, base, found_two,
):
    square = geo[SQUARE]
    basis = jnp.exp(-gamma[1] * square)
    rad_two[...] = matmul(radials[1], stacked_rows(basis))
    slope_two[...] = matmul(radials[1], stacked_rows(-gamma[1] * basis))
    slope_one[...] = matmul(radials[0], stacked_rows(-gamma[0] * jnp.exp(-gamma[0] * square)))
    code = table[3:4, :]
    live = jnp.where(code >= 0.0, 1.0, 0.0)
    energy = jnp.zeros(code.shape, f32)
    for kind in range(atom_ref.shape[0]):
        energy = energy + jnp.where(code == float(kind), atom_ref[kind], 0.0)
    fold = lambda row: sum(row[:, c : c + LANES] for c in range(0, code.shape[1], LANES))
    base[...] = jnp.zeros(base.shape, f32)
    base[0:1, :] = fold(energy)
    base[1:2, :] = fold(live)
    channels, slots = h_one.shape
    projected = matmul(weights[1], stacked_right(h_one[...]))
    both = matmul(jnp.concatenate(split2(projected), axis=0), onehot[0:slots, :])
    found_two[...] = both[0:channels] + both[channels : 2 * channels]


def factor_kernel(
    geo, rad_ref, slope_ref, feat_ref, fields_ref, left, onehot_t, weights, g_own,
    factors, g_h, g_pos,
):
    channels, slots = fields_ref.shape[1:]
    entries = feat_ref.shape[1] // slots
    scattered = matmul(left[...], onehot_t[:, 0:slots])
    g_proj = scattered[0:channels] + scattered[channels : 2 * channels]
    g_pos[...] = whole(scattered[2 * channels : 2 * channels + 4 * ROWS])
    g_h[...] = matmul(weights[4], stacked_right(g_proj)) + g_own[...]
    for lanes, edges in lane_parts(slots, entries):
        units = [[geo[U + d, :, edges[k]] for d in range(3)] for k in range(entries)]

        def body(index, carry):
            rows = tile(index)
            degrees = degree_tiles(index, channels)
            fields = [fields_ref[m, rows, lanes] for m in range(9)]
            for k in range(entries):
                h_x, h_y, h_z, one, two = direction_terms(fields, units[k])
                feat = feat_ref[rows, edges[k]]
                r1, r2 = [rad_ref[d, edges[k]] * feat for d in degrees[1:]]
                d0, d1, d2 = [slope_ref[d, edges[k]] for d in degrees]
                factors[0, rows, edges[k]] = feat * (0.5 * d0 + d1 * one + d2 * two)
                factors[1, rows, edges[k]] = r1 * fields[0] + r2 * h_x
                factors[2, rows, edges[k]] = r1 * fields[1] + r2 * h_y
                factors[3, rows, edges[k]] = r1 * fields[2] + r2 * h_z
            return carry

        lax.fori_loop(0, channels // ROWS, body, 0, unroll=FACTOR_UNROLL)


def second_layer_kernel(
    base, table, h_one, got_gx, got_core, got_chip, onehot, geo, y_ref, rad_ref, weights, reads, found_two,
    feat_ref, fields_ref, g_ref, g_own, tally,
    inv_ref,
):
    h_local = h_one[...]
    channels, slots = h_local.shape
    before, after = previous_and_next(got_core[...], got_chip[...])
    ghosts = jnp.concatenate([got_gx[...], join_halves(before, after)], axis=1)
    projected = matmul(weights[1], stacked_right(ghosts))
    both = matmul(jnp.concatenate(split2(projected), axis=0), onehot[slots:, :])
    feat_ref[...] = found_two[...] + (both[0:channels] + both[channels : 2 * channels])
    gather_sums(geo, y_ref, rad_ref, feat_ref, fields_ref, inv_ref)
    mixed = matmul(weights[2], stacked_right(inv_ref[...]))
    live = jnp.where(table[3:4, :] >= 0.0, 1.0, 0.0)
    value, slope = silu_and_slope(mixed)
    h_two = live * (h_local + value)
    energy = jnp.sum(reads[0] * h_local + reads[1] * h_two, axis=0, keepdims=True)
    tally[...] = base[...]
    tally[0:1, :] += sum(energy[:, c : c + LANES] for c in range(0, slots, LANES))
    g_ref[...] = matmul(weights[3], stacked_right((live * reads[1]) * slope))
    g_own[...] = live * (reads[0] + reads[1])


def second_gradient_kernel(
    geo, rad_ref, slope_ref, feat_ref, fields_ref, g_ref,
    g_feat, g_off,
):
    channels, slots = g_ref.shape
    entries = feat_ref.shape[1] // slots
    g_off[...] = jnp.zeros(g_off.shape, f32)
    for lanes, edges in lane_parts(slots, entries):
        units = [[geo[U + d, :, edges[k]] for d in range(3)] for k in range(entries)]

        def body(index, carry):
            rows = tile(index)
            degrees = degree_tiles(index, channels)
            g = g_ref[rows, lanes]
            fields = [(g + g) * fields_ref[m, rows, lanes] for m in range(9)]
            found = []
            for k in range(entries):
                h_x, h_y, h_z, one, two = direction_terms(fields, units[k])
                feat = feat_ref[rows, edges[k]]
                r0, r1, r2 = [rad_ref[d, edges[k]] for d in degrees]
                d0, d1, d2 = [slope_ref[d, edges[k]] for d in degrees]
                g_feat[rows, edges[k]] = g * r0 + r1 * one + r2 * two
                q1, q2 = feat * r1, feat * r2
                found += [
                    carry[4 * k] + feat * (g * d0 + d1 * one + d2 * two),
                    carry[4 * k + 1] + (q1 * fields[0] + q2 * h_x),
                    carry[4 * k + 2] + (q1 * fields[1] + q2 * h_y),
                    carry[4 * k + 3] + (q1 * fields[2] + q2 * h_z),
                ]
            return tuple(found)

        zero = jnp.zeros((ROWS, LANES), f32)
        found = lax.fori_loop(0, channels // ROWS, body, (zero,) * (4 * entries), unroll=EDGE_UNROLL)
        for k in range(entries):
            for d, item in enumerate(offset_gradients(found[4 * k : 4 * k + 4], geo, edges[k])):
                g_off[d : d + 1, edges[k]] = item


def ghost_gradient_kernel(g_feat, g_off, onehot_t, weights, left, send_gx, send_core, send_chip, g_ghost, g_target):
    channels, edge_count = g_feat.shape
    wide = onehot_t.shape[1]
    slots = g_target.shape[1]
    entries = edge_count // slots
    stacked = jnp.concatenate([*split2(g_feat[...]), pieces(g_off[...])], axis=0)
    left[...] = stacked
    scattered = matmul(stacked, onehot_t[:, slots:wide])
    g_proj = scattered[0:channels] + scattered[channels : 2 * channels]
    g_ghost[...] = whole(scattered[2 * channels : 2 * channels + 4 * ROWS])
    g_all = matmul(weights[4], stacked_right(g_proj))
    send_gx[...] = g_all[:, 0:LANES]
    to_previous, to_next = pack_halves(g_all[:, LANES : 2 * LANES])
    even = is_even()
    send_core[...] = jnp.where(even, to_next, to_previous)
    send_chip[...] = jnp.where(even, to_previous, to_next)
    g_target[...] = sum(g_off[:, k * slots : (k + 1) * slots] for k in range(entries))


def first_gradient_kernel(
    g_h, got_gx, got_core, got_chip, slope, factors, geo, g_ghost, onehot_t, send_t, weights,
    left, g_target, send_gx, send_core, send_chip,
    g_ref, g_off,
):
    channels, slots = slope.shape
    entries = geo.shape[2] // slots
    before, after = previous_and_next(got_core[...], got_chip[...])
    back = jnp.concatenate([got_gx[...], join_halves(after, before)], axis=1)
    returned = matmul(jnp.concatenate(split2(back), axis=0), send_t[...])
    g_total = g_h[...] + (returned[0:channels] + returned[channels : 2 * channels])
    g_ref[...] = matmul(weights[5], stacked_right(g_total * (2.0 * slope[...])))
    g_off[...] = jnp.zeros(g_off.shape, f32)
    for lanes, edges in lane_parts(slots, entries):

        def body(index, carry):
            rows = tile(index)
            g = g_ref[rows, lanes]
            return tuple(
                carry[4 * k + m] + g * factors[m, rows, edges[k]] for k in range(entries) for m in range(4)
            )

        zero = jnp.zeros((ROWS, LANES), f32)
        found = lax.fori_loop(0, channels // ROWS, body, (zero,) * (4 * entries), unroll=FORCE_UNROLL)
        for k in range(entries):
            for d, item in enumerate(offset_gradients(found[4 * k : 4 * k + 4], geo, edges[k])):
                g_off[d : d + 1, edges[k]] = item
    wide = onehot_t.shape[1]
    stacked = pieces(g_off[...])
    left[...] = stacked
    g_ext = whole(matmul(stacked, onehot_t[:, slots:wide])) + g_ghost[...]
    for out, piece in ((send_gx, 0), (send_core, 1), (send_chip, 1)):
        out[...] = jnp.zeros(out.shape, f32)
        out[0:ROWS, :] = g_ext[:, piece * LANES : (piece + 1) * LANES]
    g_target[...] = sum(g_off[:, k * slots : (k + 1) * slots] for k in range(entries))


def local_kernel(left, onehot_t, g_local_two, g_target_two, g_target_one, g_pos):
    slots = g_pos.shape[1]
    g_pos[...] = whole(matmul(left[...], onehot_t[:, 0:slots])) + g_local_two[...] - g_target_two[...] - g_target_one[...]


def chip_force_kernel(g_pos, got_chip, send_t, g_sum):
    half = left_half((ROWS, LANES))
    wanted = jnp.where(is_even(), 1.0, 0.0)
    kept = got_chip[0:ROWS, :] * jnp.where(half, 1.0 - wanted, wanted)
    ghosts = send_t.shape[0]
    g_sum[...] = g_pos[...] + whole(matmul(pieces(kept), send_t[ghosts - LANES : ghosts, :]))


def force_kernel(g_sum, got_gx, got_core, send_t, *rest):
    tallies, (forces, energy) = rest[:-2], rest[-2:]
    half = left_half((ROWS, LANES))
    wanted = jnp.where(is_even(), 0.0, 1.0)
    kept = got_core[0:ROWS, :] * jnp.where(half, 1.0 - wanted, wanted)
    back = jnp.concatenate([got_gx[0:ROWS, :], kept], axis=1)
    forces[...] = -(g_sum[...] + whole(matmul(pieces(back), send_t[...])))[0:3]
    sums = jnp.sum(sum(item[0:2, :] for item in tallies), axis=1, keepdims=True)
    energy[...] = sums[0:1, :] / sums[1:2, :]


def call(kernel, outs, scalars, arrays, scratch=(), name=None, raw=False, us=1.0):
    in_vmem = pl.BlockSpec(memory_space=pltpu.VMEM)
    in_smem = pl.BlockSpec(memory_space=pltpu.SMEM)
    in_hbm = pl.BlockSpec(memory_space=pltpu.HBM)
    shapes = [jax.ShapeDtypeStruct(*item) if isinstance(item[0], tuple) else jax.ShapeDtypeStruct(item, f32) for item in outs]
    return pl.pallas_call(
        kernel,
        out_shape=shapes,
        in_specs=[in_smem] * len(scalars) + [in_hbm if raw else in_vmem] * len(arrays),
        out_specs=[in_vmem] * len(outs),
        scratch_shapes=[pltpu.VMEM(item, f32) if isinstance(item, tuple) else item for item in scratch],
        compiler_params=pltpu.CompilerParams(vmem_limit_bytes=VMEM_BYTES),
        cost_estimate=pl.CostEstimate(flops=int(us * 1e9), bytes_accessed=int(us * 3e6), transcendentals=0),
        name=name,
    )(*scalars, *[pltpu.with_memory_space_constraint(item, pltpu.HBM) if raw else item for item in arrays])


def swap_core(value):
    size = lax.axis_size("yz")
    return lax.ppermute(value, "yz", [(i, i ^ 1) for i in range(size)])


def swap_chip(value):
    size = lax.axis_size("yz")
    return lax.ppermute(value, "yz", [(i, (i + 1 if i % 2 else i - 1) % size) for i in range(size)])


def shift(value, axis, by):
    size = lax.axis_size(axis)
    return lax.ppermute(value, axis, [(i, (i + by) % size) for i in range(size)])


def swap_gx(value):
    size = lax.axis_size("gx")
    if size == 2:
        return shift(value, "gx", 1)
    half = value.shape[1] // 2
    return jnp.concatenate(
        [shift(value[:, :half], "gx", 1), shift(value[:, half:], "gx", -1)], axis=1
    )


def return_gx(value):
    size = lax.axis_size("gx")
    if size == 2:
        return shift(value, "gx", 1)
    half = value.shape[1] // 2
    return jnp.concatenate(
        [shift(value[:, :half], "gx", -1), shift(value[:, half:], "gx", 1)], axis=1
    )


def partners(value, bits):
    axes = ("gx", "yz")
    size = lax.axis_size(axes)
    steps = [0]
    for bit in bits:
        steps += [step ^ (1 << bit) for step in steps]
    return [lax.ppermute(value, axes, [(i, i ^ step) for i in range(size)]) for step in steps[1:]]


def together(values, other):
    *values, other = lax.optimization_barrier((*values, other))
    return values, other


def shards(
    old_pos,
    old_species,
    block_dest,
    block_count,
    send_list,
    neighbours,
    embed,
    atom_ref,
    w_up,
    gammas,
    w_rad,
    w_mix,
    readout,
):
    entries, slots = neighbours.shape
    blocks = block_dest.shape[0]
    width = old_species.shape[0] // blocks
    channels = w_up.shape[1]
    ghosts = send_list.size
    wide = slots + ghosts
    edges = entries * slots
    rows = w_rad.shape[2]
    species = old_species.reshape(blocks, width)
    i32 = jnp.int32

    (packed,) = call(
        pack_kernel,
        [(3 * ROWS, width)],
        [],
        [block_dest.T, block_count, old_pos, species],
        [
            pltpu.SMEM((1, blocks), i32),
            pltpu.SMEM((blocks,), i32),
            old_pos.shape,
            pltpu.VMEM(species.shape, i32),
            pltpu.SemaphoreType.DMA((4,)),
        ],
        name="pack",
        raw=True,
    )
    got_chip = swap_chip(packed)
    got_core = swap_core(packed)
    onehot, send, gamma, radials, species_up, species_in, weights, reads, onehot_t, send_t = call(
        prepare_kernel,
        [
            ((wide, edges), bf16),
            ((slots, ghosts), bf16),
            (2, ROWS, edges),
            ((2, rows, 3 * ROWS), bf16),
            ((channels, 3 * ROWS), bf16),
            ((channels, 3 * ROWS), bf16),
            ((6, channels, 3 * channels), bf16),
            (2, channels, slots),
            ((edges, wide), bf16),
            ((ghosts, slots), bf16),
        ],
        [],
        [gammas, neighbours, send_list, embed, w_up, w_rad, w_mix, readout],
        [
            pltpu.SMEM(gammas.shape, f32),
            pltpu.VMEM(neighbours.shape, i32),
            pltpu.VMEM(send_list.shape, i32),
            embed.shape,
            w_up.shape,
            w_rad.shape,
            w_mix.shape,
            readout.shape,
            (ROWS, channels),
            pltpu.SemaphoreType.DMA((8,)),
        ],
        name="prepare",
        raw=True,
        us=3.0,
    )
    small = (ROWS, LANES)
    tall = (CHIP_ROWS, LANES)
    table, pick_gx, pick_core, pick_chip = call(
        assemble_kernel,
        [(ROWS, slots), small, small, tall],
        [],
        [packed, got_core, got_chip, send],
        name="assemble",
        us=0.2,
    )
    got_chip = swap_chip(pick_chip)
    got_gx = swap_gx(pick_gx)
    got_core = swap_core(pick_core)
    (found_own,) = call(
        own_positions_kernel, [(ROWS, edges)], [], [table, onehot], name="own_positions", us=0.02
    )
    flat = (channels, slots)
    square = (channels, LANES)
    half = (channels // 2, LANES)
    fields_shape = (9, channels, slots)
    h_one, slope, send_gx, send_core, send_chip, geo, angular, rad_one, feat_one, fields_one = call(
        first_layer_kernel,
        [flat, flat, square, half, half, (8, ROWS, edges), (5, ROWS, edges), (rows, edges), (channels, edges), fields_shape],
        [],
        [found_own, table, got_gx, got_core, got_chip, onehot, send, gamma, radials, species_up, species_in, weights],
        [flat],
        name="first_layer",
        us=2.5,
    )
    got_chip = swap_chip(send_chip)
    got_gx = swap_gx(send_gx)
    got_core = swap_core(send_core)
    rad_two, slope_one, slope_two, base, found_two = call(
        radial_kernel,
        [(rows, edges), (rows, edges), (rows, edges), (TALL, LANES), (channels, edges)],
        [atom_ref],
        [geo, gamma, radials, table, h_one, onehot, weights],
        name="radials",
        us=2.0,
    )
    feat_two, fields_two, g_two, g_own, tally = call(
        second_layer_kernel,
        [(channels, edges), fields_shape, flat, flat, (TALL, LANES)],
        [],
        [base, table, h_one, got_gx, got_core, got_chip, onehot, geo, angular, rad_two, weights, reads, found_two],
        [flat],
        name="second_layer",
        us=2.5,
    )
    bits = (lax.axis_size("yz") - 1).bit_length()
    all_bits = (lax.axis_size(("gx", "yz")) - 1).bit_length()
    got_sums = partners(tally, [0])
    g_feat, g_off = call(
        second_gradient_kernel,
        [(channels, edges), (ROWS, edges)],
        [],
        [geo, rad_two, slope_two, feat_two, fields_two, g_two],
        name="second_gradient",
        us=2.5,
    )
    got_sums, g_off = together(got_sums, g_off)
    tally = sum(got_sums, tally)
    got_sums = partners(tally, [bits - 1] if bits > 1 else [])
    left, send_gx, send_core, send_chip, g_ghost, g_target_two = call(
        ghost_gradient_kernel,
        [((2 * channels + 4 * ROWS, edges), bf16), square, half, half, (ROWS, ghosts), (ROWS, slots)],
        [],
        [g_feat, g_off, onehot_t, weights],
        name="ghost_gradient",
        us=1.5,
    )
    got_sums, g_ghost = together(got_sums, g_ghost)
    tally = sum(got_sums, tally)
    got_chip = swap_chip(send_chip)
    got_gx = return_gx(send_gx)
    got_core = swap_core(send_core)
    (slope_one,), tally = together([slope_one], tally)
    got_sums = partners(tally, [bit for bit in range(1, bits - 1) if bit != 2])
    factors, g_h, g_local_two = call(
        factor_kernel,
        [(4, channels, edges), flat, (ROWS, slots)],
        [],
        [geo, rad_one, slope_one, feat_one, fields_one, left, onehot_t, weights, g_own],
        name="factors",
        us=3.0,
    )
    left, g_target_one, send_gx, send_core, send_chip = call(
        first_gradient_kernel,
        [((4 * ROWS, edges), bf16), (ROWS, slots), (8, LANES), (8, LANES), (8, LANES)],
        [],
        [g_h, got_gx, got_core, got_chip, slope, factors, geo, g_ghost, onehot_t, send_t, weights],
        [flat, (ROWS, edges)],
        name="first_gradient",
        us=1.2,
    )
    got_sums, left = together(got_sums, left)
    tally = sum(got_sums, tally)
    got_sums = partners(tally, [2] if bits > 3 else [])
    got_chip = swap_chip(send_chip)
    got_gx = return_gx(send_gx)
    got_core = swap_core(send_core)
    (g_pos,) = call(
        local_kernel,
        [(ROWS, slots)],
        [],
        [left, onehot_t, g_local_two, g_target_two, g_target_one],
        name="local",
        us=0.5,
    )
    tally = sum(got_sums, tally)[:ROWS]
    tallies = [tally] + partners(tally, range(bits, all_bits))
    (g_sum,) = call(
        chip_force_kernel, [(ROWS, slots)], [], [g_pos, got_chip, send_t], name="chip_forces", us=0.1
    )
    forces, energy = call(
        force_kernel,
        [(3, slots), (1, 1)],
        [],
        [g_sum, got_gx, got_core, send_t] + tallies,
        name="forces",
    )
    return (forces, energy.reshape(()))


def solution(mesh):
    return jax.shard_map(
        shards,
        mesh=mesh,
        in_specs=(
            P(None, ("gx", "yz")),
            P(("gx", "yz")),
            P(("gx", "yz"), None),
            P(("gx", "yz")),
            P(("gx", "yz"), None),
            P(None, ("gx", "yz")),
            P(),
            P(),
            P(),
            P(),
            P(),
            P(),
            P(),
        ),
        out_specs=(P(None, ("gx", "yz")), P()),
        check_vma=False,
    )
```
